128 devices in a mesh: row: 8 (over y, z_lo), col: 16 (over z_hi, x, core).
Axes of the slice: x: 4, y: 4, z: 4 (z_hi: 2, z_lo: 2; z = z_hi * 2 + z_lo), core: 2. Of those that a mesh axis runs over, the one named last changes fastest.
Arguments:
- image: bfloat16 [128, 1024, 256], P('row', 'col'), may hold values from -7 to 7
- out_cotangent: bfloat16 [128, 1024, 256], P('row', 'col'), may hold values from -6 to 6
- norm0_gain: bfloat16 [256], replicated, may hold values from 0.099609375 to 1.8984375
- w_expand: bfloat16 [256, 1024], replicated, may hold values from -0.375 to 0.375
- w_depth: bfloat16 [3, 3, 1024], replicated, may hold values from -2 to 2
- w_squeeze: bfloat16 [1024, 64], replicated, may hold values from -0.75 to 0.75
- w_excite: bfloat16 [64, 1024], replicated, may hold values from -3 to 3
- w_project: bfloat16 [1024, 256], replicated, may hold values from -0.1875 to 0.1875
- norm1_gain: bfloat16 [256], replicated, may hold values from 0.099609375 to 1.8984375
- w_qkv: bfloat16 [256, 768], replicated, may hold values from -0.375 to 0.375
- w_out: bfloat16 [256, 256], replicated, may hold values from -0.375 to 0.375
- attn_bias: float32 [8, 64, 64], replicated, may hold values from -2 to 250
Outputs:
- block_out: bfloat16 [128, 1024, 256], P('row', 'col')
- grad_image: bfloat16 [128, 1024, 256], P('row', 'col')
- grad_norm0: float32 [256], replicated
- grad_expand: float32 [256, 1024], replicated
- grad_depth: float32 [3, 3, 1024], replicated
- grad_squeeze: float32 [1024, 64], replicated
- grad_excite: float32 [64, 1024], replicated
- grad_project: float32 [1024, 256], replicated
- grad_norm1: float32 [256], replicated
- grad_qkv: float32 [256, 768], replicated
- grad_out_proj: float32 [256, 256], replicated
- grad_bias: float32 [8, 64, 64], replicated
The draws below stay inside these ranges and needn't reach their ends.
All inputs are finite; a program needn't handle non-finite values.
Results may differ from the reference program's by a relative error of at most 0.015.
Values may be sent and summed in bfloat16 or wider, within the bound.
A program may use at most 128 MiB of HBM per device.

```python
import jax
import jax.numpy as jnp
from jax import lax

C = 256
HEADS = 8
E = 1024
SQ = 64
GRID = 8
HEIGHT = 128
WIDTH = 1024


def draw_image(key, part):
    key = jax.random.fold_in(key, 11)
    noise_key, direction_key = jax.random.split(key)
    base = jnp.clip(jax.random.normal(noise_key, (HEIGHT, WIDTH, C), jnp.float32), -5.0, 5.0)
    slope = 1.5
    direction = jax.random.rademacher(direction_key, (C,), jnp.float32)
    row_frac = jnp.arange(HEIGHT, dtype=jnp.float32)[:, None] / HEIGHT
    col_frac = jnp.arange(WIDTH, dtype=jnp.float32)[None, :] / WIDTH
    ramp = 0.3 + slope * 0.5 * (row_frac + col_frac)
    return (base + ramp[:, :, None] * direction).astype(jnp.bfloat16)


def draw_attn_bias(key, part):
    key = jax.random.fold_in(key, 23)
    base_key = jax.random.fold_in(key, 0)
    members = GRID * GRID
    base = jax.random.uniform(base_key, (HEADS, members, members), jnp.float32, -2.0, 2.0)
    return base


def block_scale(rng, dims, cuts, least, high):
    factor_of = 1.0
    for axis_at, blocks in cuts:
        heights = jax.random.uniform(jax.random.fold_in(jax.random.fold_in(rng, 6), axis_at), (blocks,), jnp.float32, least / len(cuts), high / len(cuts))
        factor_of = factor_of * jnp.repeat(jnp.exp(heights), dims[axis_at] // blocks).reshape((-1,) + (1,) * (len(dims) - 1 - axis_at))
    return factor_of


def centred(key, extent, scale, most, pieces=(), kind=jnp.bfloat16):
    entries = scale * jax.random.normal(key, extent, jnp.float32)
    if pieces:
        entries = entries * block_scale(key, extent, pieces, -0.22, 0.18)
    return jnp.clip(entries, -most, most).astype(kind)


def setup_inputs(seed: int = 0) -> dict:
    key_of = jax.random.split(jax.random.key(seed), 13)
    return {
        "image": draw_image(jax.random.fold_in(key_of[12], 71), 0),
        "out_cotangent": centred(key_of[1], (HEIGHT, WIDTH, C), 1.0, 6.0, ((0, 8), (1, 16))),
        "norm0_gain": jnp.clip(1.0 + 0.18 * jax.random.normal(key_of[2], (C,), jnp.float32), 0.099609375, 1.8984375).astype(jnp.bfloat16),
        "w_expand": centred(key_of[3], (C, E), C ** -0.5, 0.375),
        "w_depth": centred(key_of[4], (3, 3, E), 9 ** -0.5, 2.0),
        "w_squeeze": centred(key_of[5], (E, SQ), (E // 16) ** -0.5, 0.75),
        "w_excite": centred(key_of[6], (SQ, E), (max(SQ // 16, 1)) ** -0.5, 3.0),
        "w_project": centred(key_of[7], (E, C), E ** -0.5, 0.1875),
        "norm1_gain": jnp.clip(1.0 + 0.18 * jax.random.normal(key_of[8], (C,), jnp.float32), 0.099609375, 1.8984375).astype(jnp.bfloat16),
        "w_qkv": centred(key_of[9], (C, 3 * C), C ** -0.5, 0.375),
        "w_out": centred(key_of[10], (C, C), C ** -0.5, 0.375),
        "attn_bias": draw_attn_bias(jax.random.fold_in(key_of[12], 71), 0),
    }


def norm_tokens(values, scale_gain):
    average = lax.optimization_barrier(jnp.mean(values, axis=-1, keepdims=True))
    centered = values - average
    variance = lax.optimization_barrier(jnp.mean(centered * centered, axis=-1, keepdims=True))
    return centered * lax.rsqrt(variance + 1e-05) * scale_gain

def matmul_last(left_side, right_side):
    flat_rows = left_side.reshape(-1, left_side.shape[-1])
    product = jnp.dot(flat_rows, right_side, preferred_element_type=jnp.float32)
    return product.reshape(left_side.shape[:-1] + (right_side.shape[-1],))

def smooth_gelu(values):
    return jax.nn.gelu(values, approximate=True)

def depthwise(padded, kernel, row_count, col_count):
    accumulated = jnp.zeros((row_count, col_count, padded.shape[-1]), jnp.float32)
    for shift_row in range(3):
        for shift_col in range(3):
            window = padded[shift_row:shift_row + row_count, shift_col:shift_col + col_count].astype(jnp.float32)
            accumulated = accumulated + window * kernel[shift_row, shift_col].astype(jnp.float32)
    return accumulated

def depthwise_back(padded_grad, kernel, row_count, col_count):
    accumulated = jnp.zeros((row_count, col_count, padded_grad.shape[-1]), jnp.float32)
    for shift_row in range(3):
        for shift_col in range(3):
            window = padded_grad[2 - shift_row:2 - shift_row + row_count, 2 - shift_col:2 - shift_col + col_count].astype(jnp.float32)
            accumulated = accumulated + window * kernel[shift_row, shift_col].astype(jnp.float32)
    return accumulated

def kernel_grad(padded, grad_pre, row_count, col_count):
    kernel_terms = []
    for shift_row in range(3):
        for shift_col in range(3):
            window = padded[shift_row:shift_row + row_count, shift_col:shift_col + col_count].astype(jnp.float32)
            kernel_terms.append(lax.optimization_barrier(jnp.sum(window * grad_pre.astype(jnp.float32), axis=(0, 1))))
    return jnp.stack(kernel_terms).reshape(3, 3, padded.shape[-1])

def excite_gate(pooled, squeeze_wide, excite_wide):
    hidden = jax.nn.silu(jnp.dot(pooled[None, :], squeeze_wide, precision=lax.Precision.HIGHEST))
    return jax.nn.sigmoid(jnp.dot(hidden, excite_wide, precision=lax.Precision.HIGHEST))[0]

def into_groups(values):
    row_count, col_count, channels = values.shape
    parted = values.reshape(GRID, row_count // GRID, GRID, col_count // GRID, channels).transpose(1, 3, 0, 2, 4)
    return parted.reshape(-1, GRID * GRID, channels)

def from_groups(values, row_count, col_count):
    channels = values.shape[-1]
    parted = values.reshape(row_count // GRID, col_count // GRID, GRID, GRID, channels).transpose(2, 0, 3, 1, 4)
    return parted.reshape(row_count, col_count, channels)

def attention_core(normed_groups, w_qkv, attn_bias):
    groups, members, channels = normed_groups.shape
    head_count = attn_bias.shape[0]
    head_dim = channels // head_count
    packed = matmul_last(normed_groups, w_qkv).astype(jnp.bfloat16).reshape(groups, members, 3, head_count, head_dim)
    queries = packed[:, :, 0]
    key_rows = packed[:, :, 1]
    values = packed[:, :, 2]
    scores = jnp.einsum('gihd,gjhd->ghij', queries.astype(jnp.float32), key_rows.astype(jnp.float32)) * head_dim ** (-0.5)
    scores = scores + attn_bias[None]
    row_max = lax.optimization_barrier(jnp.max(scores, axis=-1, keepdims=True))
    lifted = jnp.exp(scores - row_max)
    softmaxed = lifted / lax.optimization_barrier(jnp.sum(lifted, axis=-1, keepdims=True))
    weights_low = softmaxed.astype(jnp.bfloat16).astype(jnp.float32)
    attended = jnp.einsum('ghij,gjhd->gihd', weights_low, values.astype(jnp.float32)).astype(jnp.bfloat16)
    return (attended.reshape(groups, members, channels), queries, key_rows, values, softmaxed)

def attention_back(grad_att, queries, key_rows, values, softmaxed):
    groups, members, channels = grad_att.shape
    head_count = queries.shape[2]
    head_dim = channels // head_count
    grad_heads = grad_att.reshape(groups, members, head_count, head_dim).astype(jnp.float32)
    weights_low = softmaxed.astype(jnp.bfloat16).astype(jnp.float32)
    grad_values = jnp.einsum('ghij,gihd->gjhd', weights_low, grad_heads).astype(jnp.bfloat16)
    grad_probs = jnp.einsum('gihd,gjhd->ghij', grad_heads, values.astype(jnp.float32))
    grad_scores = softmaxed * (grad_probs - lax.optimization_barrier(jnp.sum(grad_probs * softmaxed, axis=-1, keepdims=True)))
    bias_part = lax.optimization_barrier(jnp.sum(grad_scores, axis=0))
    scaled = (grad_scores * head_dim ** (-0.5)).astype(jnp.bfloat16).astype(jnp.float32)
    grad_queries = jnp.einsum('ghij,gjhd->gihd', scaled, key_rows.astype(jnp.float32)).astype(jnp.bfloat16)
    grad_keys = jnp.einsum('ghij,gihd->gjhd', scaled, queries.astype(jnp.float32)).astype(jnp.bfloat16)
    stacked = jnp.stack([grad_queries, grad_keys, grad_values], axis=2)
    return (stacked.reshape(groups, members, 3 * channels), bias_part)

def reference(image, out_cotangent, norm0_gain, w_expand, w_depth, w_squeeze, w_excite, w_project, norm1_gain, w_qkv, w_out, attn_bias):
    row_count, col_count, channels = image.shape
    cells_total = row_count * col_count
    image_float = image.astype(jnp.float32)
    gain_first = norm0_gain.astype(jnp.float32)
    gain_second = norm1_gain.astype(jnp.float32)
    normed_first = norm_tokens(image_float, gain_first).astype(jnp.bfloat16)
    expanded = matmul_last(normed_first, w_expand)
    spread = smooth_gelu(expanded).astype(jnp.bfloat16)
    padded = jnp.pad(spread, ((1, 1), (1, 1), (0, 0)))
    depth_pre = depthwise(padded, w_depth, row_count, col_count)
    activated = smooth_gelu(depth_pre)
    pooled = lax.optimization_barrier(jnp.sum(activated, axis=(0, 1))) / cells_total
    squeeze_wide = w_squeeze.astype(jnp.float32)
    excite_wide = w_excite.astype(jnp.float32)
    channel_gate = excite_gate(pooled, squeeze_wide, excite_wide)
    gated_act = (activated * channel_gate).astype(jnp.bfloat16)
    mixed_map = (image_float + matmul_last(gated_act, w_project)).astype(jnp.bfloat16)
    mixed_float = mixed_map.astype(jnp.float32)
    normed_second = norm_tokens(mixed_float, gain_second).astype(jnp.bfloat16)
    grid_normed = into_groups(normed_second)
    group_total = grid_normed.shape[0]
    block_count = 8
    grid_blocks = grid_normed.reshape(block_count, group_total // block_count, GRID * GRID, channels)

    def forward_block(block_normed):
        return attention_core(block_normed, w_qkv, attn_bias)[0]
    attended_groups = lax.map(forward_block, grid_blocks).reshape(group_total, GRID * GRID, channels)
    attended_map = from_groups(attended_groups, row_count, col_count)
    block_out = (mixed_float + matmul_last(attended_map, w_out)).astype(jnp.bfloat16)
    grad_out_proj = jnp.dot(attended_map.reshape(-1, channels).T, out_cotangent.reshape(-1, channels), preferred_element_type=jnp.float32)
    grad_att = matmul_last(out_cotangent, w_out.T).astype(jnp.bfloat16)
    grad_blocks = into_groups(grad_att).reshape(block_count, group_total // block_count, GRID * GRID, channels)

    def backward_block(pair_blocks):
        block_normed, block_grad = pair_blocks
        attended_unused, queries, key_rows, values, softmaxed = attention_core(block_normed, w_qkv, attn_bias)
        return attention_back(block_grad, queries, key_rows, values, softmaxed)
    grad_packed, bias_parts = lax.map(backward_block, (grid_blocks, grad_blocks))
    grad_packed = grad_packed.reshape(group_total, GRID * GRID, 3 * channels)
    grad_bias = lax.optimization_barrier(jnp.sum(bias_parts, axis=0))
    grad_qkv = jnp.dot(grid_normed.reshape(-1, channels).T, grad_packed.reshape(-1, 3 * channels), preferred_element_type=jnp.float32)
    grad_normed_grid = matmul_last(grad_packed, w_qkv.T).astype(jnp.bfloat16)
    grad_normed = from_groups(grad_normed_grid, row_count, col_count)
    unused_second, norm_second_vjp = jax.vjp(norm_tokens, mixed_float, gain_second)
    grad_mixed_norm, grad_norm1 = norm_second_vjp(grad_normed.astype(jnp.float32))
    grad_mixed = out_cotangent.astype(jnp.float32) + grad_mixed_norm
    grad_mixed_b = grad_mixed.astype(jnp.bfloat16)
    grad_project = jnp.dot(gated_act.reshape(-1, gated_act.shape[-1]).T, grad_mixed_b.reshape(-1, channels), preferred_element_type=jnp.float32)
    grad_gated = matmul_last(grad_mixed_b, w_project.T)
    grad_gate = lax.optimization_barrier(jnp.sum(grad_gated * activated, axis=(0, 1)))
    unused_gate, gate_vjp = jax.vjp(excite_gate, pooled, squeeze_wide, excite_wide)
    grad_pooled, grad_squeeze, grad_excite = gate_vjp(grad_gate)
    grad_activated = grad_gated * channel_gate + grad_pooled / cells_total
    unused_act, gelu_depth_vjp = jax.vjp(smooth_gelu, depth_pre)
    grad_depth_pre = gelu_depth_vjp(grad_activated)[0].astype(jnp.bfloat16)
    grad_pad = jnp.pad(grad_depth_pre, ((1, 1), (1, 1), (0, 0)))
    grad_spread = depthwise_back(grad_pad, w_depth, row_count, col_count)
    grad_depth = kernel_grad(padded, grad_depth_pre, row_count, col_count)
    unused_spread, gelu_expand_vjp = jax.vjp(smooth_gelu, expanded)
    grad_expanded = gelu_expand_vjp(grad_spread)[0].astype(jnp.bfloat16)
    grad_expand = jnp.dot(normed_first.reshape(-1, channels).T, grad_expanded.reshape(-1, grad_expanded.shape[-1]), preferred_element_type=jnp.float32)
    grad_first = matmul_last(grad_expanded, w_expand.T)
    unused_first, norm_first_vjp = jax.vjp(norm_tokens, image_float, gain_first)
    grad_image_norm, grad_norm0 = norm_first_vjp(grad_first)
    grad_image = (grad_mixed + grad_image_norm).astype(jnp.bfloat16)
    return (block_out, grad_image, grad_norm0, grad_expand, grad_depth, grad_squeeze, grad_excite, grad_project, grad_norm1, grad_qkv, grad_out_proj, grad_bias)
```

```python
import functools

import jax
import jax.numpy as jnp
from jax import lax
from jax.experimental import pallas as pl
from jax.experimental.pallas import tpu as pltpu
from jax.sharding import PartitionSpec as P

F32 = jnp.float32
BF16 = jnp.bfloat16
MESH = pl.DeviceIdType.MESH
ROWS = 8
COLS = 16
CHIPS = 64
HEADS = 8
MEMBERS = 64
GROUPS = 16
CH = 256
ANY = pl.BlockSpec(memory_space=pl.ANY)
VMEM = pl.BlockSpec(memory_space=pltpu.VMEM)


def nn(a, b):
    return jnp.dot(a, b, preferred_element_type=F32)


def nt(a, b):
    return lax.dot_general(a, b, (((1,), (1,)), ((), ())), preferred_element_type=F32)


def tn(a, b):
    return lax.dot_general(a, b, (((0,), (0,)), ((), ())), preferred_element_type=F32)


def place():
    row = lax.axis_index("row")
    col = lax.axis_index("col")
    core = lax.rem(col, 2)
    chip = row * 8 + lax.div(col, 2)
    return row, col, core, chip


def chip_device(chip, core):
    return (lax.div(chip, 8), lax.rem(chip, 8) * 2 + core)


def each_chip(chip, body):
    def step(k, carry):
        body(k, lax.rem(chip + k, CHIPS))
        return carry

    lax.fori_loop(1, CHIPS, step, 0)


def tile_sum_kernel(x_ref, o_ref, col_slots, row_slots, send_a, recv_a, send_b, recv_b):
    row, col, _, _ = place()
    barrier = pltpu.get_barrier_semaphore()
    for k in range(1, COLS):
        pl.semaphore_signal(
            barrier, inc=1, device_id=(row, lax.rem(col + k, COLS)), device_id_type=MESH
        )
    for k in range(1, ROWS):
        pl.semaphore_signal(
            barrier, inc=1, device_id=(lax.rem(row + k, ROWS), col), device_id_type=MESH
        )
    col_slots[col] = x_ref[...]
    pl.semaphore_wait(barrier, COLS + ROWS - 2)
    copies = []
    for k in range(1, COLS):
        copy = pltpu.make_async_remote_copy(
            src_ref=x_ref,
            dst_ref=col_slots.at[col],
            send_sem=send_a.at[k],
            recv_sem=recv_a.at[k],
            device_id=(row, lax.rem(col + k, COLS)),
            device_id_type=MESH,
        )
        copy.start()
        copies.append(copy)
    for copy in copies:
        copy.wait()
    total = col_slots[0]
    for k in range(1, COLS):
        total = total + col_slots[k]
    row_slots[row] = total
    copies = []
    for k in range(1, ROWS):
        copy = pltpu.make_async_remote_copy(
            src_ref=row_slots.at[row],
            dst_ref=row_slots.at[row],
            send_sem=send_b.at[k],
            recv_sem=recv_b.at[k],
            device_id=(lax.rem(row + k, ROWS), col),
            device_id_type=MESH,
        )
        copy.start()
        copies.append(copy)
    for copy in copies:
        copy.wait()
    total = row_slots[0]
    for k in range(1, ROWS):
        total = total + row_slots[k]
    o_ref[...] = total


def tile_sum(x, collective_id):
    out = pl.pallas_call(
        tile_sum_kernel,
        out_shape=jax.ShapeDtypeStruct((8, 128), F32),
        in_specs=[VMEM],
        out_specs=VMEM,
        scratch_shapes=[
            pltpu.VMEM((COLS, 8, 128), F32),
            pltpu.VMEM((ROWS, 8, 128), F32),
            pltpu.SemaphoreType.DMA((COLS,)),
            pltpu.SemaphoreType.DMA((COLS,)),
            pltpu.SemaphoreType.DMA((ROWS,)),
            pltpu.SemaphoreType.DMA((ROWS,)),
        ],
        compiler_params=pltpu.CompilerParams(collective_id=collective_id, has_side_effects=True),
        name="tile_sum",
    )(x.reshape(8, 128))
    return out.reshape(1024)


def exchange_kernel(count, *refs):
    sources, outs = refs[:count], refs[count : 2 * count]
    send_sem, recv_sem, own_sem = refs[2 * count :]
    _, _, core, chip = place()
    barrier = pltpu.get_barrier_semaphore()

    def greet(k, peer):
        pl.semaphore_signal(
            barrier, inc=1, device_id=chip_device(peer, core), device_id_type=MESH
        )

    each_chip(chip, greet)
    own = []
    for n in range(count):
        copy = pltpu.make_async_copy(sources[n].at[chip], outs[n].at[chip], own_sem.at[n])
        copy.start()
        own.append(copy)
    pl.semaphore_wait(barrier, CHIPS - 1)

    def send(k, peer):
        for n in range(count):
            pltpu.make_async_remote_copy(
                src_ref=sources[n].at[peer],
                dst_ref=outs[n].at[chip],
                send_sem=send_sem.at[n],
                recv_sem=recv_sem.at[n],
                device_id=chip_device(peer, core),
                device_id_type=MESH,
            ).start()

    each_chip(chip, send)
    for n in range(count):
        own[n].wait()
        most = pl.ds(0, CHIPS - 1)
        pltpu.make_async_copy(sources[n].at[most], outs[n].at[most], send_sem.at[n]).wait()
        pltpu.make_async_copy(sources[n].at[most], outs[n].at[most], recv_sem.at[n]).wait()


def exchange(arrays, collective_id):
    count = len(arrays)
    shape = jax.ShapeDtypeStruct((CHIPS, GROUPS, CH), BF16)
    return pl.pallas_call(
        functools.partial(exchange_kernel, count),
        out_shape=[shape] * count,
        in_specs=[ANY] * count,
        out_specs=[ANY] * count,
        scratch_shapes=[
            pltpu.SemaphoreType.DMA((count,)),
            pltpu.SemaphoreType.DMA((count,)),
            pltpu.SemaphoreType.DMA((count,)),
        ],
        compiler_params=pltpu.CompilerParams(collective_id=collective_id, has_side_effects=True),
        name="exchange",
    )(*[a.reshape(CHIPS, GROUPS, CH) for a in arrays])


def chunk_of(ref, core, chip):
    height, width = ref.shape
    across = width // 128
    first = core * (height // 2) + lax.div(chip, across) * 16
    return ref.at[
        pl.ds(pl.multiple_of(first, 16), 16),
        pl.ds(pl.multiple_of(lax.rem(chip, across) * 128, 128), 128),
    ]


def half_of(ref, core):
    half = ref.shape[0] // 2
    return ref.at[pl.ds(pl.multiple_of(core * half, half), half)]


def weight_sum_kernel(count, *refs):
    xs = refs[:count]
    small_x = refs[count]
    outs = refs[count + 1 : 2 * count + 1]
    small_o = refs[2 * count + 1]
    rest = refs[2 * count + 2 :]
    pair_in = rest[:count]
    small_pair = rest[count]
    summed = rest[count + 1 : 2 * count + 1]
    small_summed = rest[2 * count + 1]
    slots = rest[2 * count + 2 : 3 * count + 2]
    small_slots = rest[3 * count + 2]
    pair_send, pair_recv, send_sem, recv_sem, back_send, back_recv, last_send, last_recv = rest[
        3 * count + 3 :
    ]
    _, _, core, chip = place()
    other = 1 - core
    partner = chip_device(chip, other)
    barrier = pltpu.get_barrier_semaphore()

    def greet(k, peer):
        pl.semaphore_signal(
            barrier, inc=1, device_id=chip_device(peer, core), device_id_type=MESH
        )

    pl.semaphore_signal(barrier, inc=1, device_id=partner, device_id_type=MESH)
    each_chip(chip, greet)
    pl.semaphore_wait(barrier, CHIPS)

    copies = []
    for n in range(count + 1):
        src = half_of(xs[n], other) if n < count else small_x.at[other]
        dst = pair_in[n] if n < count else small_pair
        copy = pltpu.make_async_remote_copy(
            src_ref=src,
            dst_ref=dst,
            send_sem=pair_send.at[n],
            recv_sem=pair_recv.at[n],
            device_id=partner,
            device_id_type=MESH,
        )
        copy.start()
        copies.append(copy)
    for copy in copies:
        copy.wait()
    for n in range(count):
        mine = half_of(xs[n], core)
        summed[n][...] = (mine[...].astype(F32) + pair_in[n][...].astype(F32)).astype(BF16)
    small_summed[...] = small_x[core] + small_pair[...]

    def scatter(k, peer):
        for n in range(count + 1):
            if n < count:
                src, dst = chunk_of(summed[n], 0, peer), slots[n].at[chip]
            else:
                src, dst = small_summed.at[peer], small_slots.at[chip]
            pltpu.make_async_remote_copy(
                src_ref=src,
                dst_ref=dst,
                send_sem=send_sem.at[n],
                recv_sem=recv_sem.at[n],
                device_id=chip_device(peer, core),
                device_id_type=MESH,
            ).start()

    each_chip(chip, scatter)
    most = pl.ds(0, CHIPS - 1)
    for n in range(count):
        slots[n][chip] = chunk_of(summed[n], 0, chip)[...]
    small_slots[chip] = small_summed[chip]
    for n in range(count + 1):
        buf = slots[n] if n < count else small_slots
        pltpu.make_async_copy(buf.at[most], buf.at[most], recv_sem.at[n]).wait()

    for n in range(count):
        total = jnp.sum(slots[n][...].astype(F32), axis=0)
        chunk_of(outs[n], core, chip)[...] = total.astype(BF16)
    small_o[core, chip] = jnp.sum(small_slots[...], axis=0)

    def gather(k, peer):
        for n in range(count + 1):
            piece = chunk_of(outs[n], core, chip) if n < count else small_o.at[core, chip]
            pltpu.make_async_remote_copy(
                src_ref=piece,
                dst_ref=piece,
                send_sem=back_send.at[n],
                recv_sem=back_recv.at[n],
                device_id=chip_device(peer, core),
                device_id_type=MESH,
            ).start()

    each_chip(chip, gather)
    for n in range(count + 1):
        buf = slots[n] if n < count else small_slots
        pltpu.make_async_copy(buf.at[most], buf.at[most], send_sem.at[n]).wait()
        pltpu.make_async_copy(buf.at[most], buf.at[most], back_recv.at[n]).wait()
    copies = []
    for n in range(count + 1):
        piece = half_of(outs[n], core) if n < count else small_o.at[core]
        copy = pltpu.make_async_remote_copy(
            src_ref=piece,
            dst_ref=piece,
            send_sem=last_send.at[n],
            recv_sem=last_recv.at[n],
            device_id=partner,
            device_id_type=MESH,
        )
        copy.start()
        copies.append(copy)
    for n in range(count + 1):
        buf = slots[n] if n < count else small_slots
        pltpu.make_async_copy(buf.at[most], buf.at[most], back_send.at[n]).wait()
    for copy in copies:
        copy.wait()


def weight_sum(arrays, small, collective_id):
    count = len(arrays)
    width = small.shape[-1]
    sems = [pltpu.SemaphoreType.DMA((count + 1,))] * 8
    halves = [pltpu.VMEM((a.shape[0] // 2, a.shape[1]), BF16) for a in arrays]
    half_small = pltpu.VMEM((CHIPS, 1, width), F32)
    return pl.pallas_call(
        functools.partial(weight_sum_kernel, count),
        out_shape=[jax.ShapeDtypeStruct(a.shape, BF16) for a in arrays]
        + [jax.ShapeDtypeStruct((2, CHIPS, 1, width), F32)],
        in_specs=[VMEM] * (count + 1),
        out_specs=[VMEM] * (count + 1),
        scratch_shapes=halves
        + [half_small]
        + halves
        + [half_small]
        + [pltpu.VMEM((CHIPS, 16, 128), BF16)] * count
        + [half_small]
        + sems,
        compiler_params=pltpu.CompilerParams(
            collective_id=collective_id, has_side_effects=True, vmem_limit_bytes=40 * 2**20
        ),
        name="weight_sum",
    )(*arrays, small)


def attention_kernel(
    x_ref, dy_ref, w_qkv, w_out, bias_ref, att_ref, gn_ref, gw_ref, gb_ref, qkv_s, g_s, att_s, gp_s
):
    rows = MEMBERS * GROUPS
    tile = 256
    scale = 32 ** (-0.5)

    @pl.loop(0, rows // tile)
    def _(t):
        members = tile // GROUPS
        at = pl.ds(pl.multiple_of(t * tile, tile), tile)
        x = x_ref[pl.ds(t * members, members)].reshape(tile, CH)
        dy = dy_ref[pl.ds(t * members, members)].reshape(tile, CH)
        qkv = nn(x, w_qkv[...])
        for n in range(6):
            qkv_s[n, at, :] = qkv[:, n * 128 : (n + 1) * 128]
        g = nt(dy, w_out[...])
        for n in range(2):
            g_s[n, at, :] = g[:, n * 128 : (n + 1) * 128]

    gb_ref[...] = jnp.zeros_like(gb_ref)
    head_of = lax.div(lax.broadcasted_iota(jnp.int32, (1, CH), 1), 32)
    masks_f = [(head_of == h).astype(F32) for h in range(HEADS)]
    masks = [m.astype(BF16) for m in masks_f]

    def spread_heads(a):
        return jnp.concatenate([a * m for m in masks], axis=0)

    def own_heads(r):
        total = r[0:MEMBERS] * masks_f[0]
        for h in range(1, HEADS):
            total = total + r[h * MEMBERS : (h + 1) * MEMBERS] * masks_f[h]
        return total

    @pl.loop(0, GROUPS)
    def _(group):
        at = pl.ds(group, MEMBERS, stride=GROUPS)

        def take(ref, first):
            return jnp.concatenate([ref[first, at, :], ref[first + 1, at, :]], axis=1).astype(BF16)

        def put(ref, first, value):
            value = value.astype(BF16).astype(F32)
            ref[first, at, :] = value[:, :128]
            ref[first + 1, at, :] = value[:, 128:]

        q, k, v, g = take(qkv_s, 0), take(qkv_s, 2), take(qkv_s, 4), take(g_s, 0)
        q_heads, g_heads = spread_heads(q), spread_heads(g)
        scores = nt(k, q_heads) * scale + bias_ref[...]
        lifted = jnp.exp(scores - jnp.max(scores, axis=0, keepdims=True))
        probs = lifted / jnp.sum(lifted, axis=0, keepdims=True)
        low = probs.astype(BF16)
        put(att_s, 0, own_heads(tn(low, v)))
        put(gp_s, 4, nn(low, g_heads))
        grad_probs = nt(v, g_heads)
        grad_scores = probs * (grad_probs - jnp.sum(grad_probs * probs, axis=0, keepdims=True))
        gb_ref[...] += grad_scores
        scaled = (grad_scores * scale).astype(BF16)
        put(gp_s, 0, own_heads(tn(scaled, k)))
        put(gp_s, 2, nn(scaled, q_heads))

    gw_ref[...] = jnp.zeros_like(gw_ref)

    @pl.loop(0, rows // tile)
    def _(t):
        members = tile // GROUPS
        at = pl.ds(pl.multiple_of(t * tile, tile), tile)
        x = x_ref[pl.ds(t * members, members)].reshape(tile, CH)
        dy = dy_ref[pl.ds(t * members, members)].reshape(tile, CH)
        att = jnp.concatenate([att_s[n, at, :] for n in range(2)], axis=1).astype(BF16)
        gp = jnp.concatenate([gp_s[n, at, :] for n in range(6)], axis=1).astype(BF16)
        att_ref[pl.ds(t * members, members)] = att.reshape(members, GROUPS, CH)
        gn = nt(gp, w_qkv[...]).astype(BF16)
        gn_ref[pl.ds(t * members, members)] = gn.reshape(members, GROUPS, CH)
        gw_ref[:, : 3 * CH] += tn(x, gp)
        gw_ref[:, 3 * CH :] += tn(att, dy)


def attention(x, dy, w_qkv, w_out, bias_rows):
    rows = MEMBERS * GROUPS
    grid_shape = jax.ShapeDtypeStruct((MEMBERS, GROUPS, CH), BF16)
    return pl.pallas_call(
        attention_kernel,
        out_shape=[
            grid_shape,
            grid_shape,
            jax.ShapeDtypeStruct((CH, 4 * CH), F32),
            jax.ShapeDtypeStruct((MEMBERS, HEADS * MEMBERS), F32),
        ],
        in_specs=[VMEM] * 5,
        out_specs=[VMEM] * 4,
        scratch_shapes=[
            pltpu.VMEM((6, rows, 128), F32),
            pltpu.VMEM((2, rows, 128), F32),
            pltpu.VMEM((2, rows, 128), F32),
            pltpu.VMEM((6, rows, 128), F32),
        ],
        compiler_params=pltpu.CompilerParams(vmem_limit_bytes=40 * 2**20),
        name="attention",
    )(x, dy, w_qkv, w_out, bias_rows)


def with_halo(cells, sides, width):
    for axis, dim in sides:
        count = lax.axis_size(axis)
        ends = count - 1
        head = lax.slice_in_dim(cells, 0, width, axis=dim)
        tail = lax.slice_in_dim(cells, cells.shape[dim] - width, cells.shape[dim], axis=dim)
        cells = jnp.concatenate(
            [
                lax.ppermute(tail, axis, [(i, (i + 1) % count) for i in range(ends)]),
                cells,
                lax.ppermute(head, axis, [((i + 1) % count, i) for i in range(ends)]),
            ],
            axis=dim,
        )
    return cells


def norm_tokens(values, scale_gain):
    average = jnp.mean(values, axis=-1, keepdims=True)
    centered = values - average
    variance = jnp.mean(centered * centered, axis=-1, keepdims=True)
    return centered * lax.rsqrt(variance + 1e-05) * scale_gain


def matmul_last(left_side, right_side):
    flat_rows = left_side.reshape(-1, left_side.shape[-1])
    product = jnp.dot(flat_rows, right_side, preferred_element_type=F32)
    return product.reshape(left_side.shape[:-1] + (right_side.shape[-1],))


def smooth_gelu(values):
    return jax.nn.gelu(values, approximate=True)


def depthwise(padded, kernel, row_count, col_count):
    accumulated = jnp.zeros((row_count, col_count, padded.shape[-1]), F32)
    for shift_row in range(3):
        for shift_col in range(3):
            window = padded[
                shift_row : shift_row + row_count, shift_col : shift_col + col_count
            ].astype(F32)
            accumulated = accumulated + window * kernel[shift_row, shift_col].astype(F32)
    return accumulated


def depthwise_back(padded_grad, kernel, row_count, col_count):
    accumulated = jnp.zeros((row_count, col_count, padded_grad.shape[-1]), F32)
    for shift_row in range(3):
        for shift_col in range(3):
            window = padded_grad[
                2 - shift_row : 2 - shift_row + row_count, 2 - shift_col : 2 - shift_col + col_count
            ].astype(F32)
            accumulated = accumulated + window * kernel[shift_row, shift_col].astype(F32)
    return accumulated


def kernel_grad(padded, grad_pre, row_count, col_count):
    kernel_terms = []
    for shift_row in range(3):
        for shift_col in range(3):
            window = padded[
                shift_row : shift_row + row_count, shift_col : shift_col + col_count
            ].astype(F32)
            kernel_terms.append(jnp.sum(window * grad_pre.astype(F32), axis=(0, 1)))
    return jnp.stack(kernel_terms).reshape(3, 3, padded.shape[-1])


def excite_gate(pooled, squeeze_wide, excite_wide):
    hidden = jax.nn.silu(jnp.dot(pooled[None, :], squeeze_wide, precision=lax.Precision.HIGHEST))
    return jax.nn.sigmoid(jnp.dot(hidden, excite_wide, precision=lax.Precision.HIGHEST))[0]


def on_device(
    image,
    out_cotangent,
    norm0_gain,
    w_expand,
    w_depth,
    w_squeeze,
    w_excite,
    w_project,
    norm1_gain,
    w_qkv,
    w_out,
    attn_bias,
):
    row_count, col_count, channels = image.shape
    map_shape = image.shape
    cells_total = row_count * lax.axis_size("row") * col_count * lax.axis_size("col")
    (grid_cot,) = exchange([out_cotangent], 0)
    image_float = image.astype(F32)
    gain_first = norm0_gain.astype(F32)
    gain_second = norm1_gain.astype(F32)
    normed_first = norm_tokens(image_float, gain_first).astype(BF16)
    expanded = matmul_last(normed_first, w_expand)
    spread = smooth_gelu(expanded).astype(BF16)
    padded = with_halo(spread, (("row", 0), ("col", 1)), 1)
    depth_pre = depthwise(padded, w_depth, row_count, col_count)
    activated = smooth_gelu(depth_pre)
    pooled = tile_sum(jnp.sum(activated, axis=(0, 1)), 1) / cells_total
    squeeze_wide = w_squeeze.astype(F32)
    excite_wide = w_excite.astype(F32)
    channel_gate = excite_gate(pooled, squeeze_wide, excite_wide)
    gated_act = (activated * channel_gate).astype(BF16)
    mixed_map = (image_float + matmul_last(gated_act, w_project)).astype(BF16)
    mixed_float = mixed_map.astype(F32)
    normed_second = norm_tokens(mixed_float, gain_second).astype(BF16)
    (grid_normed,) = exchange([normed_second], 2)
    bias_rows = attn_bias.transpose(2, 0, 1).reshape(MEMBERS, HEADS * MEMBERS)
    grid_att, grid_grad, grad_pair, bias_grad = attention(
        grid_normed, grid_cot, w_qkv, w_out, bias_rows
    )
    attended_map, grad_normed = exchange([grid_att, grid_grad], 3)
    attended_map = attended_map.reshape(map_shape)
    grad_normed = grad_normed.reshape(map_shape)
    block_out = (mixed_float + matmul_last(attended_map, w_out)).astype(BF16)
    unused_second, norm_second_vjp = jax.vjp(norm_tokens, mixed_float, gain_second)
    grad_mixed_norm, grad_norm1 = norm_second_vjp(grad_normed.astype(F32))
    grad_mixed = out_cotangent.astype(F32) + grad_mixed_norm
    grad_mixed_b = grad_mixed.astype(BF16)
    grad_project = jnp.dot(
        gated_act.reshape(-1, gated_act.shape[-1]).T,
        grad_mixed_b.reshape(-1, channels),
        preferred_element_type=F32,
    )
    grad_gated = matmul_last(grad_mixed_b, w_project.T)
    grad_gate = tile_sum(jnp.sum(grad_gated * activated, axis=(0, 1)), 4)
    unused_gate, gate_vjp = jax.vjp(excite_gate, pooled, squeeze_wide, excite_wide)
    grad_pooled, grad_squeeze, grad_excite = gate_vjp(grad_gate)
    grad_activated = grad_gated * channel_gate + grad_pooled / cells_total
    unused_act, gelu_depth_vjp = jax.vjp(smooth_gelu, depth_pre)
    grad_depth_pre = gelu_depth_vjp(grad_activated)[0].astype(BF16)
    grad_pad = with_halo(grad_depth_pre, (("row", 0), ("col", 1)), 1)
    grad_spread = depthwise_back(grad_pad, w_depth, row_count, col_count)
    grad_depth = kernel_grad(padded, grad_depth_pre, row_count, col_count)
    unused_spread, gelu_expand_vjp = jax.vjp(smooth_gelu, expanded)
    grad_expanded = gelu_expand_vjp(grad_spread)[0].astype(BF16)
    grad_expand = jnp.dot(
        normed_first.reshape(-1, channels).T,
        grad_expanded.reshape(-1, grad_expanded.shape[-1]),
        preferred_element_type=F32,
    )
    grad_first = matmul_last(grad_expanded, w_expand.T)
    unused_first, norm_first_vjp = jax.vjp(norm_tokens, image_float, gain_first)
    grad_image_norm, grad_norm0 = norm_first_vjp(grad_first)
    grad_image = (grad_mixed + grad_image_norm).astype(BF16)

    small = jnp.concatenate(
        [grad_norm0, grad_norm1, grad_depth.reshape(-1), bias_grad.reshape(-1)]
    )
    small = jnp.pad(small, (0, 2 * CHIPS * 384 - small.shape[0])).reshape(2, CHIPS, 1, 384)
    sum_expand, sum_project, sum_pair, sum_small = weight_sum(
        [grad_expand.astype(BF16), grad_project.astype(BF16), grad_pair.astype(BF16)], small, 5
    )
    sum_small = sum_small.reshape(-1)
    depth_end = 2 * channels + w_depth.size
    sum_bias = sum_small[depth_end : depth_end + attn_bias.size]
    return (
        block_out,
        grad_image,
        sum_small[:channels],
        sum_expand.astype(F32),
        sum_small[2 * channels : depth_end].reshape(w_depth.shape),
        grad_squeeze,
        grad_excite,
        sum_project.astype(F32),
        sum_small[channels : 2 * channels],
        sum_pair[:, : 3 * channels].astype(F32),
        sum_pair[:, 3 * channels :].astype(F32),
        sum_bias.reshape(MEMBERS, HEADS, MEMBERS).transpose(1, 2, 0),
    )


def solution(mesh):
    mapped = P("row", "col", None)
    return jax.shard_map(
        on_device,
        mesh=mesh,
        in_specs=(mapped, mapped) + (P(),) * 10,
        out_specs=(mapped, mapped) + (P(),) * 10,
        check_vma=False,
    )
```

```python
import functools

import jax
import jax.numpy as jnp
from jax import lax
from jax.experimental import pallas as pl
from jax.experimental.pallas import tpu as pltpu
from jax.sharding import PartitionSpec as P

F32 = jnp.float32
BF16 = jnp.bfloat16
MESH = pl.DeviceIdType.MESH
ROWS = 8
COLS = 16
CHIPS = 64
HEADS = 8
MEMBERS = 64
GROUPS = 16
CH = 256
MAP_ROWS = 16
MAP_COLS = 64
CELLS = MAP_ROWS * MAP_COLS
CELLS_TOTAL = 131072
LANES = 8
PAD = 80
PADDED = (MAP_ROWS + 2) * PAD
TILE = 256
SCALE = 32 ** (-0.5)
GELU_A = 0.7978845608028654
GELU_B = 0.044715


def nn(a, b):
    return jnp.dot(a, b, preferred_element_type=F32)


def nt(a, b):
    return lax.dot_general(a, b, (((1,), (1,)), ((), ())), preferred_element_type=F32)


def tn(a, b):
    return lax.dot_general(a, b, (((0,), (0,)), ((), ())), preferred_element_type=F32)


def gelu(x):
    return 0.5 * x * (1.0 + jnp.tanh(GELU_A * (x + GELU_B * (x * x * x))))


def gelu_slope(x):
    square = x * x
    t = jnp.tanh(GELU_A * (x + GELU_B * (square * x)))
    return 0.5 * (1.0 + t) + (0.5 * GELU_A) * x * (1.0 - t * t) * (1.0 + (3 * GELU_B) * square)


def centre(x):
    centered = x - jnp.mean(x, axis=-1, keepdims=True)
    rstd = lax.rsqrt(jnp.mean(centered * centered, axis=-1, keepdims=True) + 1e-05)
    return centered * rstd, rstd


def norm_back(unit, rstd, grad_unit):
    first = jnp.mean(grad_unit, axis=-1, keepdims=True)
    second = jnp.mean(grad_unit * unit, axis=-1, keepdims=True)
    return rstd * (grad_unit - first - unit * second)


def fold(x):
    return jnp.sum(x.reshape(x.shape[0] // 8, 8, x.shape[1]), axis=0)


def thirds(x):
    one = x.astype(BF16).astype(F32)
    two = (x - one).astype(BF16).astype(F32)
    three = (x - one - two).astype(BF16).astype(F32)
    return one, two, three


def stack_rows(rows):
    width = rows[0].shape[1]
    rows = list(rows) + [jnp.zeros((8 - len(rows), width), F32)]
    return jnp.concatenate(rows, axis=0).astype(BF16)


def wide_product(x, w, product):
    return jnp.sum(product(stack_rows(thirds(x)), w), axis=0, keepdims=True)


def outer(a, b):
    a1, a2, a3 = thirds(a)
    b1, b2, b3 = thirds(b)
    return tn(stack_rows([a1, a1, a2, a2, a1, a3]), stack_rows([b1, b2, b1, b2, b3, b1]))


def aligned(start, size, unit=8):
    return pl.ds(pl.multiple_of(start, unit), size)


class Place:
    def __init__(self):
        self.row = lax.axis_index("row")
        self.col = lax.axis_index("col")
        self.core = lax.rem(self.col, 2)
        self.q = lax.div(self.col, 2)
        self.chip = self.row * 8 + self.q
        self.qs = [lax.rem(self.q + k, 8) for k in range(8)]
        self.cols = [q * 2 + self.core for q in self.qs]

    def partner(self):
        return (self.row, self.q * 2 + 1 - self.core)

    def q_peer(self, k):
        return self.qs[k], (self.row, self.cols[k])

    def row_peer(self, k):
        row = lax.rem(self.row + k, ROWS)
        return row, (row, self.col)

    def beside(self, up, right):
        return (lax.rem(self.row + ROWS + up, ROWS), lax.rem(self.col + COLS + right, COLS))

    def every_peer(self, body):
        def others(k, carry):
            row = lax.rem(self.row + k, ROWS)
            for n in range(1, 8):
                body(row, self.qs[n], (row, self.cols[n]))
            return carry

        def same(k, carry):
            row = lax.rem(self.row + k, ROWS)
            body(row, self.q, (row, self.col))
            return carry

        lax.fori_loop(0, ROWS, others, 0)
        lax.fori_loop(1, ROWS, same, 0)


class Links:
    def __init__(self, sems):
        self.sems = sems
        self.used = 0
        self.sent = []

    def pair(self):
        at = self.used
        self.used += 2
        return self.sems.at[at], self.sems.at[at + 1]

    def finish(self):
        for sem, buf in self.sent:
            pltpu.make_async_copy(buf, buf, sem).wait()


def push(src, dst, send, recv, device):
    pltpu.make_async_remote_copy(
        src_ref=src,
        dst_ref=dst,
        send_sem=send,
        recv_sem=recv,
        device_id=device,
        device_id_type=MESH,
    ).start()


def arrived(buf, sem):
    pltpu.make_async_copy(buf, buf, sem).wait()


class TileSum:
    def __init__(self, me, links, x, pair_slot, slots):
        self.me, self.links = me, links
        self.x, self.pair_slot, self.slots = x, pair_slot, slots
        self.s0, self.s1 = links.pair(), links.pair()

    def start(self):
        push(self.x, self.pair_slot, *self.s0, self.me.partner())
        self.links.sent.append((self.s0[0], self.x))
        arrived(self.pair_slot, self.s0[1])
        self.slots[self.me.chip] = self.x[...] + self.pair_slot[...]
        mine = self.slots.at[self.me.chip]
        self.me.every_peer(lambda row, q, device: push(mine, mine, *self.s1, device))
        self.links.sent.append((self.s1[0], self.slots.at[pl.ds(0, CHIPS - 1)]))

    def end(self):
        arrived(self.slots.at[pl.ds(0, CHIPS - 1)], self.s1[1])
        return jnp.sum(self.slots[...], axis=0)


class BigSum:
    def __init__(self, me, links, x, pair_in, summed, slots_a, total_a, slots_b, out):
        self.me, self.links = me, links
        self.x, self.pair_in, self.summed, self.out = x, pair_in, summed, out
        self.slots_a, self.total_a, self.slots_b = slots_a, total_a, slots_b
        self.half = x.shape[0] // 2
        self.across = x.shape[1] // 128
        self.sems = [links.pair() for _ in range(6)]

    def half_of(self, ref, core):
        return ref.at[aligned(core * self.half, self.half, 128)]

    def block(self, ref, base, q, row=None):
        first = base + lax.div(q, self.across) * 128
        size = 128
        if row is not None:
            first, size = first + row * 16, 16
        lane = aligned(lax.rem(q, self.across) * 128, 128, 128)
        return ref.at[aligned(first, size, 16), lane]

    def start(self):
        push(
            self.half_of(self.x, 1 - self.me.core),
            self.pair_in,
            *self.sems[0],
            self.me.partner(),
        )
        self.links.sent.append((self.sems[0][0], self.pair_in))

    def to_q(self):
        arrived(self.pair_in, self.sems[0][1])
        mine = self.half_of(self.x, self.me.core)
        for n in range(self.half // 128):
            at = pl.ds(n * 128, 128)
            self.summed[at] = (mine[at].astype(F32) + self.pair_in[at].astype(F32)).astype(BF16)
        for k in range(1, 8):
            q, device = self.me.q_peer(k)
            push(
                self.block(self.summed, 0, q), self.slots_a.at[self.me.q], *self.sems[1], device
            )
        self.links.sent.append((self.sems[1][0], self.slots_a.at[pl.ds(0, 7)]))

    def to_rows(self):
        self.slots_a[self.me.q] = self.block(self.summed, 0, self.me.q)[...]
        arrived(self.slots_a.at[pl.ds(0, 7)], self.sems[1][1])
        self.total_a[...] = jnp.sum(self.slots_a[...].astype(F32), axis=0).astype(BF16)
        for k in range(1, 8):
            row, device = self.me.row_peer(k)
            piece = self.total_a.at[aligned(row * 16, 16, 16)]
            push(piece, self.slots_b.at[self.me.row], *self.sems[2], device)
        self.links.sent.append((self.sems[2][0], self.slots_b.at[pl.ds(0, 7)]))

    def back_rows(self):
        me = self.me
        self.slots_b[me.row] = self.total_a[aligned(me.row * 16, 16, 16)]
        arrived(self.slots_b.at[pl.ds(0, 7)], self.sems[2][1])
        total = jnp.sum(self.slots_b[...].astype(F32), axis=0).astype(BF16)
        piece = self.block(self.out, me.core * self.half, me.q, me.row)
        piece[...] = total
        for k in range(1, 8):
            _, device = me.row_peer(k)
            push(piece, piece, *self.sems[3], device)
        self.links.sent.append((self.sems[3][0], self.slots_b.at[pl.ds(0, 7)]))

    def back_q(self):
        me = self.me
        arrived(self.slots_b.at[pl.ds(0, 7)], self.sems[3][1])
        piece = self.block(self.out, me.core * self.half, me.q)
        for k in range(1, 8):
            _, device = me.q_peer(k)
            push(piece, piece, *self.sems[4], device)
        self.links.sent.append((self.sems[4][0], self.slots_a.at[pl.ds(0, 7)]))

    def back_pair(self):
        me = self.me
        arrived(self.slots_a.at[pl.ds(0, 7)], self.sems[4][1])
        piece = self.half_of(self.out, me.core)
        push(piece, piece, *self.sems[5], me.partner())
        self.links.sent.append((self.sems[5][0], self.pair_in))

    def end(self):
        arrived(self.pair_in, self.sems[5][1])


class DirectSum(BigSum):
    def __init__(self, me, links, x, pair_in, summed, slots, out):
        super().__init__(me, links, x, pair_in, summed, None, None, None, out)
        self.slots = slots

    def scatter(self):
        me = self.me
        arrived(self.pair_in, self.sems[0][1])
        mine = self.half_of(self.x, me.core)
        for n in range(self.half // 128):
            at = pl.ds(n * 128, 128)
            self.summed[at] = (mine[at].astype(F32) + self.pair_in[at].astype(F32)).astype(BF16)

        def send(row, q, device):
            push(
                self.block(self.summed, 0, q, row), self.slots.at[me.chip], *self.sems[1], device
            )

        me.every_peer(send)
        self.slots[me.chip] = self.block(self.summed, 0, me.q, me.row)[...]
        self.links.sent.append((self.sems[1][0], self.slots.at[pl.ds(0, CHIPS - 1)]))

    def gather(self):
        me = self.me
        arrived(self.slots.at[pl.ds(0, CHIPS - 1)], self.sems[1][1])
        piece = self.block(self.out, me.core * self.half, me.q, me.row)
        piece[...] = jnp.sum(self.slots[...].astype(F32), axis=0).astype(BF16)
        me.every_peer(lambda row, q, device: push(piece, piece, *self.sems[2], device))
        self.links.sent.append((self.sems[2][0], self.slots.at[pl.ds(0, CHIPS - 1)]))

    def back_pair(self):
        me = self.me
        arrived(self.slots.at[pl.ds(0, CHIPS - 1)], self.sems[2][1])
        piece = self.half_of(self.out, me.core)
        push(piece, piece, *self.sems[5], me.partner())
        self.links.sent.append((self.sems[5][0], self.pair_in))


class SmallSum:
    def __init__(self, me, links, x, pair_in, summed, slots_a, slots_b, out):
        self.me, self.links = me, links
        self.x, self.pair_in, self.summed, self.out = x, pair_in, summed, out
        self.slots_a, self.slots_b = slots_a, slots_b
        self.sems = [links.pair() for _ in range(4)]

    def start(self):
        push(self.x, self.pair_in, *self.sems[0], self.me.partner())
        self.links.sent.append((self.sems[0][0], self.pair_in))

    def to_q(self):
        arrived(self.pair_in, self.sems[0][1])
        self.summed[...] = self.x[...] + self.pair_in[...]
        for k in range(1, 8):
            q, device = self.me.q_peer(k)
            piece = self.summed.at[aligned(q * 8, 8)]
            push(piece, self.slots_a.at[self.me.q], *self.sems[1], device)
        self.links.sent.append((self.sems[1][0], self.slots_a.at[pl.ds(0, 7)]))

    def to_rows(self):
        me = self.me
        self.slots_a[me.q] = self.summed[aligned(me.q * 8, 8)]
        arrived(self.slots_a.at[pl.ds(0, 7)], self.sems[1][1])
        self.slots_b[me.row] = jnp.sum(self.slots_a[...], axis=0)
        for k in range(1, 8):
            _, device = me.row_peer(k)
            piece = self.slots_b.at[me.row]
            push(piece, piece, *self.sems[2], device)
        self.links.sent.append((self.sems[2][0], self.slots_b.at[pl.ds(0, 7)]))

    def back_q(self):
        me = self.me
        arrived(self.slots_b.at[pl.ds(0, 7)], self.sems[2][1])
        piece = self.out.at[aligned(me.q * 8, 8)]
        piece[...] = jnp.sum(self.slots_b[...], axis=0)
        for k in range(1, 8):
            _, device = me.q_peer(k)
            push(piece, piece, *self.sems[3], device)
        self.links.sent.append((self.sems[3][0], self.slots_a.at[pl.ds(0, 7)]))

    def end(self):
        arrived(self.slots_a.at[pl.ds(0, 7)], self.sems[3][1])


class Exchange:
    def __init__(self, me, links, src, dst):
        self.me, self.links, self.src, self.dst = me, links, src, dst
        self.sems = links.pair()

    def send(self, row, k):
        q, col = self.me.qs[k], self.me.cols[k]
        push(self.src.at[row * 8 + q], self.dst.at[self.me.chip], *self.sems, (row, col))

    def send_row(self, row):
        for k in range(1, 8):
            self.send(row, k)

        @pl.when(row != self.me.row)
        def _():
            self.send(row, 0)

    def send_tile(self, t):
        for k in range(2):
            self.send_row(t * 2 + lax.rem(self.me.row + k, 2))

    def end(self):
        self.dst[self.me.chip] = self.src[self.me.chip]
        arrived(self.dst.at[pl.ds(0, CHIPS - 1)], self.sems[1])
        self.links.sent.append((self.sems[0], self.dst.at[pl.ds(0, CHIPS - 1)]))


class Halo:
    def __init__(
        self, me, links, rows_out, cols_out, corners_out, rows_in, cols_in, corners_in
    ):
        self.me, self.links = me, links
        self.rows_out, self.cols_out, self.corners_out = rows_out, cols_out, corners_out
        self.rows_in, self.cols_in, self.corners_in = rows_in, cols_in, corners_in
        self.sems = [links.pair() for _ in range(3)]

    def start(self):
        me = self.me
        for side, up in ((0, -1), (1, 1)):
            push(
                self.rows_out[side],
                self.rows_in.at[1 - side],
                *self.sems[0],
                me.beside(up, 0),
            )
        for side, right in ((0, -1), (1, 1)):
            strip = self.cols_out.at[side]
            push(strip, self.cols_in.at[1 - side], *self.sems[1], me.beside(0, right))
            for end, up in ((0, -1), (1, 1)):
                push(
                    self.corners_out[end * 2 + side],
                    self.corners_in.at[(1 - end) * 2 + 1 - side],
                    *self.sems[2],
                    me.beside(up, right),
                )

    def end(self):
        for n, buf in enumerate((self.rows_in, self.cols_in, self.corners_in)):
            arrived(buf, self.sems[n][1])
            self.links.sent.append((self.sems[n][0], buf))


IN_NAMES = ["image", "norm0_gain", "norm1_gain", "w_depth", "w_expand"]
LATE = dict(
    dy=((MEMBERS, GROUPS, CH), BF16),
    w_out=((CH, CH), BF16),
    bias=((HEADS, MEMBERS, MEMBERS), F32),
    w_squeeze_t=((64, 1024), BF16),
    w_excite=((64, 1024), BF16),
    w_project=((1024, CH), BF16),
    w_qkv=((CH, 768), BF16),
)
OUTS = dict(
    out_map=((MAP_ROWS, MAP_COLS, CH), BF16),
    grad_map=((MAP_ROWS, MAP_COLS, CH), BF16),
    sum_expand=((CH, 1024), BF16),
    sum_project=((1024, CH), BF16),
    sum_pair=((CH, 1024), BF16),
    sum_bias=((MEMBERS, 512), F32),
    sum_small=((64, 256), F32),
    gate_rows=((8, 1024), F32),
)


def big_scratch(name, rows, width):
    return {
        name + "_x": ((rows, width), BF16),
        name + "_pair": ((rows // 2, width), BF16),
        name + "_summed": ((rows // 2, width), BF16),
        name + "_a": ((8, 128, 128), BF16),
        name + "_total": ((128, 128), BF16),
        name + "_b": ((8, 16, 128), BF16),
    }


def small_scratch(name, width):
    return {
        name + "_x": ((64, width), F32),
        name + "_pair": ((64, width), F32),
        name + "_summed": ((64, width), F32),
        name + "_a": ((8, 8, width), F32),
        name + "_b": ((8, 8, width), F32),
    }


def tile_scratch(name):
    return {
        name + "_x": ((8, 128), F32),
        name + "_pair": ((8, 128), F32),
        name + "_slots": ((CHIPS, 8, 128), F32),
    }


SCRATCH = dict(
    taps=((16, 1024), F32),
    normed=((CELLS, CH), BF16),
    normed_t=((CH, CELLS), BF16),
    spread=((LANES, PADDED, 128), F32),
    expanded=((LANES, CELLS, 128), F32),
    depth=((LANES, CELLS, 128), F32),
    act=((LANES, CELLS, 128), BF16),
    pool_acc=((LANES, 8, 128), F32),
    edge_cols=((2, 16, CH), BF16),
    edge_rows_in=((2, MAP_COLS, CH), BF16),
    edge_cols_in=((2, 16, CH), BF16),
    edge_corners_in=((4, 16, CH), BF16),
    gate=((1, 1024), F32),
    gate_back=((1, 1024), F32),
    mixed=((CELLS, CH), BF16),
    normed_two=((MEMBERS, GROUPS, CH), BF16),
    grid_x=((MEMBERS, GROUPS, CH), BF16),
    grid_dy=((MEMBERS, GROUPS, CH), BF16),
    qkv=((6, CELLS, 128), F32),
    grid_g=((2, CELLS, 128), F32),
    att_rows=((2, CELLS, 128), F32),
    packed_back=((6, CELLS, 128), F32),
    probs=((GROUPS, MEMBERS, 512), F32),
    bias_t=((MEMBERS, 512), F32),
    att_out=((MEMBERS, GROUPS, CH), BF16),
    att_in=((MEMBERS, GROUPS, CH), BF16),
    gn_out=((MEMBERS, GROUPS, CH), BF16),
    gn_in=((MEMBERS, GROUPS, CH), BF16),
    grad_mixed=((CELLS, CH), F32),
    grad_mixed_b=((CELLS, CH), BF16),
    grad_gated=((LANES, CELLS, 128), F32),
    gate_acc=((LANES, 8, 128), F32),
    grad_pre=((LANES, PADDED, 128), F32),
    pre_rows=((2, LANES, MAP_COLS, 128), BF16),
    pre_cols=((2, LANES, 16, 128), BF16),
    pre_rows_in=((2, LANES, MAP_COLS, 128), BF16),
    pre_cols_in=((2, LANES, 16, 128), BF16),
    pre_corners=((4, 16, 128), BF16),
    pre_corners_in=((4, 16, 128), BF16),
    tap_acc=((LANES, 9, 8, 128), F32),
    grad_exp=((LANES, CELLS, 128), BF16),
    norm_acc=((2, 8, CH), F32),
    pair_acc=((CH, 1024), F32),
    **tile_scratch("pool"),
    **tile_scratch("gateg"),
    expand_x=((CH, 1024), BF16),
    expand_pair=((CH // 2, 1024), BF16),
    expand_summed=((CH // 2, 1024), BF16),
    expand_slots=((CHIPS, 16, 128), BF16),
    **big_scratch("project", 1024, CH),
    **big_scratch("pair", CH, 1024),
    **small_scratch("bias", 512),
    **small_scratch("small", 256),
)
SEMS = 96


class Refs:
    pass


def lanes_of(ref, first, at):
    return jnp.concatenate([ref[first, at, :], ref[first + 1, at, :]], axis=1)


def map_rows(t, count=4):
    return pl.ds(t * count, count)


def cell_rows(t):
    return aligned(t * TILE, TILE, TILE)


def pad_row(row, col=0):
    return pl.multiple_of(row * PAD + col, 8)


def block_kernel(*args):
    r = Refs()
    names = IN_NAMES + ["hbm_" + n for n in LATE] + ["hbm_" + n for n in OUTS]
    names += list(LATE) + list(OUTS) + list(SCRATCH) + ["sems", "late_sems", "out_sems"]
    for name, ref in zip(names, args, strict=True):
        setattr(r, name, ref)
    me = Place()
    links = Links(r.sems)

    def late(name):
        at = list(LATE).index(name)
        return pltpu.make_async_copy(
            getattr(r, "hbm_" + name), getattr(r, name), r.late_sems.at[at]
        )

    def flush(name):
        at = list(OUTS).index(name)
        return pltpu.make_async_copy(
            getattr(r, name), getattr(r, "hbm_" + name), r.out_sems.at[at]
        )

    for name in LATE:
        late(name).start()
    gain_first = r.norm0_gain[...].astype(F32).reshape(1, CH)
    gain_second = r.norm1_gain[...].astype(F32).reshape(1, CH)
    for a in range(3):
        r.taps[a * 3 : a * 3 + 3, :] = r.w_depth[a].astype(F32)
    off = r.image.shape[0] - 1

    barrier = pltpu.get_barrier_semaphore()

    def greet(row, q, device):
        pl.semaphore_signal(barrier, inc=1, device_id=device, device_id_type=MESH)

    me.every_peer(greet)
    for up in (-1, 0, 1):
        for right in (-1, 1):
            pl.semaphore_signal(
                barrier, inc=1, device_id=me.beside(up, right), device_id_type=MESH
            )

    for side, col in ((0, 0), (1, MAP_COLS - 16)):
        rows = []
        for i in range(MAP_ROWS):
            part = r.image[i, col : col + 16, :].astype(F32)
            rows.append(part[0:1] if side == 0 else part[15:16])
        r.edge_cols[side] = jnp.concatenate(rows, axis=0).astype(BF16)

    @pl.loop(0, 4)
    def _(t):
        x = r.image[map_rows(t)].reshape(TILE, CH).astype(F32)
        unit, _ = centre(x)
        r.normed[cell_rows(t)] = (unit * gain_first).astype(BF16)

    @pl.loop(0, 4)
    def _(t):
        @pl.loop(0, 4)
        def _(c):
            e = nn(r.normed[cell_rows(t)], r.w_expand[:, aligned(c * 256, 256, 256)])
            s = gelu(e).astype(BF16).astype(F32)
            for h in range(2):
                lane = slice(h * 128, (h + 1) * 128)
                r.expanded[2 * c + h, cell_rows(t), :] = e[:, lane]
                for a in range(4):
                    at = pl.ds(pad_row(1 + t * 4 + a, 8), MAP_COLS)
                    r.spread[2 * c + h, at, :] = s[a * 64 : (a + 1) * 64, lane]

    pl.semaphore_wait(barrier, CHIPS + 5)
    halo = Halo(
        me,
        links,
        (r.image.at[0], r.image.at[off]),
        r.edge_cols,
        [r.edge_cols.at[side] for side in (0, 1, 0, 1)],
        r.edge_rows_in,
        r.edge_cols_in,
        r.edge_corners_in,
    )
    halo.start()
    late("dy").wait()
    dy_out = Exchange(me, links, r.dy, r.grid_dy)

    @pl.loop(0, LANES * 4)
    def _(n):
        c, t = lax.div(n, 4), lax.rem(n, 4)
        row = lax.rem(me.row + c, ROWS)
        for k in range(2):
            q = lax.rem(me.q + t * 2 + k, 8)

            @pl.when(row * 8 + q != me.chip)
            def _():
                push(
                    r.dy.at[row * 8 + q],
                    r.grid_dy.at[me.chip],
                    *dy_out.sems,
                    (row, q * 2 + me.core),
                )

        r.expanded[c, cell_rows(t), :] = gelu_slope(r.expanded[c, cell_rows(t), :])

    halo.end()

    up_ok = (me.row > 0).astype(F32)
    down_ok = (me.row < ROWS - 1).astype(F32)
    left_ok = (me.col > 0).astype(F32)
    right_ok = (me.col < COLS - 1).astype(F32)
    around = jnp.concatenate(
        [
            r.edge_rows_in[0].astype(F32) * up_ok,
            r.edge_rows_in[1].astype(F32) * down_ok,
            r.edge_cols_in[0].astype(F32) * left_ok,
            r.edge_cols_in[1].astype(F32) * right_ok,
            r.edge_corners_in[0].astype(F32)[8:16] * (up_ok * left_ok),
            r.edge_corners_in[1].astype(F32)[8:16] * (up_ok * right_ok),
            r.edge_corners_in[2].astype(F32)[0:8] * (down_ok * left_ok),
            r.edge_corners_in[3].astype(F32)[0:8] * (down_ok * right_ok),
        ],
        axis=0,
    )
    unit, _ = centre(around)
    around_normed = (unit * gain_first).astype(BF16)
    last = (MAP_ROWS + 1) * PAD
    for c in range(4):
        s = gelu(nn(around_normed, r.w_expand[:, c * 256 : (c + 1) * 256]))
        s = s.astype(BF16).astype(F32)
        for h in range(2):
            v = s[:, h * 128 : (h + 1) * 128]
            n = 2 * c + h
            r.spread[n, 8:72, :] = v[0:64]
            r.spread[n, last + 8 : last + 72, :] = v[64:128]
            r.spread[n, pl.ds(PAD + 7, MAP_ROWS, stride=PAD), :] = v[128:144]
            r.spread[n, pl.ds(PAD + 72, MAP_ROWS, stride=PAD), :] = v[144:160]
            r.spread[n, 7:8, :] = v[167:168]
            r.spread[n, 72:73, :] = v[175:176]
            r.spread[n, last + 7 : last + 8, :] = v[176:177]
            r.spread[n, last + 72 : last + 73, :] = v[184:185]

    def taps_of(c):
        lane = aligned(c * 128, 128, 128)
        return [r.taps[k : k + 1, lane] for k in range(9)]

    @pl.loop(0, LANES)
    def _(c):
        taps = taps_of(c)

        def block(n, total):
            sums = [None] * 4
            for row in range(6):
                view = r.spread.at[c, pl.ds(pad_row(n * 4 + row), PAD)]
                for b in range(3):
                    v = view[pl.ds(7 + b, MAP_COLS), :]
                    for a in range(3):
                        i = row - a
                        if 0 <= i < 4:
                            term = v * taps[a * 3 + b]
                            sums[i] = term if sums[i] is None else sums[i] + term
            for i in range(4):
                at = aligned((n * 4 + i) * MAP_COLS, MAP_COLS, MAP_COLS)
                r.depth[c, at, :] = sums[i]
                value = gelu(sums[i])
                r.act[c, at, :] = value.astype(BF16)
                total = total + fold(value)
            return total

        total = lax.fori_loop(0, 4, block, jnp.zeros((8, 128), F32))
        r.pool_x[pl.ds(c, 1), :] = jnp.sum(total, axis=0, keepdims=True)

    pool = TileSum(me, links, r.pool_x, r.pool_pair, r.pool_slots)
    pool.start()

    @pl.loop(0, LANES * 4)
    def _(n):
        c, t = lax.div(n, 4), lax.rem(n, 4)
        r.depth[c, cell_rows(t), :] = gelu_slope(r.depth[c, cell_rows(t), :])

    dy_out.end()
    late("w_out").wait()
    late("bias").wait()

    @pl.loop(0, 4)
    def _(t):
        dy = r.grid_dy[map_rows(t, 16)].reshape(TILE, CH)
        g = nt(dy, r.w_out[...])
        for n in range(2):
            r.grid_g[n, cell_rows(t), :] = g[:, n * 128 : (n + 1) * 128]

    for h in range(0, HEADS, 2):
        both = jnp.concatenate([r.bias[h], r.bias[h + 1]], axis=0)
        r.bias_t[:, h * 64 : (h + 2) * 64] = both.T
    for t in range(4):
        r.normed_t[:, t * TILE : (t + 1) * TILE] = r.normed[t * TILE : (t + 1) * TILE].T

    def flat(tile):
        return jnp.concatenate([tile[n : n + 1] for n in range(8)], axis=1)

    pooled = flat(pool.end()) * (1.0 / CELLS_TOTAL)
    for name in ("w_squeeze_t", "w_excite", "w_project", "w_qkv"):
        late(name).wait()
    squeezed = wide_product(pooled, r.w_squeeze_t[...], nt)
    open_part = jax.nn.sigmoid(squeezed)
    hidden = squeezed * open_part
    gate = jax.nn.sigmoid(wide_product(hidden, r.w_excite[...], nn))
    r.gate[...] = gate

    grid_out = Exchange(me, links, r.normed_two, r.grid_x)
    start_tile = lax.div(me.row, 2)

    @pl.loop(0, 4)
    def _(step):
        t = lax.rem(start_tile + step, 4)
        total = r.image[map_rows(t)].reshape(TILE, CH).astype(F32)
        for c in range(4):
            lane = slice(c * 256, (c + 1) * 256)
            gated = lanes_of(r.act, 2 * c, cell_rows(t)).astype(F32) * r.gate[:, lane]
            total = total + nn(gated.astype(BF16), r.w_project[lane, :])
        mixed = total.astype(BF16)
        r.mixed[cell_rows(t)] = mixed
        unit, _ = centre(mixed.astype(F32))
        normed = (unit * gain_second).astype(BF16)
        r.normed_two[map_rows(t, 16)] = normed.reshape(16, GROUPS, CH)
        grid_out.send_tile(t)

    grid_out.end()

    @pl.loop(0, 4)
    def _(t):
        x = r.grid_x[map_rows(t, 16)].reshape(TILE, CH)
        qkv = nn(x, r.w_qkv[...])
        for n in range(6):
            r.qkv[n, cell_rows(t), :] = qkv[:, n * 128 : (n + 1) * 128]

    head_of = lax.div(lax.broadcasted_iota(jnp.int32, (1, 128), 1), 32)
    masks_f = [(head_of == h).astype(F32) for h in range(4)]
    masks = [m.astype(BF16) for m in masks_f]
    unroll = 4

    def spread_heads(a):
        return jnp.concatenate([a * m for m in masks], axis=0)

    def own_heads(v):
        total = v[0:MEMBERS] * masks_f[0]
        for h in range(1, 4):
            total = total + v[h * MEMBERS : (h + 1) * MEMBERS] * masks_f[h]
        return total

    def put(ref, n, at, value):
        ref[n, at, :] = value.astype(BF16).astype(F32)

    def group_forward(group):
        at = pl.ds(group, MEMBERS, stride=GROUPS)
        for n in range(2):
            q, k, v = [r.qkv[part * 2 + n, at, :].astype(BF16) for part in range(3)]
            lanes = slice(n * 256, (n + 1) * 256)
            scores = nt(k, spread_heads(q)) * SCALE + r.bias_t[:, lanes]
            lifted = jnp.exp(scores - jnp.max(scores, axis=0, keepdims=True))
            probs = lifted * (1.0 / jnp.sum(lifted, axis=0, keepdims=True))
            r.probs[group, :, lanes] = probs
            put(r.att_rows, n, at, own_heads(tn(probs.astype(BF16), v)))

    def group_back(group):
        at = pl.ds(group, MEMBERS, stride=GROUPS)
        bias_parts = []
        for n in range(2):
            q, k, v = [r.qkv[part * 2 + n, at, :].astype(BF16) for part in range(3)]
            lanes = slice(n * 256, (n + 1) * 256)
            q_heads = spread_heads(q)
            g_heads = spread_heads(r.grid_g[n, at, :].astype(BF16))
            probs = r.probs[group, :, lanes]
            put(r.packed_back, 4 + n, at, nn(probs.astype(BF16), g_heads))
            grad_probs = nt(v, g_heads)
            grad_scores = probs * (
                grad_probs - jnp.sum(grad_probs * probs, axis=0, keepdims=True)
            )
            bias_parts.append(grad_scores)
            scaled = (grad_scores * SCALE).astype(BF16)
            put(r.packed_back, n, at, own_heads(tn(scaled, k)))
            put(r.packed_back, 2 + n, at, nn(scaled, q_heads))
        return bias_parts

    @pl.loop(0, GROUPS // unroll)
    def _(step):
        for n in range(unroll):
            group_forward(step * unroll + n)

    @pl.loop(0, 4)
    def _(t):
        att = lanes_of(r.att_rows, 0, cell_rows(t)).astype(BF16)
        r.att_out[map_rows(t, 16)] = att.reshape(16, GROUPS, CH)

    att_back = Exchange(me, links, r.att_out, r.att_in)
    r.bias_x[...] = jnp.zeros_like(r.bias_x)

    @pl.loop(0, GROUPS // unroll)
    def _(step):
        for n in range(2):
            att_back.send_row(lax.rem(me.row + step * 2 + n, ROWS))
        total = group_back(step * unroll)
        for n in range(1, unroll):
            total = [a + b for a, b in zip(total, group_back(step * unroll + n))]
        for n in range(2):
            r.bias_x[:, n * 256 : (n + 1) * 256] += total[n]

    def packed_tile(t):
        parts = [r.packed_back[n, cell_rows(t), :] for n in range(6)]
        return jnp.concatenate(parts, axis=1).astype(BF16)

    gn_back = Exchange(me, links, r.gn_out, r.gn_in)

    @pl.loop(0, 4)
    def _(step):
        t = lax.rem(start_tile + step, 4)
        gn = nt(packed_tile(t), r.w_qkv[...]).astype(BF16)
        r.gn_out[map_rows(t, 16)] = gn.reshape(16, GROUPS, CH)
        gn_back.send_tile(t)

    bias_sum = SmallSum(
        me, links, r.bias_x, r.bias_pair, r.bias_summed, r.bias_a, r.bias_b, r.sum_bias
    )
    bias_sum.start()
    r.pair_acc[...] = jnp.zeros_like(r.pair_acc)

    @pl.loop(0, 4)
    def _(t):
        x = r.grid_x[map_rows(t, 16)].reshape(TILE, CH)
        dy = r.grid_dy[map_rows(t, 16)].reshape(TILE, CH)
        att = r.att_out[map_rows(t, 16)].reshape(TILE, CH)
        r.pair_acc[:, : 3 * CH] += tn(x, packed_tile(t))
        r.pair_acc[:, 3 * CH :] += tn(att, dy)

    r.pair_x[...] = r.pair_acc[...].astype(BF16)

    def big(name, out):
        parts = ["x", "pair", "summed", "a", "total", "b"]
        return BigSum(me, links, *[getattr(r, name + "_" + p) for p in parts], out)

    pair_sum = big("pair", r.sum_pair)
    pair_sum.start()
    gn_back.end()

    r.norm_acc[...] = jnp.zeros_like(r.norm_acc)
    r.gate_acc[...] = jnp.zeros_like(r.gate_acc)

    @pl.loop(0, 4)
    def _(t):
        unit, rstd = centre(r.mixed[cell_rows(t)].astype(F32))
        gn = r.gn_in[map_rows(t, 16)].reshape(TILE, CH).astype(F32)
        r.norm_acc[1] += fold(gn * unit)
        dy = r.dy[map_rows(t, 16)].reshape(TILE, CH).astype(F32)
        grad = dy + norm_back(unit, rstd, gn * gain_second)
        r.grad_mixed[cell_rows(t)] = grad
        grad_b = grad.astype(BF16)
        r.grad_mixed_b[cell_rows(t)] = grad_b
        for c in range(4):
            gg = nt(grad_b, r.w_project[c * 256 : (c + 1) * 256, :])
            for h in range(2):
                n = 2 * c + h
                part = gg[:, h * 128 : (h + 1) * 128]
                r.grad_gated[n, cell_rows(t), :] = part
                r.gate_acc[n] += fold(part * r.act[n, cell_rows(t), :].astype(F32))

    for n in range(LANES):
        r.gateg_x[n : n + 1, :] = jnp.sum(r.gate_acc[n], axis=0, keepdims=True)
    gate_sum = TileSum(me, links, r.gateg_x, r.gateg_pair, r.gateg_slots)
    gate_sum.start()

    att_back.end()

    @pl.loop(0, 4)
    def _(t):
        att = r.att_in[map_rows(t, 16)].reshape(TILE, CH)
        value = r.mixed[cell_rows(t)].astype(F32) + nn(att, r.w_out[...])
        r.out_map[map_rows(t)] = value.astype(BF16).reshape(4, MAP_COLS, CH)

    flush("out_map").start()
    grad_t = r.grad_mixed_b[...].T
    for c in range(4):
        lane = slice(c * 256, (c + 1) * 256)
        product = nn(grad_t, lanes_of(r.act, 2 * c, slice(None))) * r.gate[:, lane]
        r.project_x[lane, :] = product.T.astype(BF16)
    project_sum = big("project", r.sum_project)
    grad_gate = flat(gate_sum.end())
    grad_logit = grad_gate * gate * (1.0 - gate)
    grad_hidden = wide_product(grad_logit, r.w_excite[...], nt)
    grad_squeezed = grad_hidden * (open_part * (1.0 + squeezed * (1.0 - open_part)))
    r.gate_back[...] = wide_product(grad_squeezed, r.w_squeeze_t[...], nn) * (1.0 / CELLS_TOTAL)

    @pl.loop(0, LANES)
    def _(c):
        lane = aligned(c * 128, 128, 128)
        scale, shift = r.gate[:, lane], r.gate_back[:, lane]
        for t in range(4):
            at = slice(t * TILE, (t + 1) * TILE)
            g = (r.grad_gated[c, at, :] * scale + shift) * r.depth[c, at, :]
            g = g.astype(BF16).astype(F32)
            for a in range(4):
                first = (1 + t * 4 + a) * PAD + 8
                r.grad_pre[c, first : first + MAP_COLS, :] = g[a * 64 : (a + 1) * 64]

        for side, row in ((0, 1), (1, MAP_ROWS)):
            at = pl.ds(row * PAD + 8, MAP_COLS)
            r.pre_rows[side, c] = r.grad_pre[c, at, :].astype(BF16)
        for side, col in ((0, 8), (1, 71)):
            at = pl.ds(PAD + col, MAP_ROWS, stride=PAD)
            r.pre_cols[side, c] = r.grad_pre[c, at, :].astype(BF16)

    for corner, at in enumerate((PAD + 8, PAD + 71, last - PAD + 8, last - PAD + 71)):
        cells = [r.grad_pre[c, at : at + 1, :] for c in range(LANES)]
        cells.append(jnp.zeros((8, 128), F32))
        r.pre_corners[corner] = jnp.concatenate(cells, axis=0).astype(BF16)

    pre_halo = Halo(
        me,
        links,
        (r.pre_rows.at[0], r.pre_rows.at[1]),
        r.pre_cols,
        [r.pre_corners.at[n] for n in range(4)],
        r.pre_rows_in,
        r.pre_cols_in,
        r.pre_corners_in,
    )
    pre_halo.start()

    project_sum.start()
    bias_sum.to_q()
    pair_sum.to_q()
    project_sum.to_q()
    pre_halo.end()

    @pl.loop(0, LANES)
    def _(c):
        r.grad_pre[c, 8:72, :] = r.pre_rows_in[0, c].astype(F32) * up_ok
        r.grad_pre[c, last + 8 : last + 72, :] = r.pre_rows_in[1, c].astype(F32) * down_ok
        left = r.pre_cols_in[0, c].astype(F32) * left_ok
        right = r.pre_cols_in[1, c].astype(F32) * right_ok
        r.grad_pre[c, pl.ds(PAD + 7, MAP_ROWS, stride=PAD), :] = left
        r.grad_pre[c, pl.ds(PAD + 72, MAP_ROWS, stride=PAD), :] = right

    corners = (
        (7, up_ok * left_ok),
        (72, up_ok * right_ok),
        (last + 7, down_ok * left_ok),
        (last + 72, down_ok * right_ok),
    )
    for corner, (at, ok) in enumerate(corners):
        cells = r.pre_corners_in[corner].astype(F32) * ok
        for c in range(LANES):
            r.grad_pre[c, at : at + 1, :] = cells[c : c + 1]

    r.tap_acc[...] = jnp.zeros_like(r.tap_acc)

    def depth_back(c):
        taps = taps_of(c)

        @pl.loop(0, MAP_ROWS // 2)
        def _(n):
            sums = [None] * 2
            inner = [
                r.spread[c, pl.ds(pad_row(1 + n * 2 + i, 8), MAP_COLS), :] for i in range(2)
            ]
            for b in range(3):
                parts = [None] * 3
                for row in range(4):
                    view = r.grad_pre.at[c, pl.ds(pad_row(n * 2 + row), PAD)]
                    v = view[pl.ds(7 + b, MAP_COLS), :]
                    for a in range(3):
                        i = row - a
                        if 0 <= i < 2:
                            term = v * taps[(2 - a) * 3 + 2 - b]
                            sums[i] = term if sums[i] is None else sums[i] + term
                            part = fold(v * inner[i])
                            parts[a] = part if parts[a] is None else parts[a] + part
                for a in range(3):
                    r.tap_acc[c, (2 - a) * 3 + 2 - b] += parts[a]
            for i in range(2):
                at = aligned((n * 2 + i) * MAP_COLS, MAP_COLS, MAP_COLS)
                r.grad_exp[c, at, :] = (sums[i] * r.expanded[c, at, :]).astype(BF16)

    @pl.loop(0, LANES)
    def _(c):
        depth_back(c)

    for c in range(4):
        lane = slice(c * 256, (c + 1) * 256)
        product = nn(r.normed_t[...], lanes_of(r.grad_exp, 2 * c, slice(None)))
        r.expand_x[:, lane] = product.astype(BF16)
    expand_sum = DirectSum(
        me, links, r.expand_x, r.expand_pair, r.expand_summed, r.expand_slots, r.sum_expand
    )
    expand_sum.start()
    bias_sum.to_rows()
    pair_sum.to_rows()
    expand_sum.scatter()
    project_sum.to_rows()

    @pl.loop(0, 4)
    def _(t):
        grad = None
        for c in range(4):
            lane = slice(c * 256, (c + 1) * 256)
            part = nt(lanes_of(r.grad_exp, 2 * c, cell_rows(t)), r.w_expand[:, lane])
            grad = part if grad is None else grad + part
        unit, rstd = centre(r.image[map_rows(t)].reshape(TILE, CH).astype(F32))
        r.norm_acc[0] += fold(grad * unit)
        value = r.grad_mixed[cell_rows(t)] + norm_back(unit, rstd, grad * gain_first)
        r.grad_map[map_rows(t)] = value.astype(BF16).reshape(4, MAP_COLS, CH)

    r.small_x[...] = jnp.zeros_like(r.small_x)
    for c in range(LANES):
        rows = [jnp.sum(r.tap_acc[c, k], axis=0, keepdims=True) for k in range(9)]
        r.small_x[c * 8 : c * 8 + 8, :128] = jnp.concatenate(rows[:8], axis=0)
        r.small_x[c * 8 : c * 8 + 1, 128:] = rows[8]
    for n in range(2):
        sums = jnp.sum(r.norm_acc[n], axis=0, keepdims=True)
        for c in range(2):
            at = c * 8 + 1 + n
            r.small_x[at : at + 1, 128:] = sums[:, c * 128 : (c + 1) * 128]
    small_sum = SmallSum(
        me, links, r.small_x, r.small_pair, r.small_summed, r.small_a, r.small_b, r.sum_small
    )
    flush("grad_map").start()
    small_sum.start()
    bias_sum.back_q()
    pair_sum.back_rows()
    small_sum.to_q()
    expand_sum.gather()
    project_sum.back_rows()
    pair_sum.back_q()
    small_sum.to_rows()
    bias_sum.end()
    flush("sum_bias").start()
    project_sum.back_q()
    small_sum.back_q()
    pair_sum.back_pair()
    expand_sum.back_pair()
    pair_sum.end()
    flush("sum_pair").start()
    project_sum.back_pair()
    small_sum.end()
    flush("sum_small").start()
    rows = [pooled, grad_logit, jnp.pad(hidden, ((0, 0), (0, 960)))]
    rows += [jnp.pad(grad_squeezed, ((0, 0), (0, 960))), jnp.zeros((4, 1024), F32)]
    r.gate_rows[...] = jnp.concatenate(rows, axis=0)
    flush("gate_rows").start()
    expand_sum.end()
    flush("sum_expand").start()
    project_sum.end()
    flush("sum_project").start()
    for name in OUTS:
        flush(name).wait()
    links.finish()


FINAL = dict(
    block_out=((MAP_ROWS, MAP_COLS, CH), BF16),
    grad_image=((MAP_ROWS, MAP_COLS, CH), BF16),
    grad_norm0=((1, CH), F32),
    grad_expand=((CH, 1024), F32),
    grad_depth=((3, 3, 1024), F32),
    grad_squeeze=((64, 1024), F32),
    grad_excite=((64, 1024), F32),
    grad_project=((1024, CH), F32),
    grad_norm1=((1, CH), F32),
    grad_qkv=((CH, 3 * CH), F32),
    grad_out_proj=((CH, CH), F32),
    grad_bias=((HEADS, MEMBERS, MEMBERS), F32),
)


def finish_kernel(*args):
    r = Refs()
    for name, ref in zip(list(OUTS) + list(FINAL) + ["sems"], args, strict=True):
        setattr(r, name, ref)
    copies = [
        pltpu.make_async_copy(r.out_map, r.block_out, r.sems.at[0]),
        pltpu.make_async_copy(r.grad_map, r.grad_image, r.sems.at[1]),
    ]
    for copy in copies:
        copy.start()
    r.grad_expand[...] = r.sum_expand[...].astype(F32)
    r.grad_project[...] = r.sum_project[...].astype(F32)
    r.grad_qkv[...] = r.sum_pair[:, : 3 * CH].astype(F32)
    r.grad_out_proj[...] = r.sum_pair[:, 3 * CH :].astype(F32)
    for h in range(0, HEADS, 2):
        both = r.sum_bias[:, h * 64 : (h + 2) * 64].T
        r.grad_bias[h] = both[:64]
        r.grad_bias[h + 1] = both[64:]
    for k in range(9):
        if k < 8:
            rows = [r.sum_small[c * 8 + k : c * 8 + k + 1, :128] for c in range(LANES)]
        else:
            rows = [r.sum_small[c * 8 : c * 8 + 1, 128:] for c in range(LANES)]
        r.grad_depth[k // 3, k % 3 : k % 3 + 1, :] = jnp.concatenate(rows, axis=1)
    for n, out in enumerate((r.grad_norm0, r.grad_norm1)):
        rows = [r.sum_small[c * 8 + 1 + n : c * 8 + 2 + n, 128:] for c in range(2)]
        out[...] = jnp.concatenate(rows, axis=1)
    pooled, grad_logit = r.gate_rows[0:1, :], r.gate_rows[1:2, :]
    hidden, grad_squeezed = r.gate_rows[2:3, :64], r.gate_rows[3:4, :64]
    r.grad_excite[...] = outer(hidden, grad_logit)
    r.grad_squeeze[...] = outer(grad_squeezed, pooled)
    for copy in copies:
        copy.wait()


def on_device(
    image,
    out_cotangent,
    norm0_gain,
    w_expand,
    w_depth,
    w_squeeze,
    w_excite,
    w_project,
    norm1_gain,
    w_qkv,
    w_out,
    attn_bias,
):
    vmem = pl.BlockSpec(memory_space=pltpu.VMEM)
    any_space = pl.BlockSpec(memory_space=pl.ANY)
    buffers = lambda shapes: [pltpu.VMEM(*shape) for shape in shapes.values()]
    made = pl.pallas_call(
        block_kernel,
        out_shape=[jax.ShapeDtypeStruct(*shape) for shape in OUTS.values()],
        in_specs=[vmem] * len(IN_NAMES) + [any_space] * len(LATE),
        out_specs=[any_space] * len(OUTS),
        scratch_shapes=buffers(LATE)
        + buffers(OUTS)
        + buffers(SCRATCH)
        + [pltpu.SemaphoreType.DMA((n,)) for n in (SEMS, len(LATE), len(OUTS))],
        compiler_params=pltpu.CompilerParams(
            collective_id=0, has_side_effects=True, vmem_limit_bytes=63 * 2**20
        ),
        name="block",
    )(
        image,
        norm0_gain,
        norm1_gain,
        w_depth,
        w_expand,
        out_cotangent.reshape(MEMBERS, GROUPS, CH),
        w_out,
        attn_bias,
        w_squeeze.T,
        w_excite,
        w_project,
        w_qkv,
    )
    final = pl.pallas_call(
        finish_kernel,
        out_shape=[jax.ShapeDtypeStruct(*shape) for shape in FINAL.values()],
        in_specs=[any_space] * 2 + [vmem] * (len(OUTS) - 2),
        out_specs=[any_space] * 2 + [vmem] * (len(FINAL) - 2),
        scratch_shapes=[pltpu.SemaphoreType.DMA((2,))],
        compiler_params=pltpu.CompilerParams(vmem_limit_bytes=63 * 2**20),
        name="finish",
    )(*made)
    final = dict(zip(FINAL, final))
    final["grad_norm0"] = final["grad_norm0"].reshape(CH)
    final["grad_norm1"] = final["grad_norm1"].reshape(CH)
    final["grad_squeeze"] = final["grad_squeeze"].T
    return tuple(final.values())


def solution(mesh):
    mapped = P("row", "col", None)
    return jax.shard_map(
        on_device,
        mesh=mesh,
        in_specs=(mapped, mapped) + (P(),) * 10,
        out_specs=(mapped, mapped) + (P(),) * 10,
        check_vma=False,
    )
```

```python
import functools

import jax
import jax.numpy as jnp
from jax import lax
from jax.experimental import pallas as pl
from jax.experimental.pallas import tpu as pltpu
from jax.sharding import PartitionSpec as P

F32 = jnp.float32
BF16 = jnp.bfloat16
MESH = pl.DeviceIdType.MESH
ROWS = 8
COLS = 16
CHIPS = 64
HEADS = 8
MEMBERS = 64
GROUPS = 16
CH = 256
MAP_ROWS = 16
MAP_COLS = 64
CELLS = MAP_ROWS * MAP_COLS
CELLS_TOTAL = 131072
LANES = 8
PAD = 80
PADDED = (MAP_ROWS + 2) * PAD
TILE = 256
SCALE = 32 ** (-0.5)
GELU_A = 0.7978845608028654
GELU_B = 0.044715


def nn(a, b):
    return jnp.dot(a, b, preferred_element_type=F32)


def nt(a, b):
    return lax.dot_general(a, b, (((1,), (1,)), ((), ())), preferred_element_type=F32)


def tn(a, b):
    return lax.dot_general(a, b, (((0,), (0,)), ((), ())), preferred_element_type=F32)


def gelu(x):
    return 0.5 * x * (1.0 + jnp.tanh(GELU_A * (x + GELU_B * (x * x * x))))


def gelu_slope(x):
    square = x * x
    t = jnp.tanh(GELU_A * (x + GELU_B * (square * x)))
    return 0.5 * (1.0 + t) + (0.5 * GELU_A) * x * (1.0 - t * t) * (1.0 + (3 * GELU_B) * square)


def centre(x):
    centered = x - jnp.mean(x, axis=-1, keepdims=True)
    rstd = lax.rsqrt(jnp.mean(centered * centered, axis=-1, keepdims=True) + 1e-05)
    return centered * rstd, rstd


def norm_back(unit, rstd, grad_unit):
    first = jnp.mean(grad_unit, axis=-1, keepdims=True)
    second = jnp.mean(grad_unit * unit, axis=-1, keepdims=True)
    return rstd * (grad_unit - first - unit * second)


def fold(x):
    return jnp.sum(x.reshape(x.shape[0] // 8, 8, x.shape[1]), axis=0)


def thirds(x):
    one = x.astype(BF16).astype(F32)
    two = (x - one).astype(BF16).astype(F32)
    three = (x - one - two).astype(BF16).astype(F32)
    return one, two, three


def stack_rows(rows):
    width = rows[0].shape[1]
    rows = list(rows) + [jnp.zeros((8 - len(rows), width), F32)]
    return jnp.concatenate(rows, axis=0).astype(BF16)


def wide_product(x, w, product):
    return jnp.sum(product(stack_rows(thirds(x)), w), axis=0, keepdims=True)


def outer(a, b):
    a1, a2, a3 = thirds(a)
    b1, b2, b3 = thirds(b)
    return tn(stack_rows([a1, a1, a2, a2, a1, a3]), stack_rows([b1, b2, b1, b2, b3, b1]))


def aligned(start, size, unit=8):
    return pl.ds(pl.multiple_of(start, unit), size)


class Place:
    def __init__(self):
        self.row = lax.axis_index("row")
        self.col = lax.axis_index("col")
        self.core = lax.rem(self.col, 2)
        self.q = lax.div(self.col, 2)
        self.chip = self.row * 8 + self.q
        self.qs = [lax.rem(self.q + k, 8) for k in range(8)]
        self.cols = [q * 2 + self.core for q in self.qs]

    def partner(self):
        return (self.row, self.q * 2 + 1 - self.core)

    def q_peer(self, k):
        return self.qs[k], (self.row, self.cols[k])

    def row_peer(self, k):
        row = lax.rem(self.row + k, ROWS)
        return row, (row, self.col)

    def beside(self, up, right):
        return (lax.rem(self.row + ROWS + up, ROWS), lax.rem(self.col + COLS + right, COLS))

    def every_peer(self, body):
        def others(k, carry):
            row = lax.rem(self.row + k, ROWS)
            for n in range(1, 8):
                body(row, self.qs[n], (row, self.cols[n]))
            return carry

        def same(k, carry):
            row = lax.rem(self.row + k, ROWS)
            body(row, self.q, (row, self.col))
            return carry

        lax.fori_loop(0, ROWS, others, 0)
        lax.fori_loop(1, ROWS, same, 0)


class Links:
    def __init__(self, sems):
        self.sems = sems
        self.used = 0
        self.sent = []

    def pair(self):
        at = self.used
        self.used += 2
        return self.sems.at[at], self.sems.at[at + 1]

    def finish(self):
        for sem, buf in self.sent:
            pltpu.make_async_copy(buf, buf, sem).wait()


def push(src, dst, send, recv, device):
    pltpu.make_async_remote_copy(
        src_ref=src,
        dst_ref=dst,
        send_sem=send,
        recv_sem=recv,
        device_id=device,
        device_id_type=MESH,
    ).start()


def arrived(buf, sem):
    pltpu.make_async_copy(buf, buf, sem).wait()


class TileSum:
    def __init__(self, me, links, x, pair_slot, slots):
        self.me, self.links = me, links
        self.x, self.pair_slot, self.slots = x, pair_slot, slots
        self.s0, self.s1 = links.pair(), links.pair()

    def start(self):
        push(self.x, self.pair_slot, *self.s0, self.me.partner())
        self.links.sent.append((self.s0[0], self.x))
        arrived(self.pair_slot, self.s0[1])
        self.slots[self.me.chip] = self.x[...] + self.pair_slot[...]
        mine = self.slots.at[self.me.chip]
        self.me.every_peer(lambda row, q, device: push(mine, mine, *self.s1, device))
        self.links.sent.append((self.s1[0], self.slots.at[pl.ds(0, CHIPS - 1)]))

    def end(self):
        arrived(self.slots.at[pl.ds(0, CHIPS - 1)], self.s1[1])
        return jnp.sum(self.slots[...], axis=0)


class Scatter:
    def __init__(self, me, links, x, pair_in, summed, slots):
        self.me, self.links = me, links
        self.x, self.pair_in, self.summed, self.slots = x, pair_in, summed, slots
        self.sems = [links.pair() for _ in range(2)]

    def half_of(self, core):
        return self.x.at[aligned(core * 128, 128, 128)]

    def piece(self, row, q):
        return self.summed.at[aligned(row * 16, 16, 16), aligned(q * 128, 128, 128)]

    def start(self):
        push(self.half_of(1 - self.me.core), self.pair_in, *self.sems[0], self.me.partner())
        self.links.sent.append((self.sems[0][0], self.pair_in))

    def scatter(self):
        me = self.me
        arrived(self.pair_in, self.sems[0][1])
        mine = self.half_of(me.core)
        self.summed[...] = (mine[...].astype(F32) + self.pair_in[...].astype(F32)).astype(BF16)
        to = self.slots.at[me.chip]
        me.every_peer(
            lambda row, q, device: push(self.piece(row, q), to, *self.sems[1], device)
        )
        self.slots[me.chip] = self.piece(me.row, me.q)[...]

    def end(self):
        arrived(self.slots.at[pl.ds(0, CHIPS - 1)], self.sems[1][1])
        self.links.sent.append((self.sems[1][0], self.slots.at[pl.ds(0, CHIPS - 1)]))


class Gather:
    def __init__(self, me, links, out, like):
        self.me, self.links, self.out, self.like = me, links, out, like
        self.width = out.shape[1] // 8
        self.sems = [links.pair() for _ in range(2)]
        lane = aligned(me.q * self.width, self.width, 128)
        self.piece = out.at[aligned(me.core * 128 + me.row * 16, 16, 16), lane]

    def send(self, row, k):
        push(self.piece, self.piece, *self.sems[0], (row, self.me.cols[k]))

    def send_all(self):
        self.me.every_peer(
            lambda row, q, device: push(self.piece, self.piece, *self.sems[0], device)
        )

    def back_pair(self):
        me = self.me
        arrived(self.like.at[pl.ds(0, CHIPS - 1)], self.sems[0][1])
        self.links.sent.append((self.sems[0][0], self.like.at[pl.ds(0, CHIPS - 1)]))
        half = self.out.at[aligned(me.core * 128, 128, 128)]
        push(half, half, *self.sems[1], me.partner())
        self.links.sent.append((self.sems[1][0], half))

    def end(self):
        arrived(self.out.at[pl.ds(0, 128)], self.sems[1][1])


class SmallSum:
    def __init__(self, me, links, x, pair_in, summed, slots_a, slots_b, out):
        self.me, self.links = me, links
        self.x, self.pair_in, self.summed, self.out = x, pair_in, summed, out
        self.slots_a, self.slots_b = slots_a, slots_b
        self.sems = [links.pair() for _ in range(4)]

    def start(self):
        push(self.x, self.pair_in, *self.sems[0], self.me.partner())
        self.links.sent.append((self.sems[0][0], self.pair_in))

    def to_q(self):
        arrived(self.pair_in, self.sems[0][1])
        self.summed[...] = self.x[...] + self.pair_in[...]
        for k in range(1, 8):
            q, device = self.me.q_peer(k)
            piece = self.summed.at[aligned(q * 8, 8)]
            push(piece, self.slots_a.at[self.me.q], *self.sems[1], device)
        self.links.sent.append((self.sems[1][0], self.slots_a.at[pl.ds(0, 7)]))

    def to_rows(self):
        me = self.me
        self.slots_a[me.q] = self.summed[aligned(me.q * 8, 8)]
        arrived(self.slots_a.at[pl.ds(0, 7)], self.sems[1][1])
        self.slots_b[me.row] = jnp.sum(self.slots_a[...], axis=0)
        for k in range(1, 8):
            _, device = me.row_peer(k)
            piece = self.slots_b.at[me.row]
            push(piece, piece, *self.sems[2], device)
        self.links.sent.append((self.sems[2][0], self.slots_b.at[pl.ds(0, 7)]))

    def back_q(self):
        me = self.me
        arrived(self.slots_b.at[pl.ds(0, 7)], self.sems[2][1])
        piece = self.out.at[aligned(me.q * 8, 8)]
        piece[...] = jnp.sum(self.slots_b[...], axis=0)
        for k in range(1, 8):
            _, device = me.q_peer(k)
            push(piece, piece, *self.sems[3], device)
        self.links.sent.append((self.sems[3][0], self.slots_a.at[pl.ds(0, 7)]))

    def end(self):
        arrived(self.slots_a.at[pl.ds(0, 7)], self.sems[3][1])


class Exchange:
    def __init__(self, me, links, src, dst):
        self.me, self.links, self.src, self.dst = me, links, src, dst
        self.sems = links.pair()

    def send(self, row, k):
        q, col = self.me.qs[k], self.me.cols[k]
        push(self.src.at[row * 8 + q], self.dst.at[self.me.chip], *self.sems, (row, col))

    def send_row(self, row):
        for k in range(1, 8):
            self.send(row, k)

        @pl.when(row != self.me.row)
        def _():
            self.send(row, 0)

    def send_tile(self, t):
        for k in range(2):
            self.send_row(t * 2 + lax.rem(self.me.row + k, 2))

    def end(self):
        self.dst[self.me.chip] = self.src[self.me.chip]
        arrived(self.dst.at[pl.ds(0, CHIPS - 1)], self.sems[1])
        self.links.sent.append((self.sems[0], self.dst.at[pl.ds(0, CHIPS - 1)]))


class Halo:
    def __init__(
        self, me, links, rows_out, cols_out, corners_out, rows_in, cols_in, corners_in
    ):
        self.me, self.links = me, links
        self.rows_out, self.cols_out, self.corners_out = rows_out, cols_out, corners_out
        self.rows_in, self.cols_in, self.corners_in = rows_in, cols_in, corners_in
        self.sems = [links.pair() for _ in range(3)]

    def start(self):
        me = self.me
        for side, up in ((0, -1), (1, 1)):
            push(
                self.rows_out[side],
                self.rows_in.at[1 - side],
                *self.sems[0],
                me.beside(up, 0),
            )
        for side, right in ((0, -1), (1, 1)):
            strip = self.cols_out.at[side]
            push(strip, self.cols_in.at[1 - side], *self.sems[1], me.beside(0, right))
            for end, up in ((0, -1), (1, 1)):
                push(
                    self.corners_out[end * 2 + side],
                    self.corners_in.at[(1 - end) * 2 + 1 - side],
                    *self.sems[2],
                    me.beside(up, right),
                )

    def end(self):
        for n, buf in enumerate((self.rows_in, self.cols_in, self.corners_in)):
            arrived(buf, self.sems[n][1])
            self.links.sent.append((self.sems[n][0], buf))


IN_NAMES = ["image", "norm0_gain", "norm1_gain", "w_depth", "w_expand"]
LATE = dict(
    dy=((MEMBERS, GROUPS, CH), BF16),
    w_out=((CH, CH), BF16),
    bias=((HEADS, MEMBERS, MEMBERS), F32),
    w_squeeze_t=((64, 1024), BF16),
    w_excite=((64, 1024), BF16),
    w_project=((1024, CH), BF16),
    w_qkv=((CH, 768), BF16),
)
OUTS = dict(
    out_map=((MAP_ROWS, MAP_COLS, CH), BF16),
    grad_map=((MAP_ROWS, MAP_COLS, CH), BF16),
    sum_expand=((CH, 1024), BF16),
    sum_early=((CH, 2048), BF16),
    sum_bias=((MEMBERS, 512), F32),
    sum_taps=((64, 256), F32),
    sum_norms=((8, 128), F32),
    gate_rows=((8, 1024), F32),
)


def big_scratch(name):
    return {
        name + "_x": ((CH, 1024), BF16),
        name + "_pair": ((CH // 2, 1024), BF16),
        name + "_summed": ((CH // 2, 1024), BF16),
    }


def small_scratch(name, width):
    return {
        name + "_x": ((64, width), F32),
        name + "_pair": ((64, width), F32),
        name + "_summed": ((64, width), F32),
        name + "_a": ((8, 8, width), F32),
        name + "_b": ((8, 8, width), F32),
    }


def tile_scratch(name):
    return {
        name + "_x": ((8, 128), F32),
        name + "_pair": ((8, 128), F32),
        name + "_slots": ((CHIPS, 8, 128), F32),
    }


SCRATCH = dict(
    taps=((16, 1024), F32),
    normed=((CELLS, CH), BF16),
    normed_t=((CH, CELLS), BF16),
    spread=((LANES, PADDED, 128), F32),
    expanded=((LANES, CELLS, 128), F32),
    depth=((LANES, CELLS, 128), F32),
    act=((LANES, CELLS, 128), BF16),
    pool_acc=((LANES, 8, 128), F32),
    edge_cols=((2, 16, CH), BF16),
    edge_rows_in=((2, MAP_COLS, CH), BF16),
    edge_cols_in=((2, 16, CH), BF16),
    edge_corners_in=((4, 16, CH), BF16),
    gate=((1, 1024), F32),
    gate_back=((1, 1024), F32),
    mixed=((CELLS, CH), BF16),
    normed_two=((MEMBERS, GROUPS, CH), BF16),
    grid_x=((MEMBERS, GROUPS, CH), BF16),
    grid_dy=((MEMBERS, GROUPS, CH), BF16),
    qkv=((6, CELLS, 128), F32),
    grid_g=((2, CELLS, 128), F32),
    att_rows=((2, CELLS, 128), F32),
    packed_back=((6, CELLS, 128), F32),
    probs=((GROUPS, MEMBERS, 512), F32),
    bias_t=((MEMBERS, 512), F32),
    att_out=((MEMBERS, GROUPS, CH), BF16),
    att_in=((MEMBERS, GROUPS, CH), BF16),
    gn_out=((MEMBERS, GROUPS, CH), BF16),
    gn_in=((MEMBERS, GROUPS, CH), BF16),
    grad_mixed=((CELLS, CH), F32),
    grad_mixed_b=((CELLS, CH), BF16),
    grad_gated=((LANES, CELLS, 128), F32),
    gate_acc=((LANES, 8, 128), F32),
    grad_pre=((LANES, PADDED, 128), F32),
    pre_rows=((2, LANES, MAP_COLS, 128), BF16),
    pre_cols=((2, LANES, 16, 128), BF16),
    pre_rows_in=((2, LANES, MAP_COLS, 128), BF16),
    pre_cols_in=((2, LANES, 16, 128), BF16),
    pre_corners=((4, 16, 128), BF16),
    pre_corners_in=((4, 16, 128), BF16),
    tap_acc=((LANES, 9, 8, 128), F32),
    grad_exp=((LANES, CELLS, 128), BF16),
    norm_acc=((2, 8, CH), F32),
    pair_acc=((CH, 1024), F32),
    **tile_scratch("pool"),
    **tile_scratch("gateg"),
    **big_scratch("expand"),
    **big_scratch("project"),
    **big_scratch("pair"),
    expand_slots=((CHIPS, 16, 128), BF16),
    pair_slots=((CHIPS, 16, 128), BF16),
    project_slots=((CHIPS, 16, 128), BF16),
    **small_scratch("bias", 512),
    **small_scratch("taps_sum", 256),
    **tile_scratch("norms"),
)
SEMS = 96


class Refs:
    pass


def lanes_of(ref, first, at):
    return jnp.concatenate([ref[first, at, :], ref[first + 1, at, :]], axis=1)


def map_rows(t, count=4):
    return pl.ds(t * count, count)


def cell_rows(t):
    return aligned(t * TILE, TILE, TILE)


def pad_row(row, col=0):
    return pl.multiple_of(row * PAD + col, 8)


def block_kernel(*args):
    r = Refs()
    names = IN_NAMES + ["hbm_" + n for n in LATE] + ["hbm_" + n for n in OUTS]
    names += list(LATE) + list(OUTS) + list(SCRATCH) + ["sems", "late_sems", "out_sems"]
    for name, ref in zip(names, args, strict=True):
        setattr(r, name, ref)
    me = Place()
    links = Links(r.sems)

    def late(name):
        at = list(LATE).index(name)
        return pltpu.make_async_copy(
            getattr(r, "hbm_" + name), getattr(r, name), r.late_sems.at[at]
        )

    def flush(name):
        at = list(OUTS).index(name)
        return pltpu.make_async_copy(
            getattr(r, name), getattr(r, "hbm_" + name), r.out_sems.at[at]
        )

    for name in LATE:
        late(name).start()
    gain_first = r.norm0_gain[...].astype(F32).reshape(1, CH)
    gain_second = r.norm1_gain[...].astype(F32).reshape(1, CH)
    for a in range(3):
        r.taps[a * 3 : a * 3 + 3, :] = r.w_depth[a].astype(F32)
    off = r.image.shape[0] - 1

    barrier = pltpu.get_barrier_semaphore()

    def greet(row, q, device):
        pl.semaphore_signal(barrier, inc=1, device_id=device, device_id_type=MESH)

    me.every_peer(greet)
    for up in (-1, 0, 1):
        for right in (-1, 1):
            pl.semaphore_signal(
                barrier, inc=1, device_id=me.beside(up, right), device_id_type=MESH
            )

    for side, col in ((0, 0), (1, MAP_COLS - 16)):
        rows = []
        for i in range(MAP_ROWS):
            part = r.image[i, col : col + 16, :].astype(F32)
            rows.append(part[0:1] if side == 0 else part[15:16])
        r.edge_cols[side] = jnp.concatenate(rows, axis=0).astype(BF16)

    @pl.loop(0, 4)
    def _(t):
        x = r.image[map_rows(t)].reshape(TILE, CH).astype(F32)
        unit, _ = centre(x)
        r.normed[cell_rows(t)] = (unit * gain_first).astype(BF16)

    @pl.loop(0, 4)
    def _(t):
        @pl.loop(0, 4)
        def _(c):
            e = nn(r.normed[cell_rows(t)], r.w_expand[:, aligned(c * 256, 256, 256)])
            s = gelu(e).astype(BF16).astype(F32)
            for h in range(2):
                lane = slice(h * 128, (h + 1) * 128)
                r.expanded[2 * c + h, cell_rows(t), :] = e[:, lane]
                for a in range(4):
                    at = pl.ds(pad_row(1 + t * 4 + a, 8), MAP_COLS)
                    r.spread[2 * c + h, at, :] = s[a * 64 : (a + 1) * 64, lane]

    pl.semaphore_wait(barrier, CHIPS + 5)
    halo = Halo(
        me,
        links,
        (r.image.at[0], r.image.at[off]),
        r.edge_cols,
        [r.edge_cols.at[side] for side in (0, 1, 0, 1)],
        r.edge_rows_in,
        r.edge_cols_in,
        r.edge_corners_in,
    )
    halo.start()
    late("dy").wait()
    dy_out = Exchange(me, links, r.dy, r.grid_dy)

    @pl.loop(0, LANES)
    def _(c):
        row = lax.rem(me.row + c, ROWS)
        for t in range(4):
            for k in (2 * t + 1, 2 * t):
                if k:
                    dy_out.send(row, k)
            at = pl.ds(t * TILE, TILE)
            r.expanded[c, at, :] = gelu_slope(r.expanded[c, at, :])

        @pl.when(c > 0)
        def _():
            dy_out.send(row, 0)

    halo.end()

    up_ok = (me.row > 0).astype(F32)
    down_ok = (me.row < ROWS - 1).astype(F32)
    left_ok = (me.col > 0).astype(F32)
    right_ok = (me.col < COLS - 1).astype(F32)
    around = jnp.concatenate(
        [
            r.edge_rows_in[0].astype(F32) * up_ok,
            r.edge_rows_in[1].astype(F32) * down_ok,
            r.edge_cols_in[0].astype(F32) * left_ok,
            r.edge_cols_in[1].astype(F32) * right_ok,
            r.edge_corners_in[0].astype(F32)[8:16] * (up_ok * left_ok),
            r.edge_corners_in[1].astype(F32)[8:16] * (up_ok * right_ok),
            r.edge_corners_in[2].astype(F32)[0:8] * (down_ok * left_ok),
            r.edge_corners_in[3].astype(F32)[0:8] * (down_ok * right_ok),
        ],
        axis=0,
    )
    unit, _ = centre(around)
    around_normed = (unit * gain_first).astype(BF16)
    last = (MAP_ROWS + 1) * PAD
    for c in range(4):
        s = gelu(nn(around_normed, r.w_expand[:, c * 256 : (c + 1) * 256]))
        s = s.astype(BF16).astype(F32)
        for h in range(2):
            v = s[:, h * 128 : (h + 1) * 128]
            n = 2 * c + h
            r.spread[n, 8:72, :] = v[0:64]
            r.spread[n, last + 8 : last + 72, :] = v[64:128]
            r.spread[n, pl.ds(PAD + 7, MAP_ROWS, stride=PAD), :] = v[128:144]
            r.spread[n, pl.ds(PAD + 72, MAP_ROWS, stride=PAD), :] = v[144:160]
            r.spread[n, 7:8, :] = v[167:168]
            r.spread[n, 72:73, :] = v[175:176]
            r.spread[n, last + 7 : last + 8, :] = v[176:177]
            r.spread[n, last + 72 : last + 73, :] = v[184:185]

    def taps_of(c):
        lane = aligned(c * 128, 128, 128)
        return [r.taps[k : k + 1, lane] for k in range(9)]

    @pl.loop(0, LANES)
    def _(c):
        taps = taps_of(c)

        def block(n, total):
            sums = [None] * 4
            for row in range(6):
                view = r.spread.at[c, pl.ds(pad_row(n * 4 + row), PAD)]
                for b in range(3):
                    v = view[pl.ds(7 + b, MAP_COLS), :]
                    for a in range(3):
                        i = row - a
                        if 0 <= i < 4:
                            term = v * taps[a * 3 + b]
                            sums[i] = term if sums[i] is None else sums[i] + term
            for i in range(4):
                at = aligned((n * 4 + i) * MAP_COLS, MAP_COLS, MAP_COLS)
                r.depth[c, at, :] = sums[i]
                value = gelu(sums[i])
                r.act[c, at, :] = value.astype(BF16)
                total = total + fold(value)
            return total

        total = lax.fori_loop(0, 4, block, jnp.zeros((8, 128), F32))
        r.pool_x[pl.ds(c, 1), :] = jnp.sum(total, axis=0, keepdims=True)

    pool = TileSum(me, links, r.pool_x, r.pool_pair, r.pool_slots)
    pool.start()

    @pl.loop(0, LANES * 4)
    def _(n):
        c, t = lax.div(n, 4), lax.rem(n, 4)
        r.depth[c, cell_rows(t), :] = gelu_slope(r.depth[c, cell_rows(t), :])

    dy_out.end()
    late("w_out").wait()
    late("bias").wait()

    @pl.loop(0, 4)
    def _(t):
        dy = r.grid_dy[map_rows(t, 16)].reshape(TILE, CH)
        g = nt(dy, r.w_out[...])
        for n in range(2):
            r.grid_g[n, cell_rows(t), :] = g[:, n * 128 : (n + 1) * 128]

    for h in range(0, HEADS, 2):
        both = jnp.concatenate([r.bias[h], r.bias[h + 1]], axis=0)
        r.bias_t[:, h * 64 : (h + 2) * 64] = both.T
    for t in range(4):
        r.normed_t[:, t * TILE : (t + 1) * TILE] = r.normed[t * TILE : (t + 1) * TILE].T

    def flat(tile):
        return jnp.concatenate([tile[n : n + 1] for n in range(8)], axis=1)

    pooled = flat(pool.end()) * (1.0 / CELLS_TOTAL)
    for name in ("w_squeeze_t", "w_excite", "w_project", "w_qkv"):
        late(name).wait()
    squeezed = wide_product(pooled, r.w_squeeze_t[...], nt)
    open_part = jax.nn.sigmoid(squeezed)
    hidden = squeezed * open_part
    gate = jax.nn.sigmoid(wide_product(hidden, r.w_excite[...], nn))
    r.gate[...] = gate

    grid_out = Exchange(me, links, r.normed_two, r.grid_x)
    start_tile = lax.div(me.row, 2)

    @pl.loop(0, 4)
    def _(step):
        t = lax.rem(start_tile + step, 4)
        total = r.image[map_rows(t)].reshape(TILE, CH).astype(F32)
        for c in range(4):
            lane = slice(c * 256, (c + 1) * 256)
            gated = lanes_of(r.act, 2 * c, cell_rows(t)).astype(F32) * r.gate[:, lane]
            total = total + nn(gated.astype(BF16), r.w_project[lane, :])
        mixed = total.astype(BF16)
        r.mixed[cell_rows(t)] = mixed
        unit, _ = centre(mixed.astype(F32))
        normed = (unit * gain_second).astype(BF16)
        r.normed_two[map_rows(t, 16)] = normed.reshape(16, GROUPS, CH)
        grid_out.send_tile(t)

    grid_out.end()

    @pl.loop(0, 4)
    def _(t):
        x = r.grid_x[map_rows(t, 16)].reshape(TILE, CH)
        qkv = nn(x, r.w_qkv[...])
        for n in range(6):
            r.qkv[n, cell_rows(t), :] = qkv[:, n * 128 : (n + 1) * 128]

    head_of = lax.div(lax.broadcasted_iota(jnp.int32, (1, 128), 1), 32)
    masks_f = [(head_of == h).astype(F32) for h in range(4)]
    masks = [m.astype(BF16) for m in masks_f]
    unroll = 4

    def spread_heads(a):
        return jnp.concatenate([a * m for m in masks], axis=0)

    def own_heads(v):
        total = v[0:MEMBERS] * masks_f[0]
        for h in range(1, 4):
            total = total + v[h * MEMBERS : (h + 1) * MEMBERS] * masks_f[h]
        return total

    def put(ref, n, at, value):
        ref[n, at, :] = value.astype(BF16).astype(F32)

    def group_forward(group):
        at = pl.ds(group, MEMBERS, stride=GROUPS)
        for n in range(2):
            q, k, v = [r.qkv[part * 2 + n, at, :].astype(BF16) for part in range(3)]
            lanes = slice(n * 256, (n + 1) * 256)
            scores = nt(k, spread_heads(q)) * SCALE + r.bias_t[:, lanes]
            lifted = jnp.exp(scores - jnp.max(scores, axis=0, keepdims=True))
            probs = lifted * (1.0 / jnp.sum(lifted, axis=0, keepdims=True))
            r.probs[group, :, lanes] = probs
            put(r.att_rows, n, at, own_heads(tn(probs.astype(BF16), v)))

    def group_back(group):
        at = pl.ds(group, MEMBERS, stride=GROUPS)
        bias_parts = []
        for n in range(2):
            q, k, v = [r.qkv[part * 2 + n, at, :].astype(BF16) for part in range(3)]
            lanes = slice(n * 256, (n + 1) * 256)
            q_heads = spread_heads(q)
            g_heads = spread_heads(r.grid_g[n, at, :].astype(BF16))
            probs = r.probs[group, :, lanes]
            put(r.packed_back, 4 + n, at, nn(probs.astype(BF16), g_heads))
            grad_probs = nt(v, g_heads)
            grad_scores = probs * (
                grad_probs - jnp.sum(grad_probs * probs, axis=0, keepdims=True)
            )
            bias_parts.append(grad_scores)
            scaled = (grad_scores * SCALE).astype(BF16)
            put(r.packed_back, n, at, own_heads(tn(scaled, k)))
            put(r.packed_back, 2 + n, at, nn(scaled, q_heads))
        return bias_parts

    @pl.loop(0, GROUPS // unroll)
    def _(step):
        for n in range(unroll):
            group_forward(step * unroll + n)

    @pl.loop(0, 4)
    def _(t):
        att = lanes_of(r.att_rows, 0, cell_rows(t)).astype(BF16)
        r.att_out[map_rows(t, 16)] = att.reshape(16, GROUPS, CH)

    att_back = Exchange(me, links, r.att_out, r.att_in)
    r.bias_x[...] = jnp.zeros_like(r.bias_x)

    @pl.loop(0, GROUPS // unroll)
    def _(step):
        for n in range(2):
            att_back.send_row(lax.rem(me.row + step * 2 + n, ROWS))
        total = group_back(step * unroll)
        for n in range(1, unroll):
            total = [a + b for a, b in zip(total, group_back(step * unroll + n))]
        for n in range(2):
            r.bias_x[:, n * 256 : (n + 1) * 256] += total[n]

    def packed_tile(t):
        parts = [r.packed_back[n, cell_rows(t), :] for n in range(6)]
        return jnp.concatenate(parts, axis=1).astype(BF16)

    gn_back = Exchange(me, links, r.gn_out, r.gn_in)

    @pl.loop(0, 4)
    def _(step):
        t = lax.rem(start_tile + step, 4)
        gn = nt(packed_tile(t), r.w_qkv[...]).astype(BF16)
        r.gn_out[map_rows(t, 16)] = gn.reshape(16, GROUPS, CH)
        gn_back.send_tile(t)

    bias_sum = SmallSum(
        me, links, r.bias_x, r.bias_pair, r.bias_summed, r.bias_a, r.bias_b, r.sum_bias
    )
    bias_sum.start()
    r.pair_acc[...] = jnp.zeros_like(r.pair_acc)

    @pl.loop(0, 4)
    def _(t):
        x = r.grid_x[map_rows(t, 16)].reshape(TILE, CH)
        dy = r.grid_dy[map_rows(t, 16)].reshape(TILE, CH)
        att = r.att_out[map_rows(t, 16)].reshape(TILE, CH)
        r.pair_acc[:, : 3 * CH] += tn(x, packed_tile(t))
        r.pair_acc[:, 3 * CH :] += tn(att, dy)

    r.pair_x[...] = r.pair_acc[...].astype(BF16)

    def big(name):
        parts = ["x", "pair", "summed", "slots"]
        return Scatter(me, links, *[getattr(r, name + "_" + p) for p in parts])

    pair_sum = big("pair")
    pair_sum.start()
    bias_sum.to_q()
    pair_sum.scatter()
    gn_back.end()

    r.norm_acc[...] = jnp.zeros_like(r.norm_acc)
    r.gate_acc[...] = jnp.zeros_like(r.gate_acc)

    @pl.loop(0, 4)
    def _(t):
        unit, rstd = centre(r.mixed[cell_rows(t)].astype(F32))
        gn = r.gn_in[map_rows(t, 16)].reshape(TILE, CH).astype(F32)
        r.norm_acc[1] += fold(gn * unit)
        dy = r.dy[map_rows(t, 16)].reshape(TILE, CH).astype(F32)
        grad = dy + norm_back(unit, rstd, gn * gain_second)
        r.grad_mixed[cell_rows(t)] = grad
        grad_b = grad.astype(BF16)
        r.grad_mixed_b[cell_rows(t)] = grad_b
        for c in range(4):
            gg = nt(grad_b, r.w_project[c * 256 : (c + 1) * 256, :])
            for h in range(2):
                n = 2 * c + h
                part = gg[:, h * 128 : (h + 1) * 128]
                r.grad_gated[n, cell_rows(t), :] = part
                r.gate_acc[n] += fold(part * r.act[n, cell_rows(t), :].astype(F32))

    for n in range(LANES):
        r.gateg_x[n : n + 1, :] = jnp.sum(r.gate_acc[n], axis=0, keepdims=True)
    gate_sum = TileSum(me, links, r.gateg_x, r.gateg_pair, r.gateg_slots)
    gate_sum.start()

    grad_t = r.grad_mixed_b[...].T
    for c in range(4):
        lane = slice(c * 256, (c + 1) * 256)
        product = nn(grad_t, lanes_of(r.act, 2 * c, slice(None))) * r.gate[:, lane]
        r.project_x[:, lane] = product.astype(BF16)
    project_sum = big("project")
    project_sum.start()
    bias_sum.to_rows()
    project_sum.scatter()
    grad_gate = flat(gate_sum.end())
    grad_logit = grad_gate * gate * (1.0 - gate)
    grad_hidden = wide_product(grad_logit, r.w_excite[...], nt)
    grad_squeezed = grad_hidden * (open_part * (1.0 + squeezed * (1.0 - open_part)))
    r.gate_back[...] = wide_product(grad_squeezed, r.w_squeeze_t[...], nn) * (1.0 / CELLS_TOTAL)

    @pl.loop(0, LANES)
    def _(c):
        lane = aligned(c * 128, 128, 128)
        scale, shift = r.gate[:, lane], r.gate_back[:, lane]
        for t in range(4):
            at = slice(t * TILE, (t + 1) * TILE)
            g = (r.grad_gated[c, at, :] * scale + shift) * r.depth[c, at, :]
            g = g.astype(BF16).astype(F32)
            for a in range(4):
                first = (1 + t * 4 + a) * PAD + 8
                r.grad_pre[c, first : first + MAP_COLS, :] = g[a * 64 : (a + 1) * 64]

        for side, row in ((0, 1), (1, MAP_ROWS)):
            at = pl.ds(row * PAD + 8, MAP_COLS)
            r.pre_rows[side, c] = r.grad_pre[c, at, :].astype(BF16)
        for side, col in ((0, 8), (1, 71)):
            at = pl.ds(PAD + col, MAP_ROWS, stride=PAD)
            r.pre_cols[side, c] = r.grad_pre[c, at, :].astype(BF16)

    for corner, at in enumerate((PAD + 8, PAD + 71, last - PAD + 8, last - PAD + 71)):
        cells = [r.grad_pre[c, at : at + 1, :] for c in range(LANES)]
        cells.append(jnp.zeros((8, 128), F32))
        r.pre_corners[corner] = jnp.concatenate(cells, axis=0).astype(BF16)

    pre_halo = Halo(
        me,
        links,
        (r.pre_rows.at[0], r.pre_rows.at[1]),
        r.pre_cols,
        [r.pre_corners.at[n] for n in range(4)],
        r.pre_rows_in,
        r.pre_cols_in,
        r.pre_corners_in,
    )
    pre_halo.start()

    att_back.end()

    @pl.loop(0, 4)
    def _(t):
        att = r.att_in[map_rows(t, 16)].reshape(TILE, CH)
        value = r.mixed[cell_rows(t)].astype(F32) + nn(att, r.w_out[...])
        r.out_map[map_rows(t)] = value.astype(BF16).reshape(4, MAP_COLS, CH)

    flush("out_map").start()
    bias_sum.back_q()
    pre_halo.end()

    @pl.loop(0, LANES)
    def _(c):
        r.grad_pre[c, 8:72, :] = r.pre_rows_in[0, c].astype(F32) * up_ok
        r.grad_pre[c, last + 8 : last + 72, :] = r.pre_rows_in[1, c].astype(F32) * down_ok
        left = r.pre_cols_in[0, c].astype(F32) * left_ok
        right = r.pre_cols_in[1, c].astype(F32) * right_ok
        r.grad_pre[c, pl.ds(PAD + 7, MAP_ROWS, stride=PAD), :] = left
        r.grad_pre[c, pl.ds(PAD + 72, MAP_ROWS, stride=PAD), :] = right

    corners = (
        (7, up_ok * left_ok),
        (72, up_ok * right_ok),
        (last + 7, down_ok * left_ok),
        (last + 72, down_ok * right_ok),
    )
    for corner, (at, ok) in enumerate(corners):
        cells = r.pre_corners_in[corner].astype(F32) * ok
        for c in range(LANES):
            r.grad_pre[c, at : at + 1, :] = cells[c : c + 1]

    r.tap_acc[...] = jnp.zeros_like(r.tap_acc)

    def depth_back(c):
        taps = taps_of(c)

        @pl.loop(0, MAP_ROWS // 2)
        def _(n):
            sums = [None] * 2
            inner = [
                r.spread[c, pl.ds(pad_row(1 + n * 2 + i, 8), MAP_COLS), :] for i in range(2)
            ]
            for b in range(3):
                parts = [None] * 3
                for row in range(4):
                    view = r.grad_pre.at[c, pl.ds(pad_row(n * 2 + row), PAD)]
                    v = view[pl.ds(7 + b, MAP_COLS), :]
                    for a in range(3):
                        i = row - a
                        if 0 <= i < 2:
                            term = v * taps[(2 - a) * 3 + 2 - b]
                            sums[i] = term if sums[i] is None else sums[i] + term
                            part = fold(v * inner[i])
                            parts[a] = part if parts[a] is None else parts[a] + part
                for a in range(3):
                    r.tap_acc[c, (2 - a) * 3 + 2 - b] += parts[a]
            for i in range(2):
                at = aligned((n * 2 + i) * MAP_COLS, MAP_COLS, MAP_COLS)
                r.grad_exp[c, at, :] = (sums[i] * r.expanded[c, at, :]).astype(BF16)

    pair_sum.end()
    project_sum.end()
    early = Gather(me, links, r.sum_early, r.grid_dy)
    for n, slots in enumerate((r.pair_slots, r.project_slots)):
        total = jnp.sum(slots[...].astype(F32), axis=0).astype(BF16)
        early.piece[:, n * 128 : (n + 1) * 128] = total

    @pl.loop(0, LANES)
    def _(c):
        depth_back(c)
        row = lax.rem(me.row + c, ROWS)
        for k in range(1, 8):
            early.send(row, k)

        @pl.when(c > 0)
        def _():
            early.send(row, 0)

    for c in range(4):
        lane = slice(c * 256, (c + 1) * 256)
        product = nn(r.normed_t[...], lanes_of(r.grad_exp, 2 * c, slice(None)))
        r.expand_x[:, lane] = product.astype(BF16)
    expand_sum = big("expand")
    expand_sum.start()
    for c in range(LANES):
        rows = [jnp.sum(r.tap_acc[c, k], axis=0, keepdims=True) for k in range(9)]
        r.taps_sum_x[c * 8 : c * 8 + 8, :128] = jnp.concatenate(rows[:8], axis=0)
        rows = [rows[8], jnp.zeros((7, 128), F32)]
        r.taps_sum_x[c * 8 : c * 8 + 8, 128:] = jnp.concatenate(rows, axis=0)
    parts = ["x", "pair", "summed", "a", "b"]
    taps_sum = SmallSum(
        me, links, *[getattr(r, "taps_sum_" + p) for p in parts], r.sum_taps
    )
    taps_sum.start()
    expand_sum.scatter()
    taps_sum.to_q()

    @pl.loop(0, 4)
    def _(t):
        grad = None
        for c in range(4):
            lane = slice(c * 256, (c + 1) * 256)
            part = nt(lanes_of(r.grad_exp, 2 * c, cell_rows(t)), r.w_expand[:, lane])
            grad = part if grad is None else grad + part
        unit, rstd = centre(r.image[map_rows(t)].reshape(TILE, CH).astype(F32))
        r.norm_acc[0] += fold(grad * unit)
        value = r.grad_mixed[cell_rows(t)] + norm_back(unit, rstd, grad * gain_first)
        r.grad_map[map_rows(t)] = value.astype(BF16).reshape(4, MAP_COLS, CH)

    flush("grad_map").start()
    rows = []
    for n in range(2):
        sums = jnp.sum(r.norm_acc[n], axis=0, keepdims=True)
        rows += [sums[:, :128], sums[:, 128:]]
    r.norms_x[...] = jnp.concatenate(rows + [jnp.zeros((4, 128), F32)], axis=0)
    norms_sum = TileSum(me, links, r.norms_x, r.norms_pair, r.norms_slots)
    norms_sum.start()
    bias_sum.end()
    flush("sum_bias").start()
    rows = [pooled, grad_logit, jnp.pad(hidden, ((0, 0), (0, 960)))]
    rows += [jnp.pad(grad_squeezed, ((0, 0), (0, 960))), jnp.zeros((4, 1024), F32)]
    r.gate_rows[...] = jnp.concatenate(rows, axis=0)
    flush("gate_rows").start()
    taps_sum.to_rows()
    expand_sum.end()
    final = Gather(me, links, r.sum_expand, r.expand_slots)
    final.piece[...] = jnp.sum(r.expand_slots[...].astype(F32), axis=0).astype(BF16)
    final.send_all()
    early.back_pair()
    taps_sum.back_q()
    early.end()
    flush("sum_early").start()
    r.sum_norms[...] = norms_sum.end()
    flush("sum_norms").start()
    taps_sum.end()
    flush("sum_taps").start()
    final.back_pair()
    final.end()
    flush("sum_expand").start()
    for name in OUTS:
        flush(name).wait()
    links.finish()


FINAL = dict(
    block_out=((MAP_ROWS, MAP_COLS, CH), BF16),
    grad_image=((MAP_ROWS, MAP_COLS, CH), BF16),
    grad_norm0=((1, CH), F32),
    grad_expand=((CH, 1024), F32),
    grad_depth=((3, 3, 1024), F32),
    grad_squeeze=((64, 1024), F32),
    grad_excite=((64, 1024), F32),
    grad_project=((1024, CH), F32),
    grad_norm1=((1, CH), F32),
    grad_qkv=((CH, 3 * CH), F32),
    grad_out_proj=((CH, CH), F32),
    grad_bias=((HEADS, MEMBERS, MEMBERS), F32),
)


def finish_kernel(*args):
    r = Refs()
    for name, ref in zip(list(OUTS) + list(FINAL), args, strict=True):
        setattr(r, name, ref)
    r.block_out[...] = r.out_map[...]
    r.grad_image[...] = r.grad_map[...]
    r.grad_expand[...] = r.sum_expand[...].astype(F32)
    for n in range(8):
        lane = slice(n * 128, (n + 1) * 128)
        part = r.sum_early[:, n * 256 : n * 256 + 128].astype(F32)
        if n < 6:
            r.grad_qkv[:, lane] = part
        else:
            r.grad_out_proj[:, (n - 6) * 128 : (n - 5) * 128] = part
        r.grad_project[lane, :] = r.sum_early[:, n * 256 + 128 : n * 256 + 256].astype(F32).T
    for h in range(0, HEADS, 2):
        both = r.sum_bias[:, h * 64 : (h + 2) * 64].T
        r.grad_bias[h] = both[:64]
        r.grad_bias[h + 1] = both[64:]
    for k in range(9):
        if k < 8:
            rows = [r.sum_taps[c * 8 + k : c * 8 + k + 1, :128] for c in range(LANES)]
        else:
            rows = [r.sum_taps[c * 8 : c * 8 + 1, 128:] for c in range(LANES)]
        r.grad_depth[k // 3, k % 3 : k % 3 + 1, :] = jnp.concatenate(rows, axis=1)
    for n, out in enumerate((r.grad_norm0, r.grad_norm1)):
        rows = [r.sum_norms[n * 2 + c : n * 2 + c + 1, :] for c in range(2)]
        out[...] = jnp.concatenate(rows, axis=1)
    pooled, grad_logit = r.gate_rows[0:1, :], r.gate_rows[1:2, :]
    hidden, grad_squeezed = r.gate_rows[2:3, :64], r.gate_rows[3:4, :64]
    r.grad_excite[...] = outer(hidden, grad_logit)
    r.grad_squeeze[...] = outer(grad_squeezed, pooled)


def on_device(
    image,
    out_cotangent,
    norm0_gain,
    w_expand,
    w_depth,
    w_squeeze,
    w_excite,
    w_project,
    norm1_gain,
    w_qkv,
    w_out,
    attn_bias,
):
    vmem = pl.BlockSpec(memory_space=pltpu.VMEM)
    any_space = pl.BlockSpec(memory_space=pl.ANY)
    buffers = lambda shapes: [pltpu.VMEM(*shape) for shape in shapes.values()]
    made = pl.pallas_call(
        block_kernel,
        out_shape=[jax.ShapeDtypeStruct(*shape) for shape in OUTS.values()],
        in_specs=[vmem] * len(IN_NAMES) + [any_space] * len(LATE),
        out_specs=[any_space] * len(OUTS),
        scratch_shapes=buffers(LATE)
        + buffers(OUTS)
        + buffers(SCRATCH)
        + [pltpu.SemaphoreType.DMA((n,)) for n in (SEMS, len(LATE), len(OUTS))],
        compiler_params=pltpu.CompilerParams(
            collective_id=0, has_side_effects=True, vmem_limit_bytes=63 * 2**20
        ),
        name="block",
    )(
        image,
        norm0_gain,
        norm1_gain,
        w_depth,
        w_expand,
        out_cotangent.reshape(MEMBERS, GROUPS, CH),
        w_out,
        attn_bias,
        w_squeeze.T,
        w_excite,
        w_project,
        w_qkv,
    )
    final = pl.pallas_call(
        finish_kernel,
        out_shape=[jax.ShapeDtypeStruct(*shape) for shape in FINAL.values()],
        in_specs=[vmem] * len(OUTS),
        out_specs=[vmem] * len(FINAL),
        compiler_params=pltpu.CompilerParams(vmem_limit_bytes=63 * 2**20),
        name="finish",
    )(*made)
    final = dict(zip(FINAL, final))
    final["grad_norm0"] = final["grad_norm0"].reshape(CH)
    final["grad_norm1"] = final["grad_norm1"].reshape(CH)
    final["grad_squeeze"] = final["grad_squeeze"].T
    return tuple(final.values())


def solution(mesh):
    mapped = P("row", "col", None)
    return jax.shard_map(
        on_device,
        mesh=mesh,
        in_specs=(mapped, mapped) + (P(),) * 10,
        out_specs=(mapped, mapped) + (P(),) * 10,
        check_vma=False,
    )
```

```python
import functools

import jax
import jax.numpy as jnp
from jax import lax
from jax.experimental import pallas as pl
from jax.experimental.pallas import tpu as pltpu
from jax.sharding import PartitionSpec as P

F32 = jnp.float32
BF16 = jnp.bfloat16
MESH = pl.DeviceIdType.MESH
ROWS = 8
COLS = 16
CHIPS = 64
HEADS = 8
MEMBERS = 64
GROUPS = 16
CH = 256
MAP_ROWS = 16
MAP_COLS = 64
CELLS = MAP_ROWS * MAP_COLS
CELLS_TOTAL = 131072
LANES = 8
PAD = 80
PADDED = (MAP_ROWS + 2) * PAD
TILE = 256
SCALE = 32 ** (-0.5)
GELU_A = 0.7978845608028654
GELU_B = 0.044715


def nn(a, b):
    return jnp.dot(a, b, preferred_element_type=F32)


def nt(a, b):
    return lax.dot_general(a, b, (((1,), (1,)), ((), ())), preferred_element_type=F32)


def tn(a, b):
    return lax.dot_general(a, b, (((0,), (0,)), ((), ())), preferred_element_type=F32)


def gelu(x):
    return 0.5 * x * (1.0 + jnp.tanh(GELU_A * (x + GELU_B * (x * x * x))))


def gelu_slope(x):
    square = x * x
    t = jnp.tanh(GELU_A * (x + GELU_B * (square * x)))
    return 0.5 * (1.0 + t) + (0.5 * GELU_A) * x * (1.0 - t * t) * (1.0 + (3 * GELU_B) * square)


def centre(x):
    centered = x - jnp.mean(x, axis=-1, keepdims=True)
    rstd = lax.rsqrt(jnp.mean(centered * centered, axis=-1, keepdims=True) + 1e-05)
    return centered * rstd, rstd


def norm_back(unit, rstd, grad_unit):
    first = jnp.mean(grad_unit, axis=-1, keepdims=True)
    second = jnp.mean(grad_unit * unit, axis=-1, keepdims=True)
    return rstd * (grad_unit - first - unit * second)


def fold(x):
    return jnp.sum(x.reshape(x.shape[0] // 8, 8, x.shape[1]), axis=0)


def thirds(x):
    one = x.astype(BF16).astype(F32)
    two = (x - one).astype(BF16).astype(F32)
    three = (x - one - two).astype(BF16).astype(F32)
    return one, two, three


def stack_rows(rows):
    width = rows[0].shape[1]
    rows = list(rows) + [jnp.zeros((8 - len(rows), width), F32)]
    return jnp.concatenate(rows, axis=0).astype(BF16)


def wide_product(x, w, product):
    return jnp.sum(product(stack_rows(thirds(x)), w), axis=0, keepdims=True)


def outer(a, b):
    a1, a2, a3 = thirds(a)
    b1, b2, b3 = thirds(b)
    return tn(stack_rows([a1, a1, a2, a2, a1, a3]), stack_rows([b1, b2, b1, b2, b3, b1]))


def aligned(start, size, unit=8):
    return pl.ds(pl.multiple_of(start, unit), size)


class Place:
    def __init__(self):
        self.row = lax.axis_index("row")
        self.col = lax.axis_index("col")
        self.core = lax.rem(self.col, 2)
        self.q = lax.div(self.col, 2)
        self.chip = self.row * 8 + self.q
        self.qs = [lax.rem(self.q + k, 8) for k in range(8)]
        self.cols = [q * 2 + self.core for q in self.qs]

    def partner(self):
        return (self.row, self.q * 2 + 1 - self.core)

    def q_peer(self, k):
        return self.qs[k], (self.row, self.cols[k])

    def row_peer(self, k):
        row = lax.rem(self.row + k, ROWS)
        return row, (row, self.col)

    def beside(self, up, right):
        return (lax.rem(self.row + ROWS + up, ROWS), lax.rem(self.col + COLS + right, COLS))

    def every_peer(self, body):
        def others(k, carry):
            row = lax.rem(self.row + k, ROWS)
            for n in range(1, 8):
                body(row, self.qs[n], (row, self.cols[n]))
            return carry

        def same(k, carry):
            row = lax.rem(self.row + k, ROWS)
            body(row, self.q, (row, self.col))
            return carry

        lax.fori_loop(0, ROWS, others, 0)
        lax.fori_loop(1, ROWS, same, 0)


class Links:
    def __init__(self, sems):
        self.sems = sems
        self.used = 0
        self.sent = []

    def pair(self):
        at = self.used
        self.used += 2
        return self.sems.at[at], self.sems.at[at + 1]

    def finish(self):
        for sem, buf in self.sent:
            pltpu.make_async_copy(buf, buf, sem).wait()


def push(src, dst, send, recv, device):
    pltpu.make_async_remote_copy(
        src_ref=src,
        dst_ref=dst,
        send_sem=send,
        recv_sem=recv,
        device_id=device,
        device_id_type=MESH,
    ).start()


def arrived(buf, sem):
    pltpu.make_async_copy(buf, buf, sem).wait()


class TileSum:
    def __init__(self, me, links, x, pair_slot, slots):
        self.me, self.links = me, links
        self.x, self.pair_slot, self.slots = x, pair_slot, slots
        self.s0, self.s1 = links.pair(), links.pair()

    def start(self):
        push(self.x, self.pair_slot, *self.s0, self.me.partner())
        self.links.sent.append((self.s0[0], self.x))
        arrived(self.pair_slot, self.s0[1])
        self.slots[self.me.chip] = self.x[...] + self.pair_slot[...]
        mine = self.slots.at[self.me.chip]
        self.me.every_peer(lambda row, q, device: push(mine, mine, *self.s1, device))
        self.links.sent.append((self.s1[0], self.slots.at[pl.ds(0, CHIPS - 1)]))

    def end(self):
        arrived(self.slots.at[pl.ds(0, CHIPS - 1)], self.s1[1])
        return jnp.sum(self.slots[...], axis=0)


class Scatter:
    def __init__(self, me, links, x, pair_in, summed, slots):
        self.me, self.links = me, links
        self.x, self.pair_in, self.summed, self.slots = x, pair_in, summed, slots
        self.sems = [links.pair() for _ in range(2)]

    def half_of(self, core):
        return self.x.at[aligned(core * 128, 128, 128)]

    def piece(self, row, q):
        return self.summed.at[aligned(row * 16, 16, 16), aligned(q * 128, 128, 128)]

    def start(self):
        push(self.half_of(1 - self.me.core), self.pair_in, *self.sems[0], self.me.partner())
        self.links.sent.append((self.sems[0][0], self.pair_in))

    def scatter(self):
        me = self.me
        arrived(self.pair_in, self.sems[0][1])
        mine = self.half_of(me.core)
        self.summed[...] = (mine[...].astype(F32) + self.pair_in[...].astype(F32)).astype(BF16)
        to = self.slots.at[me.chip]
        me.every_peer(
            lambda row, q, device: push(self.piece(row, q), to, *self.sems[1], device)
        )
        self.slots[me.chip] = self.piece(me.row, me.q)[...]

    def end(self):
        arrived(self.slots.at[pl.ds(0, CHIPS - 1)], self.sems[1][1])
        self.links.sent.append((self.sems[1][0], self.slots.at[pl.ds(0, CHIPS - 1)]))


class Gather:
    def __init__(self, me, links, out, like):
        self.me, self.links, self.out, self.like = me, links, out, like
        self.width = out.shape[1] // 8
        self.sems = [links.pair() for _ in range(2)]
        lane = aligned(me.q * self.width, self.width, 128)
        self.piece = out.at[aligned(me.core * 128 + me.row * 16, 16, 16), lane]

    def send(self, row, k):
        push(self.piece, self.piece, *self.sems[0], (row, self.me.cols[k]))

    def send_all(self):
        self.me.every_peer(
            lambda row, q, device: push(self.piece, self.piece, *self.sems[0], device)
        )

    def back_pair(self):
        me = self.me
        arrived(self.like.at[pl.ds(0, CHIPS - 1)], self.sems[0][1])
        self.links.sent.append((self.sems[0][0], self.like.at[pl.ds(0, CHIPS - 1)]))
        half = self.out.at[aligned(me.core * 128, 128, 128)]
        push(half, half, *self.sems[1], me.partner())
        self.links.sent.append((self.sems[1][0], half))

    def end(self):
        arrived(self.out.at[pl.ds(0, 128)], self.sems[1][1])


class SmallSum:
    def __init__(self, me, links, x, pair_in, summed, slots_a, slots_b, out):
        self.me, self.links = me, links
        self.x, self.pair_in, self.summed, self.out = x, pair_in, summed, out
        self.slots_a, self.slots_b = slots_a, slots_b
        self.sems = [links.pair() for _ in range(4)]

    def start(self):
        push(self.x, self.pair_in, *self.sems[0], self.me.partner())
        self.links.sent.append((self.sems[0][0], self.pair_in))

    def to_q(self):
        arrived(self.pair_in, self.sems[0][1])
        self.summed[...] = self.x[...] + self.pair_in[...]
        for k in range(1, 8):
            q, device = self.me.q_peer(k)
            piece = self.summed.at[aligned(q * 8, 8)]
            push(piece, self.slots_a.at[self.me.q], *self.sems[1], device)
        self.links.sent.append((self.sems[1][0], self.slots_a.at[pl.ds(0, 7)]))

    def to_rows(self):
        me = self.me
        self.slots_a[me.q] = self.summed[aligned(me.q * 8, 8)]
        arrived(self.slots_a.at[pl.ds(0, 7)], self.sems[1][1])
        self.slots_b[me.row] = jnp.sum(self.slots_a[...], axis=0)
        for k in range(1, 8):
            _, device = me.row_peer(k)
            piece = self.slots_b.at[me.row]
            push(piece, piece, *self.sems[2], device)
        self.links.sent.append((self.sems[2][0], self.slots_b.at[pl.ds(0, 7)]))

    def back_q(self):
        me = self.me
        arrived(self.slots_b.at[pl.ds(0, 7)], self.sems[2][1])
        piece = self.out.at[aligned(me.q * 8, 8)]
        piece[...] = jnp.sum(self.slots_b[...], axis=0)
        for k in range(1, 8):
            _, device = me.q_peer(k)
            push(piece, piece, *self.sems[3], device)
        self.links.sent.append((self.sems[3][0], self.slots_a.at[pl.ds(0, 7)]))

    def end(self):
        arrived(self.slots_a.at[pl.ds(0, 7)], self.sems[3][1])


class Exchange:
    def __init__(self, me, links, src, dst):
        self.me, self.links, self.src, self.dst = me, links, src, dst
        self.sems = links.pair()

    def send(self, row, k):
        q, col = self.me.qs[k], self.me.cols[k]
        push(self.src.at[row * 8 + q], self.dst.at[self.me.chip], *self.sems, (row, col))

    def send_row(self, row):
        for k in range(1, 8):
            self.send(row, k)

        @pl.when(row != self.me.row)
        def _():
            self.send(row, 0)

    def send_tile(self, t):
        for k in range(2):
            self.send_row(t * 2 + lax.rem(self.me.row + k, 2))

    def end(self):
        self.dst[self.me.chip] = self.src[self.me.chip]
        arrived(self.dst.at[pl.ds(0, CHIPS - 1)], self.sems[1])
        self.links.sent.append((self.sems[0], self.dst.at[pl.ds(0, CHIPS - 1)]))


class Halo:
    def __init__(
        self, me, links, rows_out, cols_out, corners_out, rows_in, cols_in, corners_in
    ):
        self.me, self.links = me, links
        self.rows_out, self.cols_out, self.corners_out = rows_out, cols_out, corners_out
        self.rows_in, self.cols_in, self.corners_in = rows_in, cols_in, corners_in
        self.sems = [links.pair() for _ in range(3)]

    def start(self):
        me = self.me
        for side, up in ((0, -1), (1, 1)):
            push(
                self.rows_out[side],
                self.rows_in.at[1 - side],
                *self.sems[0],
                me.beside(up, 0),
            )
        for side, right in ((0, -1), (1, 1)):
            strip = self.cols_out.at[side]
            push(strip, self.cols_in.at[1 - side], *self.sems[1], me.beside(0, right))
            for end, up in ((0, -1), (1, 1)):
                push(
                    self.corners_out[end * 2 + side],
                    self.corners_in.at[(1 - end) * 2 + 1 - side],
                    *self.sems[2],
                    me.beside(up, right),
                )

    def end(self):
        for n, buf in enumerate((self.rows_in, self.cols_in, self.corners_in)):
            arrived(buf, self.sems[n][1])
            self.links.sent.append((self.sems[n][0], buf))


IN_NAMES = ["image", "norm0_gain", "norm1_gain", "w_depth", "w_expand"]
LATE = dict(
    dy=((MEMBERS, GROUPS, CH), BF16),
    w_out=((CH, CH), BF16),
    bias=((HEADS, MEMBERS, MEMBERS), F32),
    w_squeeze_t=((64, 1024), BF16),
    w_excite=((64, 1024), BF16),
    w_project=((1024, CH), BF16),
    w_qkv=((CH, 768), BF16),
)
OUTS = dict(
    out_map=((MAP_ROWS, MAP_COLS, CH), BF16),
    grad_map=((MAP_ROWS, MAP_COLS, CH), BF16),
    sum_expand=((CH, 1024), BF16),
    sum_early=((CH, 2048), BF16),
    sum_bias=((MEMBERS, 512), F32),
    sum_taps=((64, 256), F32),
    sum_norms=((8, 128), F32),
    gate_rows=((8, 1024), F32),
)


def big_scratch(name):
    return {
        name + "_x": ((CH, 1024), BF16),
        name + "_pair": ((CH // 2, 1024), BF16),
        name + "_summed": ((CH // 2, 1024), BF16),
    }


def small_scratch(name, width):
    return {
        name + "_x": ((64, width), F32),
        name + "_pair": ((64, width), F32),
        name + "_summed": ((64, width), F32),
        name + "_a": ((8, 8, width), F32),
        name + "_b": ((8, 8, width), F32),
    }


def tile_scratch(name):
    return {
        name + "_x": ((8, 128), F32),
        name + "_pair": ((8, 128), F32),
        name + "_slots": ((CHIPS, 8, 128), F32),
    }


SCRATCH = dict(
    taps=((16, 1024), F32),
    normed=((CELLS, CH), BF16),
    normed_t=((CH, CELLS), BF16),
    spread=((LANES, PADDED, 128), F32),
    expanded=((LANES, CELLS, 128), F32),
    depth=((LANES, CELLS, 128), F32),
    act=((LANES, CELLS, 128), BF16),
    pool_acc=((LANES, 8, 128), F32),
    edge_cols=((2, 16, CH), BF16),
    edge_rows_in=((2, MAP_COLS, CH), BF16),
    edge_cols_in=((2, 16, CH), BF16),
    edge_corners_in=((4, 16, CH), BF16),
    gate=((1, 1024), F32),
    gate_back=((1, 1024), F32),
    mixed=((CELLS, CH), BF16),
    normed_two=((MEMBERS, GROUPS, CH), BF16),
    grid_x=((MEMBERS, GROUPS, CH), BF16),
    grid_dy=((MEMBERS, GROUPS, CH), BF16),
    qkv=((6, CELLS, 128), F32),
    grid_g=((2, CELLS, 128), F32),
    att_rows=((2, CELLS, 128), F32),
    packed_back=((6, CELLS, 128), F32),
    probs=((GROUPS, MEMBERS, 512), F32),
    bias_t=((MEMBERS, 512), F32),
    att_out=((MEMBERS, GROUPS, CH), BF16),
    att_in=((MEMBERS, GROUPS, CH), BF16),
    gn_out=((MEMBERS, GROUPS, CH), BF16),
    gn_in=((MEMBERS, GROUPS, CH), BF16),
    grad_mixed=((CELLS, CH), F32),
    grad_mixed_b=((CELLS, CH), BF16),
    grad_gated=((LANES, CELLS, 128), F32),
    gate_acc=((LANES, 8, 128), F32),
    grad_pre=((LANES, PADDED, 128), F32),
    slope_rows=((2, LANES, MAP_COLS, 128), BF16),
    slope_cols=((2, LANES, 16, 128), BF16),
    slope_corners=((4, 16, 128), BF16),
    slope_rows_in=((2, LANES, MAP_COLS, 128), BF16),
    slope_cols_in=((2, LANES, 16, 128), BF16),
    slope_corners_in=((4, 16, 128), BF16),
    pre_rows=((2, LANES, MAP_COLS, 128), BF16),
    pre_cols=((2, LANES, 16, 128), BF16),
    pre_rows_in=((2, LANES, MAP_COLS, 128), BF16),
    pre_cols_in=((2, LANES, 16, 128), BF16),
    pre_corners=((4, 16, 128), BF16),
    pre_corners_in=((4, 16, 128), BF16),
    tap_acc=((LANES, 9, 8, 128), F32),
    grad_exp=((LANES, CELLS, 128), BF16),
    norm_acc=((2, 8, CH), F32),
    pair_acc=((CH, 1024), F32),
    **tile_scratch("pool"),
    **tile_scratch("gateg"),
    **big_scratch("expand"),
    **big_scratch("project"),
    **big_scratch("pair"),
    expand_slots=((CHIPS, 16, 128), BF16),
    pair_slots=((CHIPS, 16, 128), BF16),
    project_slots=((CHIPS, 16, 128), BF16),
    **small_scratch("bias", 512),
    **small_scratch("taps_sum", 256),
    **tile_scratch("norms"),
)
SEMS = 96


class Refs:
    pass


def lanes_of(ref, first, at):
    return jnp.concatenate([ref[first, at, :], ref[first + 1, at, :]], axis=1)


def map_rows(t, count=4):
    return pl.ds(t * count, count)


def cell_rows(t):
    return aligned(t * TILE, TILE, TILE)


def pad_row(row, col=0):
    return pl.multiple_of(row * PAD + col, 8)


def block_kernel(*args):
    r = Refs()
    names = IN_NAMES + ["hbm_" + n for n in LATE] + ["hbm_" + n for n in OUTS]
    names += list(LATE) + list(OUTS) + list(SCRATCH) + ["sems", "late_sems", "out_sems"]
    for name, ref in zip(names, args, strict=True):
        setattr(r, name, ref)
    me = Place()
    links = Links(r.sems)

    def late(name):
        at = list(LATE).index(name)
        return pltpu.make_async_copy(
            getattr(r, "hbm_" + name), getattr(r, name), r.late_sems.at[at]
        )

    def flush(name):
        at = list(OUTS).index(name)
        return pltpu.make_async_copy(
            getattr(r, name), getattr(r, "hbm_" + name), r.out_sems.at[at]
        )

    for name in LATE:
        late(name).start()
    gain_first = r.norm0_gain[...].astype(F32).reshape(1, CH)
    gain_second = r.norm1_gain[...].astype(F32).reshape(1, CH)
    for a in range(3):
        r.taps[a * 3 : a * 3 + 3, :] = r.w_depth[a].astype(F32)
    off = r.image.shape[0] - 1

    barrier = pltpu.get_barrier_semaphore()

    def greet(row, q, device):
        pl.semaphore_signal(barrier, inc=1, device_id=device, device_id_type=MESH)

    me.every_peer(greet)
    for up in (-1, 0, 1):
        for right in (-1, 1):
            pl.semaphore_signal(
                barrier, inc=1, device_id=me.beside(up, right), device_id_type=MESH
            )

    for side, col in ((0, 0), (1, MAP_COLS - 16)):
        rows = []
        for i in range(MAP_ROWS):
            part = r.image[i, col : col + 16, :].astype(F32)
            rows.append(part[0:1] if side == 0 else part[15:16])
        r.edge_cols[side] = jnp.concatenate(rows, axis=0).astype(BF16)

    @pl.loop(0, 4)
    def _(t):
        x = r.image[map_rows(t)].reshape(TILE, CH).astype(F32)
        unit, _ = centre(x)
        r.normed[cell_rows(t)] = (unit * gain_first).astype(BF16)

    @pl.loop(0, 4)
    def _(t):
        @pl.loop(0, 4)
        def _(c):
            e = nn(r.normed[cell_rows(t)], r.w_expand[:, aligned(c * 256, 256, 256)])
            s = gelu(e).astype(BF16).astype(F32)
            for h in range(2):
                lane = slice(h * 128, (h + 1) * 128)
                r.expanded[2 * c + h, cell_rows(t), :] = e[:, lane]
                for a in range(4):
                    at = pl.ds(pad_row(1 + t * 4 + a, 8), MAP_COLS)
                    r.spread[2 * c + h, at, :] = s[a * 64 : (a + 1) * 64, lane]

    pl.semaphore_wait(barrier, CHIPS + 5)
    halo = Halo(
        me,
        links,
        (r.image.at[0], r.image.at[off]),
        r.edge_cols,
        [r.edge_cols.at[side] for side in (0, 1, 0, 1)],
        r.edge_rows_in,
        r.edge_cols_in,
        r.edge_corners_in,
    )
    halo.start()
    late("dy").wait()
    dy_out = Exchange(me, links, r.dy, r.grid_dy)

    @pl.loop(0, LANES)
    def _(c):
        row = lax.rem(me.row + c, ROWS)
        for t in range(4):
            for k in (2 * t + 1, 2 * t):
                if k:
                    dy_out.send(row, k)
            at = pl.ds(t * TILE, TILE)
            r.expanded[c, at, :] = gelu_slope(r.expanded[c, at, :])

        @pl.when(c > 0)
        def _():
            dy_out.send(row, 0)

    halo.end()

    up_ok = (me.row > 0).astype(F32)
    down_ok = (me.row < ROWS - 1).astype(F32)
    left_ok = (me.col > 0).astype(F32)
    right_ok = (me.col < COLS - 1).astype(F32)
    around = jnp.concatenate(
        [
            r.edge_rows_in[0].astype(F32) * up_ok,
            r.edge_rows_in[1].astype(F32) * down_ok,
            r.edge_cols_in[0].astype(F32) * left_ok,
            r.edge_cols_in[1].astype(F32) * right_ok,
            r.edge_corners_in[0].astype(F32)[8:16] * (up_ok * left_ok),
            r.edge_corners_in[1].astype(F32)[8:16] * (up_ok * right_ok),
            r.edge_corners_in[2].astype(F32)[0:8] * (down_ok * left_ok),
            r.edge_corners_in[3].astype(F32)[0:8] * (down_ok * right_ok),
        ],
        axis=0,
    )
    unit, _ = centre(around)
    around_normed = (unit * gain_first).astype(BF16)
    last = (MAP_ROWS + 1) * PAD
    for c in range(4):
        s = gelu(nn(around_normed, r.w_expand[:, c * 256 : (c + 1) * 256]))
        s = s.astype(BF16).astype(F32)
        for h in range(2):
            v = s[:, h * 128 : (h + 1) * 128]
            n = 2 * c + h
            r.spread[n, 8:72, :] = v[0:64]
            r.spread[n, last + 8 : last + 72, :] = v[64:128]
            r.spread[n, pl.ds(PAD + 7, MAP_ROWS, stride=PAD), :] = v[128:144]
            r.spread[n, pl.ds(PAD + 72, MAP_ROWS, stride=PAD), :] = v[144:160]
            r.spread[n, 7:8, :] = v[167:168]
            r.spread[n, 72:73, :] = v[175:176]
            r.spread[n, last + 7 : last + 8, :] = v[176:177]
            r.spread[n, last + 72 : last + 73, :] = v[184:185]

    def taps_of(c):
        lane = aligned(c * 128, 128, 128)
        return [r.taps[k : k + 1, lane] for k in range(9)]

    @pl.loop(0, LANES)
    def _(c):
        taps = taps_of(c)

        def block(n, total):
            sums = [None] * 4
            for row in range(6):
                view = r.spread.at[c, pl.ds(pad_row(n * 4 + row), PAD)]
                for b in range(3):
                    v = view[pl.ds(7 + b, MAP_COLS), :]
                    for a in range(3):
                        i = row - a
                        if 0 <= i < 4:
                            term = v * taps[a * 3 + b]
                            sums[i] = term if sums[i] is None else sums[i] + term
            for i in range(4):
                at = aligned((n * 4 + i) * MAP_COLS, MAP_COLS, MAP_COLS)
                r.depth[c, at, :] = sums[i]
                value = gelu(sums[i])
                r.act[c, at, :] = value.astype(BF16)
                total = total + fold(value)
            return total

        total = lax.fori_loop(0, 4, block, jnp.zeros((8, 128), F32))
        r.pool_x[pl.ds(c, 1), :] = jnp.sum(total, axis=0, keepdims=True)

    pool = TileSum(me, links, r.pool_x, r.pool_pair, r.pool_slots)
    pool.start()

    @pl.loop(0, LANES * 4)
    def _(n):
        c, t = lax.div(n, 4), lax.rem(n, 4)
        r.depth[c, cell_rows(t), :] = gelu_slope(r.depth[c, cell_rows(t), :])

    dy_out.end()
    late("w_out").wait()
    late("bias").wait()

    @pl.loop(0, 4)
    def _(t):
        dy = r.grid_dy[map_rows(t, 16)].reshape(TILE, CH)
        g = nt(dy, r.w_out[...])
        for n in range(2):
            r.grid_g[n, cell_rows(t), :] = g[:, n * 128 : (n + 1) * 128]

    for h in range(0, HEADS, 2):
        both = jnp.concatenate([r.bias[h], r.bias[h + 1]], axis=0)
        r.bias_t[:, h * 64 : (h + 2) * 64] = both.T
    for t in range(4):
        r.normed_t[:, t * TILE : (t + 1) * TILE] = r.normed[t * TILE : (t + 1) * TILE].T

    def flat(tile):
        return jnp.concatenate([tile[n : n + 1] for n in range(8)], axis=1)

    pooled = flat(pool.end()) * (1.0 / CELLS_TOTAL)
    for name in ("w_squeeze_t", "w_excite", "w_project", "w_qkv"):
        late(name).wait()
    squeezed = wide_product(pooled, r.w_squeeze_t[...], nt)
    open_part = jax.nn.sigmoid(squeezed)
    hidden = squeezed * open_part
    gate = jax.nn.sigmoid(wide_product(hidden, r.w_excite[...], nn))
    r.gate[...] = gate

    grid_out = Exchange(me, links, r.normed_two, r.grid_x)
    start_tile = lax.div(me.row, 2)

    @pl.loop(0, 4)
    def _(step):
        t = lax.rem(start_tile + step, 4)
        total = r.image[map_rows(t)].reshape(TILE, CH).astype(F32)
        for c in range(4):
            lane = slice(c * 256, (c + 1) * 256)
            gated = lanes_of(r.act, 2 * c, cell_rows(t)).astype(F32) * r.gate[:, lane]
            total = total + nn(gated.astype(BF16), r.w_project[lane, :])
        mixed = total.astype(BF16)
        r.mixed[cell_rows(t)] = mixed
        unit, _ = centre(mixed.astype(F32))
        normed = (unit * gain_second).astype(BF16)
        r.normed_two[map_rows(t, 16)] = normed.reshape(16, GROUPS, CH)
        grid_out.send_tile(t)

    def pack_edges(ref, width, first, rows_out, cols_out, corners_out):
        final_row = first + (MAP_ROWS - 1) * width

        @pl.loop(0, LANES)
        def _(c):
            for side, at in ((0, first), (1, final_row)):
                rows_out[side, c] = ref[c, at : at + MAP_COLS, :].astype(BF16)
            for side, at in ((0, first), (1, first + MAP_COLS - 1)):
                cells = ref[c, pl.ds(at, MAP_ROWS, stride=width), :]
                cols_out[side, c] = cells.astype(BF16)

        ends = (first, first + MAP_COLS - 1, final_row, final_row + MAP_COLS - 1)
        for corner, at in enumerate(ends):
            cells = [ref[c, at : at + 1, :] for c in range(LANES)]
            cells.append(jnp.zeros((8, 128), F32))
            corners_out[corner] = jnp.concatenate(cells, axis=0).astype(BF16)

    def edge_halo(name):
        parts = ["rows", "cols", "corners", "rows_in", "cols_in", "corners_in"]
        rows, cols, corners, *arriving = [getattr(r, name + "_" + p) for p in parts]
        return Halo(
            me,
            links,
            (rows.at[0], rows.at[1]),
            cols,
            [corners.at[n] for n in range(4)],
            *arriving,
        )

    pack_edges(r.depth, MAP_COLS, 0, r.slope_rows, r.slope_cols, r.slope_corners)
    slope_halo = edge_halo("slope")
    slope_halo.start()
    grid_out.end()

    @pl.loop(0, 4)
    def _(t):
        x = r.grid_x[map_rows(t, 16)].reshape(TILE, CH)
        qkv = nn(x, r.w_qkv[...])
        for n in range(6):
            r.qkv[n, cell_rows(t), :] = qkv[:, n * 128 : (n + 1) * 128]

    head_of = lax.div(lax.broadcasted_iota(jnp.int32, (1, 128), 1), 32)
    masks_f = [(head_of == h).astype(F32) for h in range(4)]
    masks = [m.astype(BF16) for m in masks_f]
    unroll = 8

    def spread_heads(a):
        return jnp.concatenate([a * m for m in masks], axis=0)

    def own_heads(v):
        total = v[0:MEMBERS] * masks_f[0]
        for h in range(1, 4):
            total = total + v[h * MEMBERS : (h + 1) * MEMBERS] * masks_f[h]
        return total

    def put(ref, n, at, value):
        ref[n, at, :] = value.astype(BF16).astype(F32)

    def group_forward(group):
        at = pl.ds(group, MEMBERS, stride=GROUPS)
        for n in range(2):
            q, k, v = [r.qkv[part * 2 + n, at, :].astype(BF16) for part in range(3)]
            lanes = slice(n * 256, (n + 1) * 256)
            scores = nt(k, spread_heads(q)) * SCALE + r.bias_t[:, lanes]
            lifted = jnp.exp(scores - jnp.max(scores, axis=0, keepdims=True))
            probs = lifted * (1.0 / jnp.sum(lifted, axis=0, keepdims=True))
            r.probs[group, :, lanes] = probs
            put(r.att_rows, n, at, own_heads(tn(probs.astype(BF16), v)))

    def group_back(group):
        at = pl.ds(group, MEMBERS, stride=GROUPS)
        bias_parts = []
        for n in range(2):
            q, k, v = [r.qkv[part * 2 + n, at, :].astype(BF16) for part in range(3)]
            lanes = slice(n * 256, (n + 1) * 256)
            q_heads = spread_heads(q)
            g_heads = spread_heads(r.grid_g[n, at, :].astype(BF16))
            probs = r.probs[group, :, lanes]
            put(r.packed_back, 4 + n, at, nn(probs.astype(BF16), g_heads))
            grad_probs = nt(v, g_heads)
            grad_scores = probs * (
                grad_probs - jnp.sum(grad_probs * probs, axis=0, keepdims=True)
            )
            bias_parts.append(grad_scores)
            scaled = (grad_scores * SCALE).astype(BF16)
            put(r.packed_back, n, at, own_heads(tn(scaled, k)))
            put(r.packed_back, 2 + n, at, nn(scaled, q_heads))
        return bias_parts

    @pl.loop(0, GROUPS // unroll)
    def _(step):
        for n in range(unroll):
            group_forward(step * unroll + n)

    @pl.loop(0, 4)
    def _(t):
        att = lanes_of(r.att_rows, 0, cell_rows(t)).astype(BF16)
        r.att_out[map_rows(t, 16)] = att.reshape(16, GROUPS, CH)

    att_back = Exchange(me, links, r.att_out, r.att_in)
    r.bias_x[...] = jnp.zeros_like(r.bias_x)

    @pl.loop(0, GROUPS // unroll)
    def _(step):
        for n in range(4):
            att_back.send_row(lax.rem(me.row + step * 4 + n, ROWS))
        total = group_back(step * unroll)
        for n in range(1, unroll):
            total = [a + b for a, b in zip(total, group_back(step * unroll + n))]
        for n in range(2):
            r.bias_x[:, n * 256 : (n + 1) * 256] += total[n]

    def packed_tile(t):
        parts = [r.packed_back[n, cell_rows(t), :] for n in range(6)]
        return jnp.concatenate(parts, axis=1).astype(BF16)

    gn_back = Exchange(me, links, r.gn_out, r.gn_in)

    @pl.loop(0, 4)
    def _(step):
        t = lax.rem(start_tile + step, 4)
        gn = nt(packed_tile(t), r.w_qkv[...]).astype(BF16)
        r.gn_out[map_rows(t, 16)] = gn.reshape(16, GROUPS, CH)
        gn_back.send_tile(t)

    bias_sum = SmallSum(
        me, links, r.bias_x, r.bias_pair, r.bias_summed, r.bias_a, r.bias_b, r.sum_bias
    )
    bias_sum.start()
    r.pair_acc[...] = jnp.zeros_like(r.pair_acc)

    @pl.loop(0, 4)
    def _(t):
        x = r.grid_x[map_rows(t, 16)].reshape(TILE, CH)
        dy = r.grid_dy[map_rows(t, 16)].reshape(TILE, CH)
        att = r.att_out[map_rows(t, 16)].reshape(TILE, CH)
        r.pair_acc[:, : 3 * CH] += tn(x, packed_tile(t))
        r.pair_acc[:, 3 * CH :] += tn(att, dy)

    r.pair_x[...] = r.pair_acc[...].astype(BF16)

    def big(name):
        parts = ["x", "pair", "summed", "slots"]
        return Scatter(me, links, *[getattr(r, name + "_" + p) for p in parts])

    pair_sum = big("pair")
    pair_sum.start()
    bias_sum.to_q()
    pair_sum.scatter()
    gn_back.end()

    r.norm_acc[...] = jnp.zeros_like(r.norm_acc)
    r.gate_acc[...] = jnp.zeros_like(r.gate_acc)

    @pl.loop(0, 4)
    def _(t):
        unit, rstd = centre(r.mixed[cell_rows(t)].astype(F32))
        gn = r.gn_in[map_rows(t, 16)].reshape(TILE, CH).astype(F32)
        r.norm_acc[1] += fold(gn * unit)
        dy = r.dy[map_rows(t, 16)].reshape(TILE, CH).astype(F32)
        grad = dy + norm_back(unit, rstd, gn * gain_second)
        r.grad_mixed[cell_rows(t)] = grad
        grad_b = grad.astype(BF16)
        r.grad_mixed_b[cell_rows(t)] = grad_b
        for c in range(4):
            gg = nt(grad_b, r.w_project[c * 256 : (c + 1) * 256, :])
            for h in range(2):
                n = 2 * c + h
                part = gg[:, h * 128 : (h + 1) * 128]
                r.grad_gated[n, cell_rows(t), :] = part
                r.gate_acc[n] += fold(part * r.act[n, cell_rows(t), :].astype(F32))

    for n in range(LANES):
        r.gateg_x[n : n + 1, :] = jnp.sum(r.gate_acc[n], axis=0, keepdims=True)
    gate_sum = TileSum(me, links, r.gateg_x, r.gateg_pair, r.gateg_slots)
    gate_sum.start()

    @pl.loop(0, LANES)
    def _(c):
        scale = r.gate[:, aligned(c * 128, 128, 128)]
        for t in range(4):
            at = slice(t * TILE, (t + 1) * TILE)
            g = r.grad_gated[c, at, :] * scale * r.depth[c, at, :]
            for a in range(4):
                first = (1 + t * 4 + a) * PAD + 8
                r.grad_pre[c, first : first + MAP_COLS, :] = g[a * 64 : (a + 1) * 64]

    pack_edges(r.grad_pre, PAD, PAD + 8, r.pre_rows, r.pre_cols, r.pre_corners)
    pre_halo = edge_halo("pre")
    pre_halo.start()
    grad_t = r.grad_mixed_b[...].T
    for c in range(4):
        lane = slice(c * 256, (c + 1) * 256)
        product = nn(grad_t, lanes_of(r.act, 2 * c, slice(None))) * r.gate[:, lane]
        r.project_x[:, lane] = product.astype(BF16)
    project_sum = big("project")
    project_sum.start()
    bias_sum.to_rows()
    project_sum.scatter()
    slope_halo.end()
    pre_halo.end()
    grad_gate = flat(gate_sum.end())
    grad_logit = grad_gate * gate * (1.0 - gate)
    grad_hidden = wide_product(grad_logit, r.w_excite[...], nt)
    grad_squeezed = grad_hidden * (open_part * (1.0 + squeezed * (1.0 - open_part)))
    r.gate_back[...] = wide_product(grad_squeezed, r.w_squeeze_t[...], nn) * (1.0 / CELLS_TOTAL)

    @pl.loop(0, LANES)
    def _(c):
        shift = r.gate_back[:, aligned(c * 128, 128, 128)]

        def beside(part, slope, ok):
            return (part.astype(F32) + shift * slope.astype(F32)) * ok

        for row in range(MAP_ROWS):
            first = (1 + row) * PAD + 8
            at = slice(first, first + MAP_COLS)
            slope = r.depth[c, row * MAP_COLS : (row + 1) * MAP_COLS, :]
            value = r.grad_pre[c, at, :] + shift * slope
            r.grad_pre[c, at, :] = value.astype(BF16).astype(F32)
        rows = [
            beside(r.pre_rows_in[n, c], r.slope_rows_in[n, c], ok)
            for n, ok in enumerate((up_ok, down_ok))
        ]
        r.grad_pre[c, 8:72, :] = rows[0]
        r.grad_pre[c, last + 8 : last + 72, :] = rows[1]
        for n, (col, ok) in enumerate(((7, left_ok), (72, right_ok))):
            r.grad_pre[c, pl.ds(PAD + col, MAP_ROWS, stride=PAD), :] = beside(
                r.pre_cols_in[n, c], r.slope_cols_in[n, c], ok
            )

    corners = (
        (7, up_ok * left_ok),
        (72, up_ok * right_ok),
        (last + 7, down_ok * left_ok),
        (last + 72, down_ok * right_ok),
    )
    shifts = jnp.concatenate(
        [r.gate_back[:, c * 128 : (c + 1) * 128] for c in range(LANES)], axis=0
    )
    for corner, (at, ok) in enumerate(corners):
        slope = r.slope_corners_in[corner].astype(F32)[:8]
        cells = r.pre_corners_in[corner].astype(F32)[:8] + shifts * slope
        cells = cells * ok
        for c in range(LANES):
            r.grad_pre[c, at : at + 1, :] = cells[c : c + 1]

    bias_sum.back_q()

    r.tap_acc[...] = jnp.zeros_like(r.tap_acc)

    def depth_back(c):
        taps = taps_of(c)

        @pl.loop(0, MAP_ROWS // 2)
        def _(n):
            sums = [None] * 2
            inner = [
                r.spread[c, pl.ds(pad_row(1 + n * 2 + i, 8), MAP_COLS), :] for i in range(2)
            ]
            for b in range(3):
                parts = [None] * 3
                for row in range(4):
                    view = r.grad_pre.at[c, pl.ds(pad_row(n * 2 + row), PAD)]
                    v = view[pl.ds(7 + b, MAP_COLS), :]
                    for a in range(3):
                        i = row - a
                        if 0 <= i < 2:
                            term = v * taps[(2 - a) * 3 + 2 - b]
                            sums[i] = term if sums[i] is None else sums[i] + term
                            part = fold(v * inner[i])
                            parts[a] = part if parts[a] is None else parts[a] + part
                for a in range(3):
                    r.tap_acc[c, (2 - a) * 3 + 2 - b] += parts[a]
            for i in range(2):
                at = aligned((n * 2 + i) * MAP_COLS, MAP_COLS, MAP_COLS)
                r.grad_exp[c, at, :] = (sums[i] * r.expanded[c, at, :]).astype(BF16)

    pair_sum.end()
    project_sum.end()
    early = Gather(me, links, r.sum_early, r.grid_dy)
    for n, slots in enumerate((r.pair_slots, r.project_slots)):
        total = jnp.sum(slots[...].astype(F32), axis=0).astype(BF16)
        early.piece[:, n * 128 : (n + 1) * 128] = total

    @pl.loop(0, LANES)
    def _(c):
        depth_back(c)
        row = lax.rem(me.row + c, ROWS)
        for k in range(1, 8):
            early.send(row, k)

        @pl.when(c > 0)
        def _():
            early.send(row, 0)

    for c in range(4):
        lane = slice(c * 256, (c + 1) * 256)
        product = nn(r.normed_t[...], lanes_of(r.grad_exp, 2 * c, slice(None)))
        r.expand_x[:, lane] = product.astype(BF16)
    expand_sum = big("expand")
    expand_sum.start()
    for c in range(LANES):
        rows = [jnp.sum(r.tap_acc[c, k], axis=0, keepdims=True) for k in range(9)]
        r.taps_sum_x[c * 8 : c * 8 + 8, :128] = jnp.concatenate(rows[:8], axis=0)
        rows = [rows[8], jnp.zeros((7, 128), F32)]
        r.taps_sum_x[c * 8 : c * 8 + 8, 128:] = jnp.concatenate(rows, axis=0)
    parts = ["x", "pair", "summed", "a", "b"]
    taps_sum = SmallSum(
        me, links, *[getattr(r, "taps_sum_" + p) for p in parts], r.sum_taps
    )
    taps_sum.start()
    expand_sum.scatter()
    taps_sum.to_q()

    @pl.loop(0, 4)
    def _(t):
        grad = None
        for c in range(4):
            lane = slice(c * 256, (c + 1) * 256)
            part = nt(lanes_of(r.grad_exp, 2 * c, cell_rows(t)), r.w_expand[:, lane])
            grad = part if grad is None else grad + part
        unit, rstd = centre(r.image[map_rows(t)].reshape(TILE, CH).astype(F32))
        r.norm_acc[0] += fold(grad * unit)
        value = r.grad_mixed[cell_rows(t)] + norm_back(unit, rstd, grad * gain_first)
        r.grad_map[map_rows(t)] = value.astype(BF16).reshape(4, MAP_COLS, CH)

    flush("grad_map").start()
    att_back.end()

    @pl.loop(0, 4)
    def _(t):
        att = r.att_in[map_rows(t, 16)].reshape(TILE, CH)
        value = r.mixed[cell_rows(t)].astype(F32) + nn(att, r.w_out[...])
        r.out_map[map_rows(t)] = value.astype(BF16).reshape(4, MAP_COLS, CH)

    flush("out_map").start()
    rows = []
    for n in range(2):
        sums = jnp.sum(r.norm_acc[n], axis=0, keepdims=True)
        rows += [sums[:, :128], sums[:, 128:]]
    r.norms_x[...] = jnp.concatenate(rows + [jnp.zeros((4, 128), F32)], axis=0)
    norms_sum = TileSum(me, links, r.norms_x, r.norms_pair, r.norms_slots)
    norms_sum.start()
    bias_sum.end()
    flush("sum_bias").start()
    rows = [pooled, grad_logit, jnp.pad(hidden, ((0, 0), (0, 960)))]
    rows += [jnp.pad(grad_squeezed, ((0, 0), (0, 960))), jnp.zeros((4, 1024), F32)]
    r.gate_rows[...] = jnp.concatenate(rows, axis=0)
    flush("gate_rows").start()
    taps_sum.to_rows()
    expand_sum.end()
    final = Gather(me, links, r.sum_expand, r.expand_slots)
    final.piece[...] = jnp.sum(r.expand_slots[...].astype(F32), axis=0).astype(BF16)
    final.send_all()
    early.back_pair()
    taps_sum.back_q()
    early.end()
    flush("sum_early").start()
    r.sum_norms[...] = norms_sum.end()
    flush("sum_norms").start()
    taps_sum.end()
    flush("sum_taps").start()
    final.back_pair()
    final.end()
    flush("sum_expand").start()
    for name in OUTS:
        flush(name).wait()
    links.finish()


FINAL = dict(
    block_out=((MAP_ROWS, MAP_COLS, CH), BF16),
    grad_image=((MAP_ROWS, MAP_COLS, CH), BF16),
    grad_norm0=((1, CH), F32),
    grad_expand=((CH, 1024), F32),
    grad_depth=((3, 3, 1024), F32),
    grad_squeeze=((64, 1024), F32),
    grad_excite=((64, 1024), F32),
    grad_project=((1024, CH), F32),
    grad_norm1=((1, CH), F32),
    grad_qkv=((CH, 3 * CH), F32),
    grad_out_proj=((CH, CH), F32),
    grad_bias=((HEADS, MEMBERS, MEMBERS), F32),
)


def finish_kernel(*args):
    r = Refs()
    names = ["hbm_" + n for n in OUTS] + ["hbm_" + n for n in FINAL]
    names += list(OUTS) + list(FINAL)[2:] + ["in_sems", "out_sems"]
    for name, ref in zip(names, args, strict=True):
        setattr(r, name, ref)
    r.block_out, r.grad_image = r.out_map, r.grad_map

    def fetch(name):
        at = list(OUTS).index(name)
        return pltpu.make_async_copy(getattr(r, "hbm_" + name), getattr(r, name), r.in_sems.at[at])

    def flush(name):
        at = list(FINAL).index(name)
        return pltpu.make_async_copy(
            getattr(r, name), getattr(r, "hbm_" + name), r.out_sems.at[at]
        )

    order = ["sum_expand", "sum_early", "out_map", "grad_map"]
    order += ["sum_bias", "sum_taps", "sum_norms", "gate_rows"]
    for name in order:
        fetch(name).start()
    fetch("sum_expand").wait()
    r.grad_expand[...] = r.sum_expand[...].astype(F32)
    flush("grad_expand").start()
    fetch("sum_early").wait()
    for n in range(8):
        lane = slice(n * 128, (n + 1) * 128)
        part = r.sum_early[:, n * 256 : n * 256 + 128].astype(F32)
        if n < 6:
            r.grad_qkv[:, lane] = part
        else:
            r.grad_out_proj[:, (n - 6) * 128 : (n - 5) * 128] = part
    flush("grad_qkv").start()
    flush("grad_out_proj").start()
    for n in range(8):
        lane = slice(n * 128, (n + 1) * 128)
        r.grad_project[lane, :] = r.sum_early[:, n * 256 + 128 : n * 256 + 256].astype(F32).T
    flush("grad_project").start()
    fetch("out_map").wait()
    flush("block_out").start()
    fetch("grad_map").wait()
    flush("grad_image").start()
    for name in order[4:]:
        fetch(name).wait()
    for h in range(0, HEADS, 2):
        both = r.sum_bias[:, h * 64 : (h + 2) * 64].T
        r.grad_bias[h] = both[:64]
        r.grad_bias[h + 1] = both[64:]
    for k in range(9):
        if k < 8:
            rows = [r.sum_taps[c * 8 + k : c * 8 + k + 1, :128] for c in range(LANES)]
        else:
            rows = [r.sum_taps[c * 8 : c * 8 + 1, 128:] for c in range(LANES)]
        r.grad_depth[k // 3, k % 3 : k % 3 + 1, :] = jnp.concatenate(rows, axis=1)
    for n, out in enumerate((r.grad_norm0, r.grad_norm1)):
        rows = [r.sum_norms[n * 2 + c : n * 2 + c + 1, :] for c in range(2)]
        out[...] = jnp.concatenate(rows, axis=1)
    pooled, grad_logit = r.gate_rows[0:1, :], r.gate_rows[1:2, :]
    hidden, grad_squeezed = r.gate_rows[2:3, :64], r.gate_rows[3:4, :64]
    r.grad_excite[...] = outer(hidden, grad_logit)
    r.grad_squeeze[...] = outer(grad_squeezed, pooled)
    early = ["block_out", "grad_image", "grad_expand", "grad_qkv", "grad_out_proj", "grad_project"]
    for name in FINAL:
        if name not in early:
            flush(name).start()
    for name in FINAL:
        flush(name).wait()


def on_device(
    image,
    out_cotangent,
    norm0_gain,
    w_expand,
    w_depth,
    w_squeeze,
    w_excite,
    w_project,
    norm1_gain,
    w_qkv,
    w_out,
    attn_bias,
):
    vmem = pl.BlockSpec(memory_space=pltpu.VMEM)
    any_space = pl.BlockSpec(memory_space=pl.ANY)
    buffers = lambda shapes: [pltpu.VMEM(*shape) for shape in shapes.values()]
    made = pl.pallas_call(
        block_kernel,
        out_shape=[jax.ShapeDtypeStruct(*shape) for shape in OUTS.values()],
        in_specs=[vmem] * len(IN_NAMES) + [any_space] * len(LATE),
        out_specs=[any_space] * len(OUTS),
        scratch_shapes=buffers(LATE)
        + buffers(OUTS)
        + buffers(SCRATCH)
        + [pltpu.SemaphoreType.DMA((n,)) for n in (SEMS, len(LATE), len(OUTS))],
        compiler_params=pltpu.CompilerParams(
            collective_id=0, has_side_effects=True, vmem_limit_bytes=63 * 2**20
        ),
        name="block",
    )(
        image,
        norm0_gain,
        norm1_gain,
        w_depth,
        w_expand,
        out_cotangent.reshape(MEMBERS, GROUPS, CH),
        w_out,
        attn_bias,
        w_squeeze.T,
        w_excite,
        w_project,
        w_qkv,
    )
    final = pl.pallas_call(
        finish_kernel,
        out_shape=[jax.ShapeDtypeStruct(*shape) for shape in FINAL.values()],
        in_specs=[any_space] * len(OUTS),
        out_specs=[any_space] * len(FINAL),
        scratch_shapes=buffers(OUTS)
        + buffers(FINAL)[2:]
        + [pltpu.SemaphoreType.DMA((n,)) for n in (len(OUTS), len(FINAL))],
        compiler_params=pltpu.CompilerParams(vmem_limit_bytes=63 * 2**20),
        name="finish",
    )(*made)
    final = dict(zip(FINAL, final))
    final["grad_norm0"] = final["grad_norm0"].reshape(CH)
    final["grad_norm1"] = final["grad_norm1"].reshape(CH)
    final["grad_squeeze"] = final["grad_squeeze"].T
    return tuple(final.values())


def solution(mesh):
    mapped = P("row", "col", None)
    return jax.shard_map(
        on_device,
        mesh=mesh,
        in_specs=(mapped, mapped) + (P(),) * 10,
        out_specs=(mapped, mapped) + (P(),) * 10,
        check_vma=False,
    )
```

```python
import functools

import jax
import jax.numpy as jnp
from jax import lax
from jax.experimental import pallas as pl
from jax.experimental.pallas import tpu as pltpu
from jax.sharding import PartitionSpec as P

F32 = jnp.float32
BF16 = jnp.bfloat16
MESH = pl.DeviceIdType.MESH
ROWS = 8
COLS = 16
CHIPS = 64
HEADS = 8
MEMBERS = 64
GROUPS = 16
CH = 256
MAP_ROWS = 16
MAP_COLS = 64
CELLS = MAP_ROWS * MAP_COLS
CELLS_TOTAL = 131072
LANES = 8
PAD = 80
PADDED = (MAP_ROWS + 2) * PAD
TILE = 256
SCALE = 32 ** (-0.5)
GELU_A = 0.7978845608028654
GELU_B = 0.044715


def nn(a, b):
    return jnp.dot(a, b, preferred_element_type=F32)


def nt(a, b):
    return lax.dot_general(a, b, (((1,), (1,)), ((), ())), preferred_element_type=F32)


def tn(a, b):
    return lax.dot_general(a, b, (((0,), (0,)), ((), ())), preferred_element_type=F32)


def gelu(x):
    return 0.5 * x * (1.0 + jnp.tanh(GELU_A * (x + GELU_B * (x * x * x))))


def gelu_slope(x):
    square = x * x
    t = jnp.tanh(GELU_A * (x + GELU_B * (square * x)))
    return 0.5 * (1.0 + t) + (0.5 * GELU_A) * x * (1.0 - t * t) * (1.0 + (3 * GELU_B) * square)


def centre(x):
    centered = x - jnp.mean(x, axis=-1, keepdims=True)
    rstd = lax.rsqrt(jnp.mean(centered * centered, axis=-1, keepdims=True) + 1e-05)
    return centered * rstd, rstd


def norm_back(unit, rstd, grad_unit):
    first = jnp.mean(grad_unit, axis=-1, keepdims=True)
    second = jnp.mean(grad_unit * unit, axis=-1, keepdims=True)
    return rstd * (grad_unit - first - unit * second)


def fold(x):
    return jnp.sum(x.reshape(x.shape[0] // 8, 8, x.shape[1]), axis=0)


def thirds(x):
    one = x.astype(BF16).astype(F32)
    two = (x - one).astype(BF16).astype(F32)
    three = (x - one - two).astype(BF16).astype(F32)
    return one, two, three


def stack_rows(rows):
    width = rows[0].shape[1]
    rows = list(rows) + [jnp.zeros((8 - len(rows), width), F32)]
    return jnp.concatenate(rows, axis=0).astype(BF16)


def wide_product(x, w, product):
    return jnp.sum(product(stack_rows(thirds(x)), w), axis=0, keepdims=True)


def outer(a, b):
    a1, a2, a3 = thirds(a)
    b1, b2, b3 = thirds(b)
    return tn(stack_rows([a1, a1, a2, a2, a1, a3]), stack_rows([b1, b2, b1, b2, b3, b1]))


def aligned(start, size, unit=8):
    return pl.ds(pl.multiple_of(start, unit), size)


class Place:
    def __init__(self):
        self.row = lax.axis_index("row")
        self.col = lax.axis_index("col")
        self.core = lax.rem(self.col, 2)
        self.q = lax.div(self.col, 2)
        self.chip = self.row * 8 + self.q
        self.qs = [lax.rem(self.q + k, 8) for k in range(8)]
        self.cols = [q * 2 + self.core for q in self.qs]

    def partner(self):
        return (self.row, self.q * 2 + 1 - self.core)

    def q_peer(self, k):
        return self.qs[k], (self.row, self.cols[k])

    def row_peer(self, k):
        row = lax.rem(self.row + k, ROWS)
        return row, (row, self.col)

    def beside(self, up, right):
        return (lax.rem(self.row + ROWS + up, ROWS), lax.rem(self.col + COLS + right, COLS))

    def every_peer(self, body):
        def others(k, carry):
            row = lax.rem(self.row + k, ROWS)
            for n in range(1, 8):
                body(row, self.qs[n], (row, self.cols[n]))
            return carry

        def same(k, carry):
            row = lax.rem(self.row + k, ROWS)
            body(row, self.q, (row, self.col))
            return carry

        lax.fori_loop(0, ROWS, others, 0)
        lax.fori_loop(1, ROWS, same, 0)


class Links:
    def __init__(self, sems):
        self.sems = sems
        self.used = 0
        self.sent = []

    def pair(self):
        at = self.used
        self.used += 2
        return self.sems.at[at], self.sems.at[at + 1]

    def finish(self):
        for sem, buf in self.sent:
            pltpu.make_async_copy(buf, buf, sem).wait()


def push(src, dst, send, recv, device):
    pltpu.make_async_remote_copy(
        src_ref=src,
        dst_ref=dst,
        send_sem=send,
        recv_sem=recv,
        device_id=device,
        device_id_type=MESH,
    ).start()


def arrived(buf, sem):
    pltpu.make_async_copy(buf, buf, sem).wait()


class TileSum:
    def __init__(self, me, links, x, pair_slot, slots):
        self.me, self.links = me, links
        self.x, self.pair_slot, self.slots = x, pair_slot, slots
        self.s0, self.s1 = links.pair(), links.pair()

    def start(self):
        push(self.x, self.pair_slot, *self.s0, self.me.partner())
        self.links.sent.append((self.s0[0], self.x))
        arrived(self.pair_slot, self.s0[1])
        self.slots[self.me.chip] = self.x[...] + self.pair_slot[...]
        mine = self.slots.at[self.me.chip]
        self.me.every_peer(lambda row, q, device: push(mine, mine, *self.s1, device))
        self.links.sent.append((self.s1[0], self.slots.at[pl.ds(0, CHIPS - 1)]))

    def end(self):
        arrived(self.slots.at[pl.ds(0, CHIPS - 1)], self.s1[1])
        return jnp.sum(self.slots[...], axis=0)


class Scatter:
    def __init__(self, me, links, x, pair_in, summed, slots):
        self.me, self.links = me, links
        self.x, self.pair_in, self.summed, self.slots = x, pair_in, summed, slots
        self.sems = [links.pair() for _ in range(2)]

    def half_of(self, core):
        return self.x.at[aligned(core * 128, 128, 128)]

    def piece(self, row, q):
        return self.summed.at[aligned(row * 16, 16, 16), aligned(q * 128, 128, 128)]

    def start(self):
        push(self.half_of(1 - self.me.core), self.pair_in, *self.sems[0], self.me.partner())
        self.links.sent.append((self.sems[0][0], self.pair_in))

    def scatter(self):
        me = self.me
        arrived(self.pair_in, self.sems[0][1])
        mine = self.half_of(me.core)
        self.summed[...] = (mine[...].astype(F32) + self.pair_in[...].astype(F32)).astype(BF16)
        to = self.slots.at[me.chip]
        me.every_peer(
            lambda row, q, device: push(self.piece(row, q), to, *self.sems[1], device)
        )
        self.slots[me.chip] = self.piece(me.row, me.q)[...]

    def end(self):
        arrived(self.slots.at[pl.ds(0, CHIPS - 1)], self.sems[1][1])
        self.links.sent.append((self.sems[1][0], self.slots.at[pl.ds(0, CHIPS - 1)]))


class HalvesScatter(Scatter):
    def __init__(self, *args):
        super().__init__(*args)
        self.pairs = [self.sems[0], self.links.pair()]

    def start(self, n):
        lane = pl.ds(n * 512, 512)
        other = aligned((1 - self.me.core) * 128, 128, 128)
        to = self.pair_in.at[:, lane]
        push(self.x.at[other, lane], to, *self.pairs[n], self.me.partner())
        self.links.sent.append((self.pairs[n][0], to))

    def scatter(self):
        me = self.me
        mine = aligned(me.core * 128, 128, 128)
        for n in range(2):
            lane = pl.ds(n * 512, 512)
            arrived(self.pair_in.at[:, lane], self.pairs[n][1])
            total = self.x[mine, lane].astype(F32) + self.pair_in[:, lane].astype(F32)
            self.summed[:, lane] = total.astype(BF16)
        to = self.slots.at[me.chip]
        me.every_peer(
            lambda row, q, device: push(self.piece(row, q), to, *self.sems[1], device)
        )
        self.slots[me.chip] = self.piece(me.row, me.q)[...]


class Gather:
    def __init__(self, me, links, out, like):
        self.me, self.links, self.out, self.like = me, links, out, like
        self.width = out.shape[1] // 8
        self.sems = [links.pair() for _ in range(2)]
        lane = aligned(me.q * self.width, self.width, 128)
        self.piece = out.at[aligned(me.core * 128 + me.row * 16, 16, 16), lane]

    def send(self, row, k):
        push(self.piece, self.piece, *self.sems[0], (row, self.me.cols[k]))

    def send_all(self):
        self.me.every_peer(
            lambda row, q, device: push(self.piece, self.piece, *self.sems[0], device)
        )

    def back_pair(self):
        me = self.me
        arrived(self.like.at[pl.ds(0, CHIPS - 1)], self.sems[0][1])
        self.links.sent.append((self.sems[0][0], self.like.at[pl.ds(0, CHIPS - 1)]))
        half = self.out.at[aligned(me.core * 128, 128, 128)]
        push(half, half, *self.sems[1], me.partner())
        self.links.sent.append((self.sems[1][0], half))

    def end(self):
        arrived(self.out.at[pl.ds(0, 128)], self.sems[1][1])


class SmallSum:
    def __init__(self, me, links, x, pair_in, summed, slots_a, slots_b, out):
        self.me, self.links = me, links
        self.x, self.pair_in, self.summed, self.out = x, pair_in, summed, out
        self.slots_a, self.slots_b = slots_a, slots_b
        self.sems = [links.pair() for _ in range(4)]

    def start(self):
        push(self.x, self.pair_in, *self.sems[0], self.me.partner())
        self.links.sent.append((self.sems[0][0], self.pair_in))

    def to_q(self):
        arrived(self.pair_in, self.sems[0][1])
        self.summed[...] = self.x[...] + self.pair_in[...]
        for k in range(1, 8):
            q, device = self.me.q_peer(k)
            piece = self.summed.at[aligned(q * 8, 8)]
            push(piece, self.slots_a.at[self.me.q], *self.sems[1], device)
        self.links.sent.append((self.sems[1][0], self.slots_a.at[pl.ds(0, 7)]))

    def to_rows(self):
        me = self.me
        self.slots_a[me.q] = self.summed[aligned(me.q * 8, 8)]
        arrived(self.slots_a.at[pl.ds(0, 7)], self.sems[1][1])
        self.slots_b[me.row] = jnp.sum(self.slots_a[...], axis=0)
        for k in range(1, 8):
            _, device = me.row_peer(k)
            piece = self.slots_b.at[me.row]
            push(piece, piece, *self.sems[2], device)
        self.links.sent.append((self.sems[2][0], self.slots_b.at[pl.ds(0, 7)]))

    def back_q(self):
        me = self.me
        arrived(self.slots_b.at[pl.ds(0, 7)], self.sems[2][1])
        piece = self.out.at[aligned(me.q * 8, 8)]
        piece[...] = jnp.sum(self.slots_b[...], axis=0)
        for k in range(1, 8):
            _, device = me.q_peer(k)
            push(piece, piece, *self.sems[3], device)
        self.links.sent.append((self.sems[3][0], self.slots_a.at[pl.ds(0, 7)]))

    def end(self):
        arrived(self.slots_a.at[pl.ds(0, 7)], self.sems[3][1])


class Exchange:
    def __init__(self, me, links, src, dst):
        self.me, self.links, self.src, self.dst = me, links, src, dst
        self.sems = links.pair()

    def send(self, row, k):
        q, col = self.me.qs[k], self.me.cols[k]
        push(self.src.at[row * 8 + q], self.dst.at[self.me.chip], *self.sems, (row, col))

    def send_row(self, row):
        for k in range(1, 8):
            self.send(row, k)

        @pl.when(row != self.me.row)
        def _():
            self.send(row, 0)

    def send_tile(self, t):
        for k in range(2):
            self.send_row(t * 2 + lax.rem(self.me.row + k, 2))

    def end(self):
        self.dst[self.me.chip] = self.src[self.me.chip]
        arrived(self.dst.at[pl.ds(0, CHIPS - 1)], self.sems[1])
        self.links.sent.append((self.sems[0], self.dst.at[pl.ds(0, CHIPS - 1)]))


class Halo:
    def __init__(
        self, me, links, rows_out, cols_out, corners_out, rows_in, cols_in, corners_in
    ):
        self.me, self.links = me, links
        self.rows_out, self.cols_out, self.corners_out = rows_out, cols_out, corners_out
        self.rows_in, self.cols_in, self.corners_in = rows_in, cols_in, corners_in
        self.sems = [links.pair() for _ in range(3)]

    def start(self):
        me = self.me
        for side, up in ((0, -1), (1, 1)):
            push(
                self.rows_out[side],
                self.rows_in.at[1 - side],
                *self.sems[0],
                me.beside(up, 0),
            )
        for side, right in ((0, -1), (1, 1)):
            strip = self.cols_out.at[side]
            push(strip, self.cols_in.at[1 - side], *self.sems[1], me.beside(0, right))
            for end, up in ((0, -1), (1, 1)):
                push(
                    self.corners_out[end * 2 + side],
                    self.corners_in.at[(1 - end) * 2 + 1 - side],
                    *self.sems[2],
                    me.beside(up, right),
                )

    def end(self):
        for n, buf in enumerate((self.rows_in, self.cols_in, self.corners_in)):
            arrived(buf, self.sems[n][1])
            self.links.sent.append((self.sems[n][0], buf))


IN_NAMES = ["norm0_gain", "norm1_gain", "w_depth"]
LATE = dict(
    image=((MAP_ROWS, MAP_COLS, CH), BF16),
    w_expand=((CH, 1024), BF16),
    dy=((MEMBERS, GROUPS, CH), BF16),
    w_out=((CH, CH), BF16),
    bias=((HEADS, MEMBERS, MEMBERS), F32),
    w_squeeze_t=((64, 1024), BF16),
    w_excite=((64, 1024), BF16),
    w_project=((1024, CH), BF16),
    w_qkv=((CH, 768), BF16),
)
OUTS = dict(
    out_map=((MAP_ROWS, MAP_COLS, CH), BF16),
    grad_map=((MAP_ROWS, MAP_COLS, CH), BF16),
    sum_expand=((CH, 1024), BF16),
    sum_early=((CH, 2048), BF16),
    sum_bias=((MEMBERS, 512), F32),
    sum_taps=((64, 256), F32),
    sum_norms=((8, 128), F32),
    gate_rows=((8, 1024), F32),
)


def big_scratch(name):
    return {
        name + "_x": ((CH, 1024), BF16),
        name + "_pair": ((CH // 2, 1024), BF16),
        name + "_summed": ((CH // 2, 1024), BF16),
    }


def small_scratch(name, width):
    return {
        name + "_x": ((64, width), F32),
        name + "_pair": ((64, width), F32),
        name + "_summed": ((64, width), F32),
        name + "_a": ((8, 8, width), F32),
        name + "_b": ((8, 8, width), F32),
    }


def tile_scratch(name):
    return {
        name + "_x": ((8, 128), F32),
        name + "_pair": ((8, 128), F32),
        name + "_slots": ((CHIPS, 8, 128), F32),
    }


SCRATCH = dict(
    taps=((16, 1024), F32),
    normed=((CELLS, CH), BF16),
    normed_t=((CH, CELLS), BF16),
    spread=((LANES, PADDED, 128), F32),
    expanded=((LANES, CELLS, 128), F32),
    depth=((LANES, CELLS, 128), F32),
    act=((LANES, CELLS, 128), BF16),
    pool_acc=((LANES, 8, 128), F32),
    edge_cols=((2, 16, CH), BF16),
    edge_rows_in=((2, MAP_COLS, CH), BF16),
    edge_cols_in=((2, 16, CH), BF16),
    edge_corners_in=((4, 16, CH), BF16),
    gate=((1, 1024), F32),
    gate_back=((1, 1024), F32),
    mixed=((CELLS, CH), BF16),
    normed_two=((MEMBERS, GROUPS, CH), BF16),
    grid_x=((MEMBERS, GROUPS, CH), BF16),
    grid_dy=((MEMBERS, GROUPS, CH), BF16),
    qkv=((6, CELLS, 128), F32),
    grid_g=((2, CELLS, 128), F32),
    att_rows=((2, CELLS, 128), F32),
    packed_back=((6, CELLS, 128), F32),
    probs=((GROUPS, MEMBERS, 512), F32),
    bias_t=((MEMBERS, 512), F32),
    att_out=((MEMBERS, GROUPS, CH), BF16),
    att_in=((MEMBERS, GROUPS, CH), BF16),
    gn_out=((MEMBERS, GROUPS, CH), BF16),
    gn_in=((MEMBERS, GROUPS, CH), BF16),
    grad_mixed=((CELLS, CH), F32),
    grad_mixed_b=((CELLS, CH), BF16),
    grad_gated=((LANES, CELLS, 128), F32),
    gate_acc=((LANES, 8, 128), F32),
    grad_pre=((LANES, PADDED, 128), F32),
    slope_rows=((2, LANES, MAP_COLS, 128), BF16),
    slope_cols=((2, LANES, 16, 128), BF16),
    slope_corners=((4, 16, 128), BF16),
    slope_rows_in=((2, LANES, MAP_COLS, 128), BF16),
    slope_cols_in=((2, LANES, 16, 128), BF16),
    slope_corners_in=((4, 16, 128), BF16),
    pre_rows=((2, LANES, MAP_COLS, 128), BF16),
    pre_cols=((2, LANES, 16, 128), BF16),
    pre_rows_in=((2, LANES, MAP_COLS, 128), BF16),
    pre_cols_in=((2, LANES, 16, 128), BF16),
    pre_corners=((4, 16, 128), BF16),
    pre_corners_in=((4, 16, 128), BF16),
    tap_acc=((LANES, 9, 8, 128), F32),
    grad_exp=((LANES, CELLS, 128), BF16),
    norm_acc=((2, 8, CH), F32),
    pair_acc=((CH, 1024), F32),
    **tile_scratch("pool"),
    **tile_scratch("gateg"),
    **big_scratch("expand"),
    **big_scratch("project"),
    **big_scratch("pair"),
    expand_slots=((CHIPS, 16, 128), BF16),
    pair_slots=((CHIPS, 16, 128), BF16),
    project_slots=((CHIPS, 16, 128), BF16),
    **small_scratch("bias", 512),
    **small_scratch("taps_sum", 256),
    **tile_scratch("norms"),
)
SEMS = 96


class Refs:
    pass


def lanes_of(ref, first, at):
    return jnp.concatenate([ref[first, at, :], ref[first + 1, at, :]], axis=1)


def map_rows(t, count=4):
    return pl.ds(t * count, count)


def cell_rows(t):
    return aligned(t * TILE, TILE, TILE)


def pad_row(row, col=0):
    return pl.multiple_of(row * PAD + col, 8)


def block_kernel(*args):
    r = Refs()
    names = IN_NAMES + ["hbm_" + n for n in LATE] + ["hbm_" + n for n in OUTS]
    names += list(LATE) + list(OUTS) + list(SCRATCH) + ["sems", "late_sems", "out_sems"]
    for name, ref in zip(names, args, strict=True):
        setattr(r, name, ref)
    me = Place()
    links = Links(r.sems)

    def late(name):
        at = list(LATE).index(name)
        return pltpu.make_async_copy(
            getattr(r, "hbm_" + name), getattr(r, name), r.late_sems.at[at]
        )

    def flush(name):
        at = list(OUTS).index(name)
        return pltpu.make_async_copy(
            getattr(r, name), getattr(r, "hbm_" + name), r.out_sems.at[at]
        )

    for name in LATE:
        late(name).start()
    off = r.image.shape[0] - 1

    barrier = pltpu.get_barrier_semaphore()

    def greet(row, q, device):
        pl.semaphore_signal(barrier, inc=1, device_id=device, device_id_type=MESH)

    me.every_peer(greet)
    for up in (-1, 0, 1):
        for right in (-1, 1):
            pl.semaphore_signal(
                barrier, inc=1, device_id=me.beside(up, right), device_id_type=MESH
            )

    gain_first = r.norm0_gain[...].astype(F32).reshape(1, CH)
    gain_second = r.norm1_gain[...].astype(F32).reshape(1, CH)
    for a in range(3):
        r.taps[a * 3 : a * 3 + 3, :] = r.w_depth[a].astype(F32)

    late("image").wait()
    for side, col in ((0, 0), (1, MAP_COLS - 16)):
        rows = []
        for i in range(MAP_ROWS):
            part = r.image[i, col : col + 16, :].astype(F32)
            rows.append(part[0:1] if side == 0 else part[15:16])
        r.edge_cols[side] = jnp.concatenate(rows, axis=0).astype(BF16)

    @pl.loop(0, 4, unroll=4)
    def _(t):
        x = r.image[map_rows(t)].reshape(TILE, CH).astype(F32)
        unit, _ = centre(x)
        r.normed[cell_rows(t)] = (unit * gain_first).astype(BF16)

    late("w_expand").wait()

    @pl.loop(0, 4)
    def _(t):
        for c in range(4):
            e = nn(r.normed[cell_rows(t)], r.w_expand[:, c * 256 : (c + 1) * 256])
            s = gelu(e).astype(BF16).astype(F32)
            for h in range(2):
                lane = slice(h * 128, (h + 1) * 128)
                r.expanded[2 * c + h, cell_rows(t), :] = e[:, lane]
                for a in range(4):
                    at = pl.ds(pad_row(1 + t * 4 + a, 8), MAP_COLS)
                    r.spread[2 * c + h, at, :] = s[a * 64 : (a + 1) * 64, lane]

    pl.semaphore_wait(barrier, CHIPS + 5)
    halo = Halo(
        me,
        links,
        (r.image.at[0], r.image.at[off]),
        r.edge_cols,
        [r.edge_cols.at[side] for side in (0, 1, 0, 1)],
        r.edge_rows_in,
        r.edge_cols_in,
        r.edge_corners_in,
    )
    halo.start()
    late("dy").wait()
    dy_out = Exchange(me, links, r.dy, r.grid_dy)

    @pl.loop(0, LANES)
    def _(c):
        row = lax.rem(me.row + c, ROWS)
        for t in range(4):
            for k in (2 * t + 1, 2 * t):
                if k:
                    dy_out.send(row, k)
            at = pl.ds(t * TILE, TILE)
            r.expanded[c, at, :] = gelu_slope(r.expanded[c, at, :])

        @pl.when(c > 0)
        def _():
            dy_out.send(row, 0)

    halo.end()

    up_ok = (me.row > 0).astype(F32)
    down_ok = (me.row < ROWS - 1).astype(F32)
    left_ok = (me.col > 0).astype(F32)
    right_ok = (me.col < COLS - 1).astype(F32)
    around = jnp.concatenate(
        [
            r.edge_rows_in[0].astype(F32) * up_ok,
            r.edge_rows_in[1].astype(F32) * down_ok,
            r.edge_cols_in[0].astype(F32) * left_ok,
            r.edge_cols_in[1].astype(F32) * right_ok,
            r.edge_corners_in[0].astype(F32)[8:16] * (up_ok * left_ok),
            r.edge_corners_in[1].astype(F32)[8:16] * (up_ok * right_ok),
            r.edge_corners_in[2].astype(F32)[0:8] * (down_ok * left_ok),
            r.edge_corners_in[3].astype(F32)[0:8] * (down_ok * right_ok),
        ],
        axis=0,
    )
    unit, _ = centre(around)
    around_normed = (unit * gain_first).astype(BF16)
    last = (MAP_ROWS + 1) * PAD
    for c in range(4):
        s = gelu(nn(around_normed, r.w_expand[:, c * 256 : (c + 1) * 256]))
        s = s.astype(BF16).astype(F32)
        for h in range(2):
            v = s[:, h * 128 : (h + 1) * 128]
            n = 2 * c + h
            r.spread[n, 8:72, :] = v[0:64]
            r.spread[n, last + 8 : last + 72, :] = v[64:128]
            r.spread[n, pl.ds(PAD + 7, MAP_ROWS, stride=PAD), :] = v[128:144]
            r.spread[n, pl.ds(PAD + 72, MAP_ROWS, stride=PAD), :] = v[144:160]
            r.spread[n, 7:8, :] = v[167:168]
            r.spread[n, 72:73, :] = v[175:176]
            r.spread[n, last + 7 : last + 8, :] = v[176:177]
            r.spread[n, last + 72 : last + 73, :] = v[184:185]

    def taps_of(c):
        lane = aligned(c * 128, 128, 128)
        return [r.taps[k : k + 1, lane] for k in range(9)]

    @pl.loop(0, LANES)
    def _(c):
        taps = taps_of(c)

        def block(n, total):
            sums = [None] * 4
            for row in range(6):
                view = r.spread.at[c, pl.ds(pad_row(n * 4 + row), PAD)]
                for b in range(3):
                    v = view[pl.ds(7 + b, MAP_COLS), :]
                    for a in range(3):
                        i = row - a
                        if 0 <= i < 4:
                            term = v * taps[a * 3 + b]
                            sums[i] = term if sums[i] is None else sums[i] + term
            for i in range(4):
                at = aligned((n * 4 + i) * MAP_COLS, MAP_COLS, MAP_COLS)
                r.depth[c, at, :] = sums[i]
                value = gelu(sums[i])
                r.act[c, at, :] = value.astype(BF16)
                total = total + fold(value)
            return total

        total = lax.fori_loop(0, 4, block, jnp.zeros((8, 128), F32), unroll=2)
        r.pool_x[pl.ds(c, 1), :] = jnp.sum(total, axis=0, keepdims=True)

    pool = TileSum(me, links, r.pool_x, r.pool_pair, r.pool_slots)
    pool.start()

    @pl.loop(0, LANES * 4)
    def _(n):
        c, t = lax.div(n, 4), lax.rem(n, 4)
        r.depth[c, cell_rows(t), :] = gelu_slope(r.depth[c, cell_rows(t), :])

    dy_out.end()
    late("w_out").wait()
    late("bias").wait()

    @pl.loop(0, 4)
    def _(t):
        dy = r.grid_dy[map_rows(t, 16)].reshape(TILE, CH)
        g = nt(dy, r.w_out[...])
        for n in range(2):
            r.grid_g[n, cell_rows(t), :] = g[:, n * 128 : (n + 1) * 128]

    for h in range(0, HEADS, 2):
        both = jnp.concatenate([r.bias[h], r.bias[h + 1]], axis=0)
        r.bias_t[:, h * 64 : (h + 2) * 64] = both.T
    for t in range(4):
        r.normed_t[:, t * TILE : (t + 1) * TILE] = r.normed[t * TILE : (t + 1) * TILE].T

    def flat(tile):
        return jnp.concatenate([tile[n : n + 1] for n in range(8)], axis=1)

    pooled = flat(pool.end()) * (1.0 / CELLS_TOTAL)
    for name in ("w_squeeze_t", "w_excite", "w_project", "w_qkv"):
        late(name).wait()
    squeezed = wide_product(pooled, r.w_squeeze_t[...], nt)
    open_part = jax.nn.sigmoid(squeezed)
    hidden = squeezed * open_part
    gate = jax.nn.sigmoid(wide_product(hidden, r.w_excite[...], nn))
    r.gate[...] = gate

    grid_out = Exchange(me, links, r.normed_two, r.grid_x)
    start_tile = lax.div(me.row, 2)

    @pl.loop(0, 4, unroll=2)
    def _(step):
        t = lax.rem(start_tile + step, 4)
        total = r.image[map_rows(t)].reshape(TILE, CH).astype(F32)
        for c in range(4):
            lane = slice(c * 256, (c + 1) * 256)
            gated = lanes_of(r.act, 2 * c, cell_rows(t)).astype(F32) * r.gate[:, lane]
            total = total + nn(gated.astype(BF16), r.w_project[lane, :])
        mixed = total.astype(BF16)
        r.mixed[cell_rows(t)] = mixed
        unit, _ = centre(mixed.astype(F32))
        normed = (unit * gain_second).astype(BF16)
        r.normed_two[map_rows(t, 16)] = normed.reshape(16, GROUPS, CH)
        grid_out.send_tile(t)

    def pack_edges(ref, width, first, rows_out, cols_out, corners_out):
        final_row = first + (MAP_ROWS - 1) * width

        @pl.loop(0, LANES)
        def _(c):
            for side, at in ((0, first), (1, final_row)):
                rows_out[side, c] = ref[c, at : at + MAP_COLS, :].astype(BF16)
            for side, at in ((0, first), (1, first + MAP_COLS - 1)):
                cells = ref[c, pl.ds(at, MAP_ROWS, stride=width), :]
                cols_out[side, c] = cells.astype(BF16)

        ends = (first, first + MAP_COLS - 1, final_row, final_row + MAP_COLS - 1)
        for corner, at in enumerate(ends):
            cells = [ref[c, at : at + 1, :] for c in range(LANES)]
            cells.append(jnp.zeros((8, 128), F32))
            corners_out[corner] = jnp.concatenate(cells, axis=0).astype(BF16)

    def edge_halo(name):
        parts = ["rows", "cols", "corners", "rows_in", "cols_in", "corners_in"]
        rows, cols, corners, *arriving = [getattr(r, name + "_" + p) for p in parts]
        return Halo(
            me,
            links,
            (rows.at[0], rows.at[1]),
            cols,
            [corners.at[n] for n in range(4)],
            *arriving,
        )

    pack_edges(r.depth, MAP_COLS, 0, r.slope_rows, r.slope_cols, r.slope_corners)
    slope_halo = edge_halo("slope")
    slope_halo.start()
    grid_out.end()

    @pl.loop(0, 4, unroll=2)
    def _(t):
        x = r.grid_x[map_rows(t, 16)].reshape(TILE, CH)
        qkv = nn(x, r.w_qkv[...])
        for n in range(6):
            r.qkv[n, cell_rows(t), :] = qkv[:, n * 128 : (n + 1) * 128]

    head_of = lax.div(lax.broadcasted_iota(jnp.int32, (1, 128), 1), 32)
    masks_f = [(head_of == h).astype(F32) for h in range(4)]
    masks = [m.astype(BF16) for m in masks_f]
    unroll = 8

    def spread_heads(a):
        return jnp.concatenate([a * m for m in masks], axis=0)

    def own_heads(v):
        total = v[0:MEMBERS] * masks_f[0]
        for h in range(1, 4):
            total = total + v[h * MEMBERS : (h + 1) * MEMBERS] * masks_f[h]
        return total

    def put(ref, n, at, value):
        ref[n, at, :] = value.astype(BF16).astype(F32)

    def group_forward(group):
        at = pl.ds(group, MEMBERS, stride=GROUPS)
        for n in range(2):
            q, k, v = [r.qkv[part * 2 + n, at, :].astype(BF16) for part in range(3)]
            lanes = slice(n * 256, (n + 1) * 256)
            scores = nt(k, spread_heads(q)) * SCALE + r.bias_t[:, lanes]
            lifted = jnp.exp(scores - jnp.max(scores, axis=0, keepdims=True))
            probs = lifted * (1.0 / jnp.sum(lifted, axis=0, keepdims=True))
            r.probs[group, :, lanes] = probs
            put(r.att_rows, n, at, own_heads(tn(probs.astype(BF16), v)))

    def group_back(group):
        at = pl.ds(group, MEMBERS, stride=GROUPS)
        bias_parts = []
        for n in range(2):
            q, k, v = [r.qkv[part * 2 + n, at, :].astype(BF16) for part in range(3)]
            lanes = slice(n * 256, (n + 1) * 256)
            q_heads = spread_heads(q)
            g_heads = spread_heads(r.grid_g[n, at, :].astype(BF16))
            probs = r.probs[group, :, lanes]
            put(r.packed_back, 4 + n, at, nn(probs.astype(BF16), g_heads))
            grad_probs = nt(v, g_heads)
            grad_scores = probs * (
                grad_probs - jnp.sum(grad_probs * probs, axis=0, keepdims=True)
            )
            bias_parts.append(grad_scores)
            scaled = (grad_scores * SCALE).astype(BF16)
            put(r.packed_back, n, at, own_heads(tn(scaled, k)))
            put(r.packed_back, 2 + n, at, nn(scaled, q_heads))
        return bias_parts

    @pl.loop(0, GROUPS // unroll)
    def _(step):
        for n in range(unroll):
            group_forward(step * unroll + n)

    @pl.loop(0, 4)
    def _(t):
        att = lanes_of(r.att_rows, 0, cell_rows(t)).astype(BF16)
        r.att_out[map_rows(t, 16)] = att.reshape(16, GROUPS, CH)

    att_back = Exchange(me, links, r.att_out, r.att_in)
    r.bias_x[...] = jnp.zeros_like(r.bias_x)

    @pl.loop(0, GROUPS // unroll)
    def _(step):
        for n in range(4):
            att_back.send_row(lax.rem(me.row + step * 4 + n, ROWS))
        total = group_back(step * unroll)
        for n in range(1, unroll):
            total = [a + b for a, b in zip(total, group_back(step * unroll + n))]
        for n in range(2):
            r.bias_x[:, n * 256 : (n + 1) * 256] += total[n]

    def packed_tile(t):
        parts = [r.packed_back[n, cell_rows(t), :] for n in range(6)]
        return jnp.concatenate(parts, axis=1).astype(BF16)

    gn_back = Exchange(me, links, r.gn_out, r.gn_in)

    @pl.loop(0, 4, unroll=2)
    def _(step):
        t = lax.rem(start_tile + step, 4)
        gn = nt(packed_tile(t), r.w_qkv[...]).astype(BF16)
        r.gn_out[map_rows(t, 16)] = gn.reshape(16, GROUPS, CH)
        gn_back.send_tile(t)

    bias_sum = SmallSum(
        me, links, r.bias_x, r.bias_pair, r.bias_summed, r.bias_a, r.bias_b, r.sum_bias
    )
    bias_sum.start()
    r.pair_acc[...] = jnp.zeros_like(r.pair_acc)

    @pl.loop(0, 4)
    def _(t):
        x = r.grid_x[map_rows(t, 16)].reshape(TILE, CH)
        dy = r.grid_dy[map_rows(t, 16)].reshape(TILE, CH)
        att = r.att_out[map_rows(t, 16)].reshape(TILE, CH)
        r.pair_acc[:, : 3 * CH] += tn(x, packed_tile(t))
        r.pair_acc[:, 3 * CH :] += tn(att, dy)

    r.pair_x[...] = r.pair_acc[...].astype(BF16)

    def big(name, kind=Scatter):
        parts = ["x", "pair", "summed", "slots"]
        return kind(me, links, *[getattr(r, name + "_" + p) for p in parts])

    pair_sum = big("pair")
    pair_sum.start()
    bias_sum.to_q()
    pair_sum.scatter()
    gn_back.end()

    r.norm_acc[...] = jnp.zeros_like(r.norm_acc)
    r.gate_acc[...] = jnp.zeros_like(r.gate_acc)

    @pl.loop(0, 4, unroll=2)
    def _(t):
        unit, rstd = centre(r.mixed[cell_rows(t)].astype(F32))
        gn = r.gn_in[map_rows(t, 16)].reshape(TILE, CH).astype(F32)
        r.norm_acc[1] += fold(gn * unit)
        dy = r.dy[map_rows(t, 16)].reshape(TILE, CH).astype(F32)
        grad = dy + norm_back(unit, rstd, gn * gain_second)
        r.grad_mixed[cell_rows(t)] = grad
        grad_b = grad.astype(BF16)
        r.grad_mixed_b[cell_rows(t)] = grad_b
        for c in range(4):
            gg = nt(grad_b, r.w_project[c * 256 : (c + 1) * 256, :])
            for h in range(2):
                n = 2 * c + h
                part = gg[:, h * 128 : (h + 1) * 128]
                r.grad_gated[n, cell_rows(t), :] = part
                r.gate_acc[n] += fold(part * r.act[n, cell_rows(t), :].astype(F32))

    for n in range(LANES):
        r.gateg_x[n : n + 1, :] = jnp.sum(r.gate_acc[n], axis=0, keepdims=True)
    gate_sum = TileSum(me, links, r.gateg_x, r.gateg_pair, r.gateg_slots)
    gate_sum.start()

    @pl.loop(0, LANES)
    def _(c):
        scale = r.gate[:, aligned(c * 128, 128, 128)]
        for t in range(4):
            at = slice(t * TILE, (t + 1) * TILE)
            g = r.grad_gated[c, at, :] * scale * r.depth[c, at, :]
            for a in range(4):
                first = (1 + t * 4 + a) * PAD + 8
                r.grad_pre[c, first : first + MAP_COLS, :] = g[a * 64 : (a + 1) * 64]

    pack_edges(r.grad_pre, PAD, PAD + 8, r.pre_rows, r.pre_cols, r.pre_corners)
    pre_halo = edge_halo("pre")
    pre_halo.start()
    grad_t = r.grad_mixed_b[...].T
    for c in range(4):
        lane = slice(c * 256, (c + 1) * 256)
        product = nn(grad_t, lanes_of(r.act, 2 * c, slice(None))) * r.gate[:, lane]
        r.project_x[:, lane] = product.astype(BF16)
    project_sum = big("project")
    project_sum.start()
    bias_sum.to_rows()
    project_sum.scatter()
    slope_halo.end()
    pre_halo.end()
    grad_gate = flat(gate_sum.end())
    grad_logit = grad_gate * gate * (1.0 - gate)
    grad_hidden = wide_product(grad_logit, r.w_excite[...], nt)
    grad_squeezed = grad_hidden * (open_part * (1.0 + squeezed * (1.0 - open_part)))
    r.gate_back[...] = wide_product(grad_squeezed, r.w_squeeze_t[...], nn) * (1.0 / CELLS_TOTAL)

    @pl.loop(0, LANES)
    def _(c):
        shift = r.gate_back[:, aligned(c * 128, 128, 128)]

        def beside(part, slope, ok):
            return (part.astype(F32) + shift * slope.astype(F32)) * ok

        for row in range(MAP_ROWS):
            first = (1 + row) * PAD + 8
            at = slice(first, first + MAP_COLS)
            slope = r.depth[c, row * MAP_COLS : (row + 1) * MAP_COLS, :]
            value = r.grad_pre[c, at, :] + shift * slope
            r.grad_pre[c, at, :] = value.astype(BF16).astype(F32)
        rows = [
            beside(r.pre_rows_in[n, c], r.slope_rows_in[n, c], ok)
            for n, ok in enumerate((up_ok, down_ok))
        ]
        r.grad_pre[c, 8:72, :] = rows[0]
        r.grad_pre[c, last + 8 : last + 72, :] = rows[1]
        for n, (col, ok) in enumerate(((7, left_ok), (72, right_ok))):
            r.grad_pre[c, pl.ds(PAD + col, MAP_ROWS, stride=PAD), :] = beside(
                r.pre_cols_in[n, c], r.slope_cols_in[n, c], ok
            )

    corners = (
        (7, up_ok * left_ok),
        (72, up_ok * right_ok),
        (last + 7, down_ok * left_ok),
        (last + 72, down_ok * right_ok),
    )
    shifts = jnp.concatenate(
        [r.gate_back[:, c * 128 : (c + 1) * 128] for c in range(LANES)], axis=0
    )
    for corner, (at, ok) in enumerate(corners):
        slope = r.slope_corners_in[corner].astype(F32)[:8]
        cells = r.pre_corners_in[corner].astype(F32)[:8] + shifts * slope
        cells = cells * ok
        for c in range(LANES):
            r.grad_pre[c, at : at + 1, :] = cells[c : c + 1]

    bias_sum.back_q()

    r.tap_acc[...] = jnp.zeros_like(r.tap_acc)

    def depth_back(c):
        taps = taps_of(c)

        @pl.loop(0, MAP_ROWS // 2, unroll=2)
        def _(n):
            sums = [None] * 2
            inner = [
                r.spread[c, pl.ds(pad_row(1 + n * 2 + i, 8), MAP_COLS), :] for i in range(2)
            ]
            for b in range(3):
                parts = [None] * 3
                for row in range(4):
                    view = r.grad_pre.at[c, pl.ds(pad_row(n * 2 + row), PAD)]
                    v = view[pl.ds(7 + b, MAP_COLS), :]
                    for a in range(3):
                        i = row - a
                        if 0 <= i < 2:
                            term = v * taps[(2 - a) * 3 + 2 - b]
                            sums[i] = term if sums[i] is None else sums[i] + term
                            part = fold(v * inner[i])
                            parts[a] = part if parts[a] is None else parts[a] + part
                for a in range(3):
                    r.tap_acc[c, (2 - a) * 3 + 2 - b] += parts[a]
            for i in range(2):
                at = aligned((n * 2 + i) * MAP_COLS, MAP_COLS, MAP_COLS)
                r.grad_exp[c, at, :] = (sums[i] * r.expanded[c, at, :]).astype(BF16)

    pair_sum.end()
    project_sum.end()
    early = Gather(me, links, r.sum_early, r.grid_dy)
    for n, slots in enumerate((r.pair_slots, r.project_slots)):
        total = jnp.sum(slots[...].astype(F32), axis=0).astype(BF16)
        early.piece[:, n * 128 : (n + 1) * 128] = total

    @pl.loop(0, LANES)
    def _(c):
        depth_back(c)
        row = lax.rem(me.row + c, ROWS)
        for k in range(1, 8):
            early.send(row, k)

        @pl.when(c > 0)
        def _():
            early.send(row, 0)

    expand_sum = big("expand", HalvesScatter)
    for c in range(4):
        lane = slice(c * 256, (c + 1) * 256)
        product = nn(r.normed_t[...], lanes_of(r.grad_exp, 2 * c, slice(None)))
        r.expand_x[:, lane] = product.astype(BF16)
        if c % 2:
            expand_sum.start(c // 2)
    for c in range(LANES):
        rows = [jnp.sum(r.tap_acc[c, k], axis=0, keepdims=True) for k in range(9)]
        r.taps_sum_x[c * 8 : c * 8 + 8, :128] = jnp.concatenate(rows[:8], axis=0)
        rows = [rows[8], jnp.zeros((7, 128), F32)]
        r.taps_sum_x[c * 8 : c * 8 + 8, 128:] = jnp.concatenate(rows, axis=0)
    parts = ["x", "pair", "summed", "a", "b"]
    taps_sum = SmallSum(
        me, links, *[getattr(r, "taps_sum_" + p) for p in parts], r.sum_taps
    )
    taps_sum.start()
    expand_sum.scatter()
    taps_sum.to_q()

    @pl.loop(0, 4)
    def _(t):
        grad = None
        for c in range(4):
            lane = slice(c * 256, (c + 1) * 256)
            part = nt(lanes_of(r.grad_exp, 2 * c, cell_rows(t)), r.w_expand[:, lane])
            grad = part if grad is None else grad + part
        unit, rstd = centre(r.image[map_rows(t)].reshape(TILE, CH).astype(F32))
        r.norm_acc[0] += fold(grad * unit)
        value = r.grad_mixed[cell_rows(t)] + norm_back(unit, rstd, grad * gain_first)
        r.grad_map[map_rows(t)] = value.astype(BF16).reshape(4, MAP_COLS, CH)

    flush("grad_map").start()
    att_back.end()

    @pl.loop(0, 4)
    def _(t):
        att = r.att_in[map_rows(t, 16)].reshape(TILE, CH)
        value = r.mixed[cell_rows(t)].astype(F32) + nn(att, r.w_out[...])
        r.out_map[map_rows(t)] = value.astype(BF16).reshape(4, MAP_COLS, CH)

    flush("out_map").start()
    rows = []
    for n in range(2):
        sums = jnp.sum(r.norm_acc[n], axis=0, keepdims=True)
        rows += [sums[:, :128], sums[:, 128:]]
    r.norms_x[...] = jnp.concatenate(rows + [jnp.zeros((4, 128), F32)], axis=0)
    norms_sum = TileSum(me, links, r.norms_x, r.norms_pair, r.norms_slots)
    norms_sum.start()
    bias_sum.end()
    flush("sum_bias").start()
    rows = [pooled, grad_logit, jnp.pad(hidden, ((0, 0), (0, 960)))]
    rows += [jnp.pad(grad_squeezed, ((0, 0), (0, 960))), jnp.zeros((4, 1024), F32)]
    r.gate_rows[...] = jnp.concatenate(rows, axis=0)
    flush("gate_rows").start()
    taps_sum.to_rows()
    expand_sum.end()
    final = Gather(me, links, r.sum_expand, r.expand_slots)
    final.piece[...] = jnp.sum(r.expand_slots[...].astype(F32), axis=0).astype(BF16)
    final.send_all()
    early.back_pair()
    taps_sum.back_q()
    early.end()
    flush("sum_early").start()
    r.sum_norms[...] = norms_sum.end()
    flush("sum_norms").start()
    taps_sum.end()
    flush("sum_taps").start()
    final.back_pair()
    final.end()
    flush("sum_expand").start()
    for name in OUTS:
        flush(name).wait()
    links.finish()


FINAL = dict(
    block_out=((MAP_ROWS, MAP_COLS, CH), BF16),
    grad_image=((MAP_ROWS, MAP_COLS, CH), BF16),
    grad_norm0=((1, CH), F32),
    grad_expand=((CH, 1024), F32),
    grad_depth=((3, 3, 1024), F32),
    grad_squeeze=((64, 1024), F32),
    grad_excite=((64, 1024), F32),
    grad_project=((1024, CH), F32),
    grad_norm1=((1, CH), F32),
    grad_qkv=((CH, 3 * CH), F32),
    grad_out_proj=((CH, CH), F32),
    grad_bias=((HEADS, MEMBERS, MEMBERS), F32),
)


def finish_kernel(*args):
    r = Refs()
    names = ["hbm_" + n for n in OUTS] + ["hbm_" + n for n in FINAL]
    names += list(OUTS) + list(FINAL)[2:] + ["in_sems", "out_sems"]
    for name, ref in zip(names, args, strict=True):
        setattr(r, name, ref)
    r.block_out, r.grad_image = r.out_map, r.grad_map

    def fetch(name):
        at = list(OUTS).index(name)
        return pltpu.make_async_copy(getattr(r, "hbm_" + name), getattr(r, name), r.in_sems.at[at])

    def flush(name):
        at = list(FINAL).index(name)
        return pltpu.make_async_copy(
            getattr(r, name), getattr(r, "hbm_" + name), r.out_sems.at[at]
        )

    order = ["sum_expand", "sum_early", "out_map", "grad_map"]
    order += ["sum_bias", "sum_taps", "sum_norms", "gate_rows"]
    for name in order:
        fetch(name).start()
    fetch("sum_expand").wait()
    r.grad_expand[...] = r.sum_expand[...].astype(F32)
    flush("grad_expand").start()
    fetch("sum_early").wait()
    for n in range(8):
        lane = slice(n * 128, (n + 1) * 128)
        part = r.sum_early[:, n * 256 : n * 256 + 128].astype(F32)
        if n < 6:
            r.grad_qkv[:, lane] = part
        else:
            r.grad_out_proj[:, (n - 6) * 128 : (n - 5) * 128] = part
    flush("grad_qkv").start()
    flush("grad_out_proj").start()
    for n in range(8):
        lane = slice(n * 128, (n + 1) * 128)
        r.grad_project[lane, :] = r.sum_early[:, n * 256 + 128 : n * 256 + 256].astype(F32).T
    flush("grad_project").start()
    fetch("out_map").wait()
    flush("block_out").start()
    fetch("grad_map").wait()
    flush("grad_image").start()
    for name in order[4:]:
        fetch(name).wait()
    for h in range(0, HEADS, 2):
        both = r.sum_bias[:, h * 64 : (h + 2) * 64].T
        r.grad_bias[h] = both[:64]
        r.grad_bias[h + 1] = both[64:]
    for k in range(9):
        if k < 8:
            rows = [r.sum_taps[c * 8 + k : c * 8 + k + 1, :128] for c in range(LANES)]
        else:
            rows = [r.sum_taps[c * 8 : c * 8 + 1, 128:] for c in range(LANES)]
        r.grad_depth[k // 3, k % 3 : k % 3 + 1, :] = jnp.concatenate(rows, axis=1)
    for n, out in enumerate((r.grad_norm0, r.grad_norm1)):
        rows = [r.sum_norms[n * 2 + c : n * 2 + c + 1, :] for c in range(2)]
        out[...] = jnp.concatenate(rows, axis=1)
    pooled, grad_logit = r.gate_rows[0:1, :], r.gate_rows[1:2, :]
    hidden, grad_squeezed = r.gate_rows[2:3, :64], r.gate_rows[3:4, :64]
    r.grad_excite[...] = outer(hidden, grad_logit)
    r.grad_squeeze[...] = outer(grad_squeezed, pooled)
    early = ["block_out", "grad_image", "grad_expand", "grad_qkv", "grad_out_proj", "grad_project"]
    for name in FINAL:
        if name not in early:
            flush(name).start()
    for name in FINAL:
        flush(name).wait()


def on_device(
    image,
    out_cotangent,
    norm0_gain,
    w_expand,
    w_depth,
    w_squeeze,
    w_excite,
    w_project,
    norm1_gain,
    w_qkv,
    w_out,
    attn_bias,
):
    vmem = pl.BlockSpec(memory_space=pltpu.VMEM)
    any_space = pl.BlockSpec(memory_space=pl.ANY)
    buffers = lambda shapes: [pltpu.VMEM(*shape) for shape in shapes.values()]
    made = pl.pallas_call(
        block_kernel,
        out_shape=[jax.ShapeDtypeStruct(*shape) for shape in OUTS.values()],
        in_specs=[vmem] * len(IN_NAMES) + [any_space] * len(LATE),
        out_specs=[any_space] * len(OUTS),
        scratch_shapes=buffers(LATE)
        + buffers(OUTS)
        + buffers(SCRATCH)
        + [pltpu.SemaphoreType.DMA((n,)) for n in (SEMS, len(LATE), len(OUTS))],
        compiler_params=pltpu.CompilerParams(
            collective_id=0, has_side_effects=True, vmem_limit_bytes=63 * 2**20
        ),
        name="block",
    )(
        norm0_gain,
        norm1_gain,
        w_depth,
        image,
        w_expand,
        out_cotangent.reshape(MEMBERS, GROUPS, CH),
        w_out,
        attn_bias,
        w_squeeze.T,
        w_excite,
        w_project,
        w_qkv,
    )
    final = pl.pallas_call(
        finish_kernel,
        out_shape=[jax.ShapeDtypeStruct(*shape) for shape in FINAL.values()],
        in_specs=[any_space] * len(OUTS),
        out_specs=[any_space] * len(FINAL),
        scratch_shapes=buffers(OUTS)
        + buffers(FINAL)[2:]
        + [pltpu.SemaphoreType.DMA((n,)) for n in (len(OUTS), len(FINAL))],
        compiler_params=pltpu.CompilerParams(vmem_limit_bytes=63 * 2**20),
        name="finish",
    )(*made)
    final = dict(zip(FINAL, final))
    final["grad_norm0"] = final["grad_norm0"].reshape(CH)
    final["grad_norm1"] = final["grad_norm1"].reshape(CH)
    final["grad_squeeze"] = final["grad_squeeze"].T
    return tuple(final.values())


def solution(mesh):
    mapped = P("row", "col", None)
    return jax.shard_map(
        on_device,
        mesh=mesh,
        in_specs=(mapped, mapped) + (P(),) * 10,
        out_specs=(mapped, mapped) + (P(),) * 10,
        check_vma=False,
    )
```

```python
import functools

import jax
import jax.numpy as jnp
from jax import lax
from jax.experimental import pallas as pl
from jax.experimental.pallas import tpu as pltpu
from jax.sharding import PartitionSpec as P

F32 = jnp.float32
BF16 = jnp.bfloat16
MESH = pl.DeviceIdType.MESH
ROWS = 8
COLS = 16
CHIPS = 64
HEADS = 8
MEMBERS = 64
GROUPS = 16
CH = 256
MAP_ROWS = 16
MAP_COLS = 64
CELLS = MAP_ROWS * MAP_COLS
CELLS_TOTAL = 131072
LANES = 8
PAD = 80
PADDED = (MAP_ROWS + 2) * PAD
TILE = 256
SCALE = 32 ** (-0.5)
GELU_A = 0.7978845608028654
GELU_B = 0.044715


def nn(a, b):
    return jnp.dot(a, b, preferred_element_type=F32)


def nt(a, b):
    return lax.dot_general(a, b, (((1,), (1,)), ((), ())), preferred_element_type=F32)


def tn(a, b):
    return lax.dot_general(a, b, (((0,), (0,)), ((), ())), preferred_element_type=F32)


def gelu(x):
    return 0.5 * x * (1.0 + jnp.tanh(GELU_A * (x + GELU_B * (x * x * x))))


def gelu_slope(x):
    square = x * x
    t = jnp.tanh(GELU_A * (x + GELU_B * (square * x)))
    return 0.5 * (1.0 + t) + (0.5 * GELU_A) * x * (1.0 - t * t) * (1.0 + (3 * GELU_B) * square)


def centre(x):
    centered = x - jnp.mean(x, axis=-1, keepdims=True)
    rstd = lax.rsqrt(jnp.mean(centered * centered, axis=-1, keepdims=True) + 1e-05)
    return centered * rstd, rstd


def norm_back(unit, rstd, grad_unit):
    first = jnp.mean(grad_unit, axis=-1, keepdims=True)
    second = jnp.mean(grad_unit * unit, axis=-1, keepdims=True)
    return rstd * (grad_unit - first - unit * second)


def fold(x):
    return jnp.sum(x.reshape(x.shape[0] // 8, 8, x.shape[1]), axis=0)


def thirds(x):
    one = x.astype(BF16).astype(F32)
    two = (x - one).astype(BF16).astype(F32)
    three = (x - one - two).astype(BF16).astype(F32)
    return one, two, three


def stack_rows(rows):
    width = rows[0].shape[1]
    rows = list(rows) + [jnp.zeros((8 - len(rows), width), F32)]
    return jnp.concatenate(rows, axis=0).astype(BF16)


def wide_product(x, w, product):
    return jnp.sum(product(stack_rows(thirds(x)), w), axis=0, keepdims=True)


def outer(a, b):
    a1, a2, a3 = thirds(a)
    b1, b2, b3 = thirds(b)
    return tn(stack_rows([a1, a1, a2, a2, a1, a3]), stack_rows([b1, b2, b1, b2, b3, b1]))


def aligned(start, size, unit=8):
    return pl.ds(pl.multiple_of(start, unit), size)


class Place:
    def __init__(self):
        self.row = lax.axis_index("row")
        self.col = lax.axis_index("col")
        self.core = lax.rem(self.col, 2)
        self.q = lax.div(self.col, 2)
        self.chip = self.row * 8 + self.q
        self.qs = [lax.rem(self.q + k, 8) for k in range(8)]
        self.cols = [q * 2 + self.core for q in self.qs]

    def partner(self):
        return (self.row, self.q * 2 + 1 - self.core)

    def q_peer(self, k):
        return self.qs[k], (self.row, self.cols[k])

    def row_peer(self, k):
        row = lax.rem(self.row + k, ROWS)
        return row, (row, self.col)

    def beside(self, up, right):
        return (lax.rem(self.row + ROWS + up, ROWS), lax.rem(self.col + COLS + right, COLS))

    def every_peer(self, body):
        def others(k, carry):
            row = lax.rem(self.row + k, ROWS)
            for n in range(1, 8):
                body(row, self.qs[n], (row, self.cols[n]))
            return carry

        def same(k, carry):
            row = lax.rem(self.row + k, ROWS)
            body(row, self.q, (row, self.col))
            return carry

        lax.fori_loop(0, ROWS, others, 0)
        lax.fori_loop(1, ROWS, same, 0)


class Links:
    def __init__(self, sems):
        self.sems = sems
        self.used = 0
        self.sent = []

    def pair(self):
        at = self.used
        self.used += 2
        return self.sems.at[at], self.sems.at[at + 1]

    def finish(self):
        for sem, buf in self.sent:
            pltpu.make_async_copy(buf, buf, sem).wait()


def push(src, dst, send, recv, device):
    pltpu.make_async_remote_copy(
        src_ref=src,
        dst_ref=dst,
        send_sem=send,
        recv_sem=recv,
        device_id=device,
        device_id_type=MESH,
    ).start()


def arrived(buf, sem):
    pltpu.make_async_copy(buf, buf, sem).wait()


class TileSum:
    def __init__(self, me, links, x, pair_slot, slots):
        self.me, self.links = me, links
        self.x, self.pair_slot, self.slots = x, pair_slot, slots
        self.s0, self.s1 = links.pair(), links.pair()

    def start(self):
        push(self.x, self.pair_slot, *self.s0, self.me.partner())
        self.links.sent.append((self.s0[0], self.x))
        arrived(self.pair_slot, self.s0[1])
        self.slots[self.me.chip] = self.x[...] + self.pair_slot[...]
        mine = self.slots.at[self.me.chip]
        self.me.every_peer(lambda row, q, device: push(mine, mine, *self.s1, device))
        self.links.sent.append((self.s1[0], self.slots.at[pl.ds(0, CHIPS - 1)]))

    def end(self):
        arrived(self.slots.at[pl.ds(0, CHIPS - 1)], self.s1[1])
        return jnp.sum(self.slots[...], axis=0)


class Scatter:
    def __init__(self, me, links, x, pair_in, summed, slots):
        self.me, self.links = me, links
        self.x, self.pair_in, self.summed, self.slots = x, pair_in, summed, slots
        self.sems = [links.pair() for _ in range(2)]

    def half_of(self, core):
        return self.x.at[aligned(core * 128, 128, 128)]

    def piece(self, row, q):
        return self.summed.at[aligned(row * 16, 16, 16), aligned(q * 128, 128, 128)]

    def start(self):
        push(self.half_of(1 - self.me.core), self.pair_in, *self.sems[0], self.me.partner())
        self.links.sent.append((self.sems[0][0], self.pair_in))

    def scatter(self):
        me = self.me
        arrived(self.pair_in, self.sems[0][1])
        mine = self.half_of(me.core)
        self.summed[...] = (mine[...].astype(F32) + self.pair_in[...].astype(F32)).astype(BF16)
        to = self.slots.at[me.chip]
        me.every_peer(
            lambda row, q, device: push(self.piece(row, q), to, *self.sems[1], device)
        )
        self.slots[me.chip] = self.piece(me.row, me.q)[...]

    def end(self):
        arrived(self.slots.at[pl.ds(0, CHIPS - 1)], self.sems[1][1])
        self.links.sent.append((self.sems[1][0], self.slots.at[pl.ds(0, CHIPS - 1)]))


class HalvesScatter(Scatter):
    def __init__(self, *args):
        super().__init__(*args)
        self.pairs = [self.sems[0], self.links.pair()]

    def start(self, n):
        lane = pl.ds(n * 512, 512)
        other = aligned((1 - self.me.core) * 128, 128, 128)
        to = self.pair_in.at[:, lane]
        push(self.x.at[other, lane], to, *self.pairs[n], self.me.partner())
        self.links.sent.append((self.pairs[n][0], to))

    def scatter(self):
        me = self.me
        mine = aligned(me.core * 128, 128, 128)
        for n in range(2):
            lane = pl.ds(n * 512, 512)
            arrived(self.pair_in.at[:, lane], self.pairs[n][1])
            total = self.x[mine, lane].astype(F32) + self.pair_in[:, lane].astype(F32)
            self.summed[:, lane] = total.astype(BF16)
        to = self.slots.at[me.chip]
        me.every_peer(
            lambda row, q, device: push(self.piece(row, q), to, *self.sems[1], device)
        )
        self.slots[me.chip] = self.piece(me.row, me.q)[...]


class Gather:
    def __init__(self, me, links, out, like):
        self.me, self.links, self.out, self.like = me, links, out, like
        self.width = out.shape[1] // 8
        self.sems = [links.pair() for _ in range(2)]
        lane = aligned(me.q * self.width, self.width, 128)
        self.piece = out.at[aligned(me.core * 128 + me.row * 16, 16, 16), lane]

    def send(self, row, k):
        push(self.piece, self.piece, *self.sems[0], (row, self.me.cols[k]))

    def send_all(self):
        self.me.every_peer(
            lambda row, q, device: push(self.piece, self.piece, *self.sems[0], device)
        )

    def back_pair(self):
        me = self.me
        arrived(self.like.at[pl.ds(0, CHIPS - 1)], self.sems[0][1])
        self.links.sent.append((self.sems[0][0], self.like.at[pl.ds(0, CHIPS - 1)]))
        half = self.out.at[aligned(me.core * 128, 128, 128)]
        push(half, half, *self.sems[1], me.partner())
        self.links.sent.append((self.sems[1][0], half))

    def end(self):
        arrived(self.out.at[pl.ds(0, 128)], self.sems[1][1])


class SmallSum:
    def __init__(self, me, links, x, pair_in, summed, slots_a, slots_b, out):
        self.me, self.links = me, links
        self.x, self.pair_in, self.summed, self.out = x, pair_in, summed, out
        self.slots_a, self.slots_b = slots_a, slots_b
        self.sems = [links.pair() for _ in range(4)]

    def start(self):
        push(self.x, self.pair_in, *self.sems[0], self.me.partner())
        self.links.sent.append((self.sems[0][0], self.pair_in))

    def to_q(self):
        arrived(self.pair_in, self.sems[0][1])
        self.summed[...] = self.x[...] + self.pair_in[...]
        for k in range(1, 8):
            q, device = self.me.q_peer(k)
            piece = self.summed.at[aligned(q * 8, 8)]
            push(piece, self.slots_a.at[self.me.q], *self.sems[1], device)
        self.links.sent.append((self.sems[1][0], self.slots_a.at[pl.ds(0, 7)]))

    def to_rows(self):
        me = self.me
        self.slots_a[me.q] = self.summed[aligned(me.q * 8, 8)]
        arrived(self.slots_a.at[pl.ds(0, 7)], self.sems[1][1])
        self.slots_b[me.row] = jnp.sum(self.slots_a[...], axis=0)
        for k in range(1, 8):
            _, device = me.row_peer(k)
            piece = self.slots_b.at[me.row]
            push(piece, piece, *self.sems[2], device)
        self.links.sent.append((self.sems[2][0], self.slots_b.at[pl.ds(0, 7)]))

    def back_q(self):
        me = self.me
        arrived(self.slots_b.at[pl.ds(0, 7)], self.sems[2][1])
        piece = self.out.at[aligned(me.q * 8, 8)]
        piece[...] = jnp.sum(self.slots_b[...], axis=0)
        for k in range(1, 8):
            _, device = me.q_peer(k)
            push(piece, piece, *self.sems[3], device)
        self.links.sent.append((self.sems[3][0], self.slots_a.at[pl.ds(0, 7)]))

    def end(self):
        arrived(self.slots_a.at[pl.ds(0, 7)], self.sems[3][1])


class Exchange:
    def __init__(self, me, links, src, dst):
        self.me, self.links, self.src, self.dst = me, links, src, dst
        self.sems = links.pair()

    def send(self, row, k):
        q, col = self.me.qs[k], self.me.cols[k]
        push(self.src.at[row * 8 + q], self.dst.at[self.me.chip], *self.sems, (row, col))

    def send_row(self, row):
        for k in range(1, 8):
            self.send(row, k)

        @pl.when(row != self.me.row)
        def _():
            self.send(row, 0)

    def send_tile(self, t):
        for k in range(2):
            self.send_row(t * 2 + lax.rem(self.me.row + k, 2))

    def end(self):
        self.dst[self.me.chip] = self.src[self.me.chip]
        arrived(self.dst.at[pl.ds(0, CHIPS - 1)], self.sems[1])
        self.links.sent.append((self.sems[0], self.dst.at[pl.ds(0, CHIPS - 1)]))


class Halo:
    def __init__(
        self, me, links, rows_out, cols_out, corners_out, rows_in, cols_in, corners_in
    ):
        self.me, self.links = me, links
        self.rows_out, self.cols_out, self.corners_out = rows_out, cols_out, corners_out
        self.rows_in, self.cols_in, self.corners_in = rows_in, cols_in, corners_in
        self.sems = [links.pair() for _ in range(3)]

    def start(self):
        me = self.me
        for side, up in ((0, -1), (1, 1)):
            push(
                self.rows_out[side],
                self.rows_in.at[1 - side],
                *self.sems[0],
                me.beside(up, 0),
            )
        for side, right in ((0, -1), (1, 1)):
            strip = self.cols_out.at[side]
            push(strip, self.cols_in.at[1 - side], *self.sems[1], me.beside(0, right))
            for end, up in ((0, -1), (1, 1)):
                push(
                    self.corners_out[end * 2 + side],
                    self.corners_in.at[(1 - end) * 2 + 1 - side],
                    *self.sems[2],
                    me.beside(up, right),
                )

    def end(self):
        for n, buf in enumerate((self.rows_in, self.cols_in, self.corners_in)):
            arrived(buf, self.sems[n][1])
            self.links.sent.append((self.sems[n][0], buf))


IN_NAMES = ["norm0_gain", "norm1_gain", "w_depth"]
LATE = dict(
    image=((MAP_ROWS, MAP_COLS, CH), BF16),
    w_expand=((CH, 1024), BF16),
    dy=((MEMBERS, GROUPS, CH), BF16),
    w_out=((CH, CH), BF16),
    bias=((HEADS, MEMBERS, MEMBERS), F32),
    w_squeeze_t=((64, 1024), BF16),
    w_excite=((64, 1024), BF16),
    w_project=((1024, CH), BF16),
    w_qkv=((CH, 768), BF16),
)
OUTS = dict(
    out_map=((MAP_ROWS, MAP_COLS, CH), BF16),
    grad_map=((MAP_ROWS, MAP_COLS, CH), BF16),
    sum_expand=((CH, 1024), BF16),
    sum_early=((CH, 2048), BF16),
    sum_bias=((MEMBERS, 512), F32),
    sum_taps=((64, 256), F32),
    sum_norms=((8, 128), F32),
    gate_rows=((8, 1024), F32),
)


def big_scratch(name):
    return {
        name + "_x": ((CH, 1024), BF16),
        name + "_pair": ((CH // 2, 1024), BF16),
        name + "_summed": ((CH // 2, 1024), BF16),
    }


def small_scratch(name, width):
    return {
        name + "_x": ((64, width), F32),
        name + "_pair": ((64, width), F32),
        name + "_summed": ((64, width), F32),
        name + "_a": ((8, 8, width), F32),
        name + "_b": ((8, 8, width), F32),
    }


def tile_scratch(name):
    return {
        name + "_x": ((8, 128), F32),
        name + "_pair": ((8, 128), F32),
        name + "_slots": ((CHIPS, 8, 128), F32),
    }


SCRATCH = dict(
    taps=((16, 1024), F32),
    normed=((CELLS, CH), BF16),
    normed_t=((CH, CELLS), BF16),
    spread=((LANES, PADDED, 128), F32),
    expanded=((LANES, CELLS, 128), F32),
    depth=((LANES, CELLS, 128), F32),
    act=((LANES, CELLS, 128), BF16),
    pool_acc=((LANES, 8, 128), F32),
    edge_cols=((2, 16, CH), BF16),
    edge_rows_in=((2, MAP_COLS, CH), BF16),
    edge_cols_in=((2, 16, CH), BF16),
    edge_corners_in=((4, 16, CH), BF16),
    gate=((1, 1024), F32),
    gate_back=((1, 1024), F32),
    mixed=((CELLS, CH), BF16),
    normed_two=((MEMBERS, GROUPS, CH), BF16),
    grid_x=((MEMBERS, GROUPS, CH), BF16),
    grid_dy=((MEMBERS, GROUPS, CH), BF16),
    qkv=((6, CELLS, 128), F32),
    grid_g=((2, CELLS, 128), F32),
    att_rows=((2, CELLS, 128), F32),
    packed_back=((6, CELLS, 128), F32),
    probs=((GROUPS, MEMBERS, 512), F32),
    bias_t=((MEMBERS, 512), F32),
    att_out=((MEMBERS, GROUPS, CH), BF16),
    att_in=((MEMBERS, GROUPS, CH), BF16),
    gn_out=((MEMBERS, GROUPS, CH), BF16),
    gn_in=((MEMBERS, GROUPS, CH), BF16),
    grad_mixed=((CELLS, CH), F32),
    grad_mixed_b=((CELLS, CH), BF16),
    grad_gated=((LANES, CELLS, 128), F32),
    gate_acc=((LANES, 8, 128), F32),
    grad_pre=((LANES, PADDED, 128), F32),
    slope_rows=((2, LANES, MAP_COLS, 128), BF16),
    slope_cols=((2, LANES, 16, 128), BF16),
    slope_corners=((4, 16, 128), BF16),
    slope_rows_in=((2, LANES, MAP_COLS, 128), BF16),
    slope_cols_in=((2, LANES, 16, 128), BF16),
    slope_corners_in=((4, 16, 128), BF16),
    pre_rows=((2, LANES, MAP_COLS, 128), BF16),
    pre_cols=((2, LANES, 16, 128), BF16),
    pre_rows_in=((2, LANES, MAP_COLS, 128), BF16),
    pre_cols_in=((2, LANES, 16, 128), BF16),
    pre_corners=((4, 16, 128), BF16),
    pre_corners_in=((4, 16, 128), BF16),
    tap_acc=((LANES, 9, 8, 128), F32),
    grad_exp=((LANES, CELLS, 128), BF16),
    norm_acc=((2, 8, CH), F32),
    pair_acc=((CH, 1024), F32),
    **tile_scratch("pool"),
    **tile_scratch("gateg"),
    **big_scratch("expand"),
    **big_scratch("project"),
    **big_scratch("pair"),
    expand_slots=((CHIPS, 16, 128), BF16),
    pair_slots=((CHIPS, 16, 128), BF16),
    project_slots=((CHIPS, 16, 128), BF16),
    **small_scratch("bias", 512),
    **small_scratch("taps_sum", 256),
    **tile_scratch("norms"),
)
SEMS = 96


class Refs:
    pass


def lanes_of(ref, first, at):
    return jnp.concatenate([ref[first, at, :], ref[first + 1, at, :]], axis=1)


def map_rows(t, count=4):
    return pl.ds(t * count, count)


def cell_rows(t):
    return aligned(t * TILE, TILE, TILE)


def pad_row(row, col=0):
    return pl.multiple_of(row * PAD + col, 8)


def block_kernel(*args):
    r = Refs()
    names = IN_NAMES + ["hbm_" + n for n in LATE] + ["hbm_" + n for n in OUTS]
    names += list(LATE) + list(OUTS) + list(SCRATCH) + ["sems", "late_sems", "out_sems"]
    for name, ref in zip(names, args, strict=True):
        setattr(r, name, ref)
    me = Place()
    links = Links(r.sems)

    def late(name):
        at = list(LATE).index(name)
        return pltpu.make_async_copy(
            getattr(r, "hbm_" + name), getattr(r, name), r.late_sems.at[at]
        )

    def flush(name):
        at = list(OUTS).index(name)
        return pltpu.make_async_copy(
            getattr(r, name), getattr(r, "hbm_" + name), r.out_sems.at[at]
        )

    for name in LATE:
        late(name).start()
    off = r.image.shape[0] - 1

    barrier = pltpu.get_barrier_semaphore()

    def greet(row, q, device):
        pl.semaphore_signal(barrier, inc=1, device_id=device, device_id_type=MESH)

    me.every_peer(greet)
    for up in (-1, 0, 1):
        for right in (-1, 1):
            pl.semaphore_signal(
                barrier, inc=1, device_id=me.beside(up, right), device_id_type=MESH
            )

    gain_first = r.norm0_gain[...].astype(F32).reshape(1, CH)
    gain_second = r.norm1_gain[...].astype(F32).reshape(1, CH)
    for a in range(3):
        r.taps[a * 3 : a * 3 + 3, :] = r.w_depth[a].astype(F32)

    late("image").wait()
    for side, col in ((0, 0), (1, MAP_COLS - 16)):
        rows = []
        for i in range(MAP_ROWS):
            part = r.image[i, col : col + 16, :].astype(F32)
            rows.append(part[0:1] if side == 0 else part[15:16])
        r.edge_cols[side] = jnp.concatenate(rows, axis=0).astype(BF16)

    @pl.loop(0, 4, unroll=4)
    def _(t):
        x = r.image[map_rows(t)].reshape(TILE, CH).astype(F32)
        unit, _ = centre(x)
        r.normed[cell_rows(t)] = (unit * gain_first).astype(BF16)

    late("w_expand").wait()

    @pl.loop(0, 4)
    def _(t):
        for c in range(4):
            e = nn(r.normed[cell_rows(t)], r.w_expand[:, c * 256 : (c + 1) * 256])
            s = gelu(e).astype(BF16).astype(F32)
            for h in range(2):
                lane = slice(h * 128, (h + 1) * 128)
                r.expanded[2 * c + h, cell_rows(t), :] = e[:, lane]
                for a in range(4):
                    at = pl.ds(pad_row(1 + t * 4 + a, 8), MAP_COLS)
                    r.spread[2 * c + h, at, :] = s[a * 64 : (a + 1) * 64, lane]

    pl.semaphore_wait(barrier, CHIPS + 5)
    halo = Halo(
        me,
        links,
        (r.image.at[0], r.image.at[off]),
        r.edge_cols,
        [r.edge_cols.at[side] for side in (0, 1, 0, 1)],
        r.edge_rows_in,
        r.edge_cols_in,
        r.edge_corners_in,
    )
    halo.start()
    late("dy").wait()
    dy_out = Exchange(me, links, r.dy, r.grid_dy)

    @pl.loop(0, LANES)
    def _(c):
        row = lax.rem(me.row + c, ROWS)
        for t in range(4):
            for k in (2 * t + 1, 2 * t):
                if k:
                    dy_out.send(row, k)
            at = pl.ds(t * TILE, TILE)
            r.expanded[c, at, :] = gelu_slope(r.expanded[c, at, :])

        @pl.when(c > 0)
        def _():
            dy_out.send(row, 0)

    halo.end()

    up_ok = (me.row > 0).astype(F32)
    down_ok = (me.row < ROWS - 1).astype(F32)
    left_ok = (me.col > 0).astype(F32)
    right_ok = (me.col < COLS - 1).astype(F32)
    around = jnp.concatenate(
        [
            r.edge_rows_in[0].astype(F32) * up_ok,
            r.edge_rows_in[1].astype(F32) * down_ok,
            r.edge_cols_in[0].astype(F32) * left_ok,
            r.edge_cols_in[1].astype(F32) * right_ok,
            r.edge_corners_in[0].astype(F32)[8:16] * (up_ok * left_ok),
            r.edge_corners_in[1].astype(F32)[8:16] * (up_ok * right_ok),
            r.edge_corners_in[2].astype(F32)[0:8] * (down_ok * left_ok),
            r.edge_corners_in[3].astype(F32)[0:8] * (down_ok * right_ok),
        ],
        axis=0,
    )
    unit, _ = centre(around)
    around_normed = (unit * gain_first).astype(BF16)
    last = (MAP_ROWS + 1) * PAD
    for c in range(4):
        s = gelu(nn(around_normed, r.w_expand[:, c * 256 : (c + 1) * 256]))
        s = s.astype(BF16).astype(F32)
        for h in range(2):
            v = s[:, h * 128 : (h + 1) * 128]
            n = 2 * c + h
            r.spread[n, 8:72, :] = v[0:64]
            r.spread[n, last + 8 : last + 72, :] = v[64:128]
            r.spread[n, pl.ds(PAD + 7, MAP_ROWS, stride=PAD), :] = v[128:144]
            r.spread[n, pl.ds(PAD + 72, MAP_ROWS, stride=PAD), :] = v[144:160]
            r.spread[n, 7:8, :] = v[167:168]
            r.spread[n, 72:73, :] = v[175:176]
            r.spread[n, last + 7 : last + 8, :] = v[176:177]
            r.spread[n, last + 72 : last + 73, :] = v[184:185]

    def taps_of(c):
        lane = aligned(c * 128, 128, 128)
        return [r.taps[k : k + 1, lane] for k in range(9)]

    @pl.loop(0, LANES)
    def _(c):
        taps = taps_of(c)

        def block(n, total):
            sums = [None] * 4
            for row in range(6):
                view = r.spread.at[c, pl.ds(pad_row(n * 4 + row), PAD)]
                for b in range(3):
                    v = view[pl.ds(7 + b, MAP_COLS), :]
                    for a in range(3):
                        i = row - a
                        if 0 <= i < 4:
                            term = v * taps[a * 3 + b]
                            sums[i] = term if sums[i] is None else sums[i] + term
            for i in range(4):
                at = aligned((n * 4 + i) * MAP_COLS, MAP_COLS, MAP_COLS)
                r.depth[c, at, :] = sums[i]
                value = gelu(sums[i])
                r.act[c, at, :] = value.astype(BF16)
                total = total + fold(value)
            return total

        total = lax.fori_loop(0, 4, block, jnp.zeros((8, 128), F32), unroll=4)
        r.pool_x[pl.ds(c, 1), :] = jnp.sum(total, axis=0, keepdims=True)

    pool = TileSum(me, links, r.pool_x, r.pool_pair, r.pool_slots)
    pool.start()

    @pl.loop(0, LANES * 4)
    def _(n):
        c, t = lax.div(n, 4), lax.rem(n, 4)
        r.depth[c, cell_rows(t), :] = gelu_slope(r.depth[c, cell_rows(t), :])

    dy_out.end()
    late("w_out").wait()
    late("bias").wait()

    @pl.loop(0, 4)
    def _(t):
        dy = r.grid_dy[map_rows(t, 16)].reshape(TILE, CH)
        g = nt(dy, r.w_out[...])
        for n in range(2):
            r.grid_g[n, cell_rows(t), :] = g[:, n * 128 : (n + 1) * 128]

    for h in range(0, HEADS, 2):
        both = jnp.concatenate([r.bias[h], r.bias[h + 1]], axis=0)
        r.bias_t[:, h * 64 : (h + 2) * 64] = both.T
    for t in range(4):
        r.normed_t[:, t * TILE : (t + 1) * TILE] = r.normed[t * TILE : (t + 1) * TILE].T

    def flat(tile):
        return jnp.concatenate([tile[n : n + 1] for n in range(8)], axis=1)

    pooled = flat(pool.end()) * (1.0 / CELLS_TOTAL)
    for name in ("w_squeeze_t", "w_excite", "w_project", "w_qkv"):
        late(name).wait()
    squeezed = wide_product(pooled, r.w_squeeze_t[...], nt)
    open_part = jax.nn.sigmoid(squeezed)
    hidden = squeezed * open_part
    gate = jax.nn.sigmoid(wide_product(hidden, r.w_excite[...], nn))
    r.gate[...] = gate

    grid_out = Exchange(me, links, r.normed_two, r.grid_x)
    start_tile = lax.div(me.row, 2)

    @pl.loop(0, 4, unroll=4)
    def _(step):
        t = lax.rem(start_tile + step, 4)
        total = r.image[map_rows(t)].reshape(TILE, CH).astype(F32)
        for c in range(4):
            lane = slice(c * 256, (c + 1) * 256)
            gated = lanes_of(r.act, 2 * c, cell_rows(t)).astype(F32) * r.gate[:, lane]
            total = total + nn(gated.astype(BF16), r.w_project[lane, :])
        mixed = total.astype(BF16)
        r.mixed[cell_rows(t)] = mixed
        unit, _ = centre(mixed.astype(F32))
        normed = (unit * gain_second).astype(BF16)
        r.normed_two[map_rows(t, 16)] = normed.reshape(16, GROUPS, CH)
        grid_out.send_tile(t)

    def pack_edges(ref, width, first, rows_out, cols_out, corners_out):
        final_row = first + (MAP_ROWS - 1) * width

        @pl.loop(0, LANES)
        def _(c):
            for side, at in ((0, first), (1, final_row)):
                rows_out[side, c] = ref[c, at : at + MAP_COLS, :].astype(BF16)
            for side, at in ((0, first), (1, first + MAP_COLS - 1)):
                cells = ref[c, pl.ds(at, MAP_ROWS, stride=width), :]
                cols_out[side, c] = cells.astype(BF16)

        ends = (first, first + MAP_COLS - 1, final_row, final_row + MAP_COLS - 1)
        for corner, at in enumerate(ends):
            cells = [ref[c, at : at + 1, :] for c in range(LANES)]
            cells.append(jnp.zeros((8, 128), F32))
            corners_out[corner] = jnp.concatenate(cells, axis=0).astype(BF16)

    def edge_halo(name):
        parts = ["rows", "cols", "corners", "rows_in", "cols_in", "corners_in"]
        rows, cols, corners, *arriving = [getattr(r, name + "_" + p) for p in parts]
        return Halo(
            me,
            links,
            (rows.at[0], rows.at[1]),
            cols,
            [corners.at[n] for n in range(4)],
            *arriving,
        )

    pack_edges(r.depth, MAP_COLS, 0, r.slope_rows, r.slope_cols, r.slope_corners)
    slope_halo = edge_halo("slope")
    slope_halo.start()
    grid_out.end()

    @pl.loop(0, 4, unroll=4)
    def _(t):
        x = r.grid_x[map_rows(t, 16)].reshape(TILE, CH)
        qkv = nn(x, r.w_qkv[...])
        for n in range(6):
            r.qkv[n, cell_rows(t), :] = qkv[:, n * 128 : (n + 1) * 128]

    head_of = lax.div(lax.broadcasted_iota(jnp.int32, (1, 128), 1), 32)
    masks_f = [(head_of == h).astype(F32) for h in range(4)]
    masks = [m.astype(BF16) for m in masks_f]
    unroll = 8

    def spread_heads(a):
        return jnp.concatenate([a * m for m in masks], axis=0)

    def own_heads(v):
        total = v[0:MEMBERS] * masks_f[0]
        for h in range(1, 4):
            total = total + v[h * MEMBERS : (h + 1) * MEMBERS] * masks_f[h]
        return total

    def put(ref, n, at, value):
        ref[n, at, :] = value.astype(BF16).astype(F32)

    def group_forward(group):
        at = pl.ds(group, MEMBERS, stride=GROUPS)
        for n in range(2):
            q, k, v = [r.qkv[part * 2 + n, at, :].astype(BF16) for part in range(3)]
            lanes = slice(n * 256, (n + 1) * 256)
            scores = nt(k, spread_heads(q)) * SCALE + r.bias_t[:, lanes]
            lifted = jnp.exp(scores - jnp.max(scores, axis=0, keepdims=True))
            probs = lifted * (1.0 / jnp.sum(lifted, axis=0, keepdims=True))
            r.probs[group, :, lanes] = probs
            put(r.att_rows, n, at, own_heads(tn(probs.astype(BF16), v)))

    def group_back(group):
        at = pl.ds(group, MEMBERS, stride=GROUPS)
        bias_parts = []
        for n in range(2):
            q, k, v = [r.qkv[part * 2 + n, at, :].astype(BF16) for part in range(3)]
            lanes = slice(n * 256, (n + 1) * 256)
            q_heads = spread_heads(q)
            g_heads = spread_heads(r.grid_g[n, at, :].astype(BF16))
            probs = r.probs[group, :, lanes]
            put(r.packed_back, 4 + n, at, nn(probs.astype(BF16), g_heads))
            grad_probs = nt(v, g_heads)
            grad_scores = probs * (
                grad_probs - jnp.sum(grad_probs * probs, axis=0, keepdims=True)
            )
            bias_parts.append(grad_scores)
            scaled = (grad_scores * SCALE).astype(BF16)
            put(r.packed_back, n, at, own_heads(tn(scaled, k)))
            put(r.packed_back, 2 + n, at, nn(scaled, q_heads))
        return bias_parts

    @pl.loop(0, GROUPS // unroll)
    def _(step):
        for n in range(unroll):
            group_forward(step * unroll + n)

    @pl.loop(0, 4)
    def _(t):
        att = lanes_of(r.att_rows, 0, cell_rows(t)).astype(BF16)
        r.att_out[map_rows(t, 16)] = att.reshape(16, GROUPS, CH)

    att_back = Exchange(me, links, r.att_out, r.att_in)
    r.bias_x[...] = jnp.zeros_like(r.bias_x)

    @pl.loop(0, GROUPS // unroll)
    def _(step):
        for n in range(4):
            att_back.send_row(lax.rem(me.row + step * 4 + n, ROWS))
        total = group_back(step * unroll)
        for n in range(1, unroll):
            total = [a + b for a, b in zip(total, group_back(step * unroll + n))]
        for n in range(2):
            r.bias_x[:, n * 256 : (n + 1) * 256] += total[n]

    def packed_tile(t):
        parts = [r.packed_back[n, cell_rows(t), :] for n in range(6)]
        return jnp.concatenate(parts, axis=1).astype(BF16)

    gn_back = Exchange(me, links, r.gn_out, r.gn_in)

    @pl.loop(0, 4, unroll=4)
    def _(step):
        t = lax.rem(start_tile + step, 4)
        gn = nt(packed_tile(t), r.w_qkv[...]).astype(BF16)
        r.gn_out[map_rows(t, 16)] = gn.reshape(16, GROUPS, CH)
        gn_back.send_tile(t)

    bias_sum = SmallSum(
        me, links, r.bias_x, r.bias_pair, r.bias_summed, r.bias_a, r.bias_b, r.sum_bias
    )
    bias_sum.start()
    r.pair_acc[...] = jnp.zeros_like(r.pair_acc)

    @pl.loop(0, 4)
    def _(t):
        x = r.grid_x[map_rows(t, 16)].reshape(TILE, CH)
        dy = r.grid_dy[map_rows(t, 16)].reshape(TILE, CH)
        att = r.att_out[map_rows(t, 16)].reshape(TILE, CH)
        r.pair_acc[:, : 3 * CH] += tn(x, packed_tile(t))
        r.pair_acc[:, 3 * CH :] += tn(att, dy)

    r.pair_x[...] = r.pair_acc[...].astype(BF16)

    def big(name, kind=Scatter):
        parts = ["x", "pair", "summed", "slots"]
        return kind(me, links, *[getattr(r, name + "_" + p) for p in parts])

    pair_sum = big("pair")
    pair_sum.start()
    bias_sum.to_q()
    pair_sum.scatter()
    gn_back.end()

    r.norm_acc[...] = jnp.zeros_like(r.norm_acc)
    r.gate_acc[...] = jnp.zeros_like(r.gate_acc)

    @pl.loop(0, 4, unroll=4)
    def _(t):
        unit, rstd = centre(r.mixed[cell_rows(t)].astype(F32))
        gn = r.gn_in[map_rows(t, 16)].reshape(TILE, CH).astype(F32)
        r.norm_acc[1] += fold(gn * unit)
        dy = r.dy[map_rows(t, 16)].reshape(TILE, CH).astype(F32)
        grad = dy + norm_back(unit, rstd, gn * gain_second)
        r.grad_mixed[cell_rows(t)] = grad
        grad_b = grad.astype(BF16)
        r.grad_mixed_b[cell_rows(t)] = grad_b
        for c in range(4):
            gg = nt(grad_b, r.w_project[c * 256 : (c + 1) * 256, :])
            for h in range(2):
                n = 2 * c + h
                part = gg[:, h * 128 : (h + 1) * 128]
                r.grad_gated[n, cell_rows(t), :] = part
                r.gate_acc[n] += fold(part * r.act[n, cell_rows(t), :].astype(F32))

    for n in range(LANES):
        r.gateg_x[n : n + 1, :] = jnp.sum(r.gate_acc[n], axis=0, keepdims=True)
    gate_sum = TileSum(me, links, r.gateg_x, r.gateg_pair, r.gateg_slots)
    gate_sum.start()

    @pl.loop(0, LANES)
    def _(c):
        scale = r.gate[:, aligned(c * 128, 128, 128)]
        for t in range(4):
            at = slice(t * TILE, (t + 1) * TILE)
            g = r.grad_gated[c, at, :] * scale * r.depth[c, at, :]
            for a in range(4):
                first = (1 + t * 4 + a) * PAD + 8
                r.grad_pre[c, first : first + MAP_COLS, :] = g[a * 64 : (a + 1) * 64]

    pack_edges(r.grad_pre, PAD, PAD + 8, r.pre_rows, r.pre_cols, r.pre_corners)
    pre_halo = edge_halo("pre")
    pre_halo.start()
    grad_t = r.grad_mixed_b[...].T
    for c in range(4):
        lane = slice(c * 256, (c + 1) * 256)
        product = nn(grad_t, lanes_of(r.act, 2 * c, slice(None))) * r.gate[:, lane]
        r.project_x[:, lane] = product.astype(BF16)
    project_sum = big("project")
    project_sum.start()
    bias_sum.to_rows()
    project_sum.scatter()
    slope_halo.end()
    pre_halo.end()
    grad_gate = flat(gate_sum.end())
    grad_logit = grad_gate * gate * (1.0 - gate)
    grad_hidden = wide_product(grad_logit, r.w_excite[...], nt)
    grad_squeezed = grad_hidden * (open_part * (1.0 + squeezed * (1.0 - open_part)))
    r.gate_back[...] = wide_product(grad_squeezed, r.w_squeeze_t[...], nn) * (1.0 / CELLS_TOTAL)

    @pl.loop(0, LANES)
    def _(c):
        shift = r.gate_back[:, aligned(c * 128, 128, 128)]

        def beside(part, slope, ok):
            return (part.astype(F32) + shift * slope.astype(F32)) * ok

        for row in range(MAP_ROWS):
            first = (1 + row) * PAD + 8
            at = slice(first, first + MAP_COLS)
            slope = r.depth[c, row * MAP_COLS : (row + 1) * MAP_COLS, :]
            value = r.grad_pre[c, at, :] + shift * slope
            r.grad_pre[c, at, :] = value.astype(BF16).astype(F32)
        rows = [
            beside(r.pre_rows_in[n, c], r.slope_rows_in[n, c], ok)
            for n, ok in enumerate((up_ok, down_ok))
        ]
        r.grad_pre[c, 8:72, :] = rows[0]
        r.grad_pre[c, last + 8 : last + 72, :] = rows[1]
        for n, (col, ok) in enumerate(((7, left_ok), (72, right_ok))):
            r.grad_pre[c, pl.ds(PAD + col, MAP_ROWS, stride=PAD), :] = beside(
                r.pre_cols_in[n, c], r.slope_cols_in[n, c], ok
            )

    corners = (
        (7, up_ok * left_ok),
        (72, up_ok * right_ok),
        (last + 7, down_ok * left_ok),
        (last + 72, down_ok * right_ok),
    )
    shifts = jnp.concatenate(
        [r.gate_back[:, c * 128 : (c + 1) * 128] for c in range(LANES)], axis=0
    )
    for corner, (at, ok) in enumerate(corners):
        slope = r.slope_corners_in[corner].astype(F32)[:8]
        cells = r.pre_corners_in[corner].astype(F32)[:8] + shifts * slope
        cells = cells * ok
        for c in range(LANES):
            r.grad_pre[c, at : at + 1, :] = cells[c : c + 1]

    bias_sum.back_q()

    r.tap_acc[...] = jnp.zeros_like(r.tap_acc)

    def depth_back(c):
        taps = taps_of(c)

        @pl.loop(0, MAP_ROWS // 2, unroll=4)
        def _(n):
            sums = [None] * 2
            inner = [
                r.spread[c, pl.ds(pad_row(1 + n * 2 + i, 8), MAP_COLS), :] for i in range(2)
            ]
            for b in range(3):
                parts = [None] * 3
                for row in range(4):
                    view = r.grad_pre.at[c, pl.ds(pad_row(n * 2 + row), PAD)]
                    v = view[pl.ds(7 + b, MAP_COLS), :]
                    for a in range(3):
                        i = row - a
                        if 0 <= i < 2:
                            term = v * taps[(2 - a) * 3 + 2 - b]
                            sums[i] = term if sums[i] is None else sums[i] + term
                            part = fold(v * inner[i])
                            parts[a] = part if parts[a] is None else parts[a] + part
                for a in range(3):
                    r.tap_acc[c, (2 - a) * 3 + 2 - b] += parts[a]
            for i in range(2):
                at = aligned((n * 2 + i) * MAP_COLS, MAP_COLS, MAP_COLS)
                r.grad_exp[c, at, :] = (sums[i] * r.expanded[c, at, :]).astype(BF16)

    pair_sum.end()
    project_sum.end()
    early = Gather(me, links, r.sum_early, r.grid_dy)
    for n, slots in enumerate((r.pair_slots, r.project_slots)):
        total = jnp.sum(slots[...].astype(F32), axis=0).astype(BF16)
        early.piece[:, n * 128 : (n + 1) * 128] = total

    @pl.loop(0, LANES)
    def _(c):
        depth_back(c)
        row = lax.rem(me.row + c, ROWS)
        for k in range(1, 8):
            early.send(row, k)

        @pl.when(c > 0)
        def _():
            early.send(row, 0)

    expand_sum = big("expand", HalvesScatter)
    for c in range(4):
        lane = slice(c * 256, (c + 1) * 256)
        product = nn(r.normed_t[...], lanes_of(r.grad_exp, 2 * c, slice(None)))
        r.expand_x[:, lane] = product.astype(BF16)
        if c % 2:
            expand_sum.start(c // 2)
    for c in range(LANES):
        rows = [jnp.sum(r.tap_acc[c, k], axis=0, keepdims=True) for k in range(9)]
        r.taps_sum_x[c * 8 : c * 8 + 8, :128] = jnp.concatenate(rows[:8], axis=0)
        rows = [rows[8], jnp.zeros((7, 128), F32)]
        r.taps_sum_x[c * 8 : c * 8 + 8, 128:] = jnp.concatenate(rows, axis=0)
    parts = ["x", "pair", "summed", "a", "b"]
    taps_sum = SmallSum(
        me, links, *[getattr(r, "taps_sum_" + p) for p in parts], r.sum_taps
    )
    taps_sum.start()
    expand_sum.scatter()
    taps_sum.to_q()

    @pl.loop(0, 4)
    def _(t):
        grad = None
        for c in range(4):
            lane = slice(c * 256, (c + 1) * 256)
            part = nt(lanes_of(r.grad_exp, 2 * c, cell_rows(t)), r.w_expand[:, lane])
            grad = part if grad is None else grad + part
        unit, rstd = centre(r.image[map_rows(t)].reshape(TILE, CH).astype(F32))
        r.norm_acc[0] += fold(grad * unit)
        value = r.grad_mixed[cell_rows(t)] + norm_back(unit, rstd, grad * gain_first)
        r.grad_map[map_rows(t)] = value.astype(BF16).reshape(4, MAP_COLS, CH)

    flush("grad_map").start()
    att_back.end()

    @pl.loop(0, 4)
    def _(t):
        att = r.att_in[map_rows(t, 16)].reshape(TILE, CH)
        value = r.mixed[cell_rows(t)].astype(F32) + nn(att, r.w_out[...])
        r.out_map[map_rows(t)] = value.astype(BF16).reshape(4, MAP_COLS, CH)

    flush("out_map").start()
    rows = []
    for n in range(2):
        sums = jnp.sum(r.norm_acc[n], axis=0, keepdims=True)
        rows += [sums[:, :128], sums[:, 128:]]
    r.norms_x[...] = jnp.concatenate(rows + [jnp.zeros((4, 128), F32)], axis=0)
    norms_sum = TileSum(me, links, r.norms_x, r.norms_pair, r.norms_slots)
    norms_sum.start()
    bias_sum.end()
    flush("sum_bias").start()
    rows = [pooled, grad_logit, jnp.pad(hidden, ((0, 0), (0, 960)))]
    rows += [jnp.pad(grad_squeezed, ((0, 0), (0, 960))), jnp.zeros((4, 1024), F32)]
    r.gate_rows[...] = jnp.concatenate(rows, axis=0)
    flush("gate_rows").start()
    taps_sum.to_rows()
    expand_sum.end()
    final = Gather(me, links, r.sum_expand, r.expand_slots)
    final.piece[...] = jnp.sum(r.expand_slots[...].astype(F32), axis=0).astype(BF16)
    final.send_all()
    early.back_pair()
    taps_sum.back_q()
    early.end()
    flush("sum_early").start()
    r.sum_norms[...] = norms_sum.end()
    flush("sum_norms").start()
    taps_sum.end()
    flush("sum_taps").start()
    final.back_pair()
    final.end()
    flush("sum_expand").start()
    for name in OUTS:
        flush(name).wait()
    links.finish()


FINAL = dict(
    block_out=((MAP_ROWS, MAP_COLS, CH), BF16),
    grad_image=((MAP_ROWS, MAP_COLS, CH), BF16),
    grad_norm0=((1, CH), F32),
    grad_expand=((CH, 1024), F32),
    grad_depth=((3, 3, 1024), F32),
    grad_squeeze=((64, 1024), F32),
    grad_excite=((64, 1024), F32),
    grad_project=((1024, CH), F32),
    grad_norm1=((1, CH), F32),
    grad_qkv=((CH, 3 * CH), F32),
    grad_out_proj=((CH, CH), F32),
    grad_bias=((HEADS, MEMBERS, MEMBERS), F32),
)


def finish_kernel(*args):
    r = Refs()
    names = ["hbm_" + n for n in OUTS] + ["hbm_" + n for n in FINAL]
    names += list(OUTS) + list(FINAL)[2:] + ["in_sems", "out_sems"]
    for name, ref in zip(names, args, strict=True):
        setattr(r, name, ref)
    r.block_out, r.grad_image = r.out_map, r.grad_map

    def fetch(name):
        at = list(OUTS).index(name)
        return pltpu.make_async_copy(getattr(r, "hbm_" + name), getattr(r, name), r.in_sems.at[at])

    def flush(name):
        at = list(FINAL).index(name)
        return pltpu.make_async_copy(
            getattr(r, name), getattr(r, "hbm_" + name), r.out_sems.at[at]
        )

    order = ["sum_expand", "sum_early", "out_map", "grad_map"]
    order += ["sum_bias", "sum_taps", "sum_norms", "gate_rows"]
    for name in order:
        fetch(name).start()
    fetch("sum_expand").wait()
    r.grad_expand[...] = r.sum_expand[...].astype(F32)
    flush("grad_expand").start()
    fetch("sum_early").wait()
    for n in range(8):
        lane = slice(n * 128, (n + 1) * 128)
        part = r.sum_early[:, n * 256 : n * 256 + 128].astype(F32)
        if n < 6:
            r.grad_qkv[:, lane] = part
        else:
            r.grad_out_proj[:, (n - 6) * 128 : (n - 5) * 128] = part
    flush("grad_qkv").start()
    flush("grad_out_proj").start()
    for n in range(8):
        lane = slice(n * 128, (n + 1) * 128)
        r.grad_project[lane, :] = r.sum_early[:, n * 256 + 128 : n * 256 + 256].astype(F32).T
    flush("grad_project").start()
    fetch("out_map").wait()
    flush("block_out").start()
    fetch("grad_map").wait()
    flush("grad_image").start()
    for name in order[4:]:
        fetch(name).wait()
    for h in range(0, HEADS, 2):
        both = r.sum_bias[:, h * 64 : (h + 2) * 64].T
        r.grad_bias[h] = both[:64]
        r.grad_bias[h + 1] = both[64:]
    for k in range(9):
        if k < 8:
            rows = [r.sum_taps[c * 8 + k : c * 8 + k + 1, :128] for c in range(LANES)]
        else:
            rows = [r.sum_taps[c * 8 : c * 8 + 1, 128:] for c in range(LANES)]
        r.grad_depth[k // 3, k % 3 : k % 3 + 1, :] = jnp.concatenate(rows, axis=1)
    for n, out in enumerate((r.grad_norm0, r.grad_norm1)):
        rows = [r.sum_norms[n * 2 + c : n * 2 + c + 1, :] for c in range(2)]
        out[...] = jnp.concatenate(rows, axis=1)
    pooled, grad_logit = r.gate_rows[0:1, :], r.gate_rows[1:2, :]
    hidden, grad_squeezed = r.gate_rows[2:3, :64], r.gate_rows[3:4, :64]
    r.grad_excite[...] = outer(hidden, grad_logit)
    r.grad_squeeze[...] = outer(grad_squeezed, pooled)
    early = ["block_out", "grad_image", "grad_expand", "grad_qkv", "grad_out_proj", "grad_project"]
    for name in FINAL:
        if name not in early:
            flush(name).start()
    for name in FINAL:
        flush(name).wait()


def on_device(
    image,
    out_cotangent,
    norm0_gain,
    w_expand,
    w_depth,
    w_squeeze,
    w_excite,
    w_project,
    norm1_gain,
    w_qkv,
    w_out,
    attn_bias,
):
    vmem = pl.BlockSpec(memory_space=pltpu.VMEM)
    any_space = pl.BlockSpec(memory_space=pl.ANY)
    buffers = lambda shapes: [pltpu.VMEM(*shape) for shape in shapes.values()]
    made = pl.pallas_call(
        block_kernel,
        out_shape=[jax.ShapeDtypeStruct(*shape) for shape in OUTS.values()],
        in_specs=[vmem] * len(IN_NAMES) + [any_space] * len(LATE),
        out_specs=[any_space] * len(OUTS),
        scratch_shapes=buffers(LATE)
        + buffers(OUTS)
        + buffers(SCRATCH)
        + [pltpu.SemaphoreType.DMA((n,)) for n in (SEMS, len(LATE), len(OUTS))],
        compiler_params=pltpu.CompilerParams(
            collective_id=0, has_side_effects=True, vmem_limit_bytes=63 * 2**20
        ),
        name="block",
    )(
        norm0_gain,
        norm1_gain,
        w_depth,
        image,
        w_expand,
        out_cotangent.reshape(MEMBERS, GROUPS, CH),
        w_out,
        attn_bias,
        w_squeeze.T,
        w_excite,
        w_project,
        w_qkv,
    )
    final = pl.pallas_call(
        finish_kernel,
        out_shape=[jax.ShapeDtypeStruct(*shape) for shape in FINAL.values()],
        in_specs=[any_space] * len(OUTS),
        out_specs=[any_space] * len(FINAL),
        scratch_shapes=buffers(OUTS)
        + buffers(FINAL)[2:]
        + [pltpu.SemaphoreType.DMA((n,)) for n in (len(OUTS), len(FINAL))],
        compiler_params=pltpu.CompilerParams(vmem_limit_bytes=63 * 2**20),
        name="finish",
    )(*made)
    final = dict(zip(FINAL, final))
    final["grad_norm0"] = final["grad_norm0"].reshape(CH)
    final["grad_norm1"] = final["grad_norm1"].reshape(CH)
    final["grad_squeeze"] = final["grad_squeeze"].T
    return tuple(final.values())


def solution(mesh):
    mapped = P("row", "col", None)
    return jax.shard_map(
        on_device,
        mesh=mesh,
        in_specs=(mapped, mapped) + (P(),) * 10,
        out_specs=(mapped, mapped) + (P(),) * 10,
        check_vma=False,
    )
```
